32 devices in a mesh: dp: 16 (over z, y, x), mod: 2 (over core).
Axes of the slice: x: 2, y: 2, z: 4, core: 2. Of those that a mesh axis runs over, the one named last changes fastest.
Arguments:
- vision_feats: bfloat16 [2048, 2, 64, 512], P('dp', None, None, 'mod'), may hold values from -6 to 6
- vision_grid: int32 [2048, 2, 2], P(('dp', 'mod')), may hold values from 5 to 8
- proprio: bfloat16 [2048, 2, 16, 32], P(('dp', 'mod')), may hold values from -6 to 6
- proprio_mask: int32 [2048, 2, 16], P(('dp', 'mod')), may hold values from 0 to 1, as said below
- token_valid: int32 [2048, 64], P(('dp', 'mod')), may hold values from 0 to 1, as said below
- mix_weight: int32 [2048], P(('dp', 'mod')), may hold values from 1 to 4
- out_cot: bfloat16 [2048, 64, 128], P(('dp', 'mod')), may hold values from -6 to 6
- feat_proj: bfloat16 [512, 128], P('mod'), may hold values from -0.25 to 0.25
- vis_query: bfloat16 [16, 128], replicated, may hold values from -6 to 6
- vis_wq: bfloat16 [128, 128], replicated, may hold values from -0.5 to 0.5
- vis_kv: bfloat16 [128, 256], replicated, may hold values from -0.5 to 0.5
- vis_wo: bfloat16 [128, 128], replicated, may hold values from -1.5 to 1.5
- prop_w1: bfloat16 [32, 128], replicated, may hold values from -1 to 1
- prop_w2: bfloat16 [128, 128], replicated, may hold values from -0.5 to 0.5
- prop_query: bfloat16 [16, 128], replicated, may hold values from -6 to 6
- prop_wq: bfloat16 [128, 128], replicated, may hold values from -0.5 to 0.5
- prop_kv: bfloat16 [128, 256], replicated, may hold values from -0.5 to 0.5
- prop_wo: bfloat16 [128, 128], replicated, may hold values from -1.5 to 1.5
- ln1_gain: bfloat16 [128], replicated, may hold values from 0.099609375 to 1.8984375
- ln1_bias: bfloat16 [128], replicated, may hold values from -3 to 3
- qkv_weight: bfloat16 [128, 384], replicated, may hold values from -0.5 to 0.5
- attn_out: bfloat16 [128, 128], replicated, may hold values from -1.5 to 1.5
- ln2_gain: bfloat16 [128], replicated, may hold values from 0.099609375 to 1.8984375
- ln2_bias: bfloat16 [128], replicated, may hold values from -3 to 3
- mlp_in: bfloat16 [128, 512], replicated, may hold values from -0.5 to 0.5
- mlp_out: bfloat16 [512, 128], replicated, may hold values from -0.25 to 0.25
Outputs:
- output: bfloat16 [2048, 64, 128], P(('dp', 'mod'))
- grad_vision: bfloat16 [2048, 2, 64, 512], P('dp', None, None, 'mod')
- grad_proprio: bfloat16 [2048, 2, 16, 32], P(('dp', 'mod'))
- grad_feat_proj: float32 [512, 128], P('mod')
- grad_vis_query: float32 [16, 128], replicated
- grad_vis_wq: float32 [128, 128], replicated
- grad_vis_kv: float32 [128, 256], replicated
- grad_vis_wo: float32 [128, 128], replicated
- grad_prop_w1: float32 [32, 128], replicated
- grad_prop_w2: float32 [128, 128], replicated
- grad_prop_query: float32 [16, 128], replicated
- grad_prop_wq: float32 [128, 128], replicated
- grad_prop_kv: float32 [128, 256], replicated
- grad_prop_wo: float32 [128, 128], replicated
- grad_ln1_gain: float32 [128], replicated
- grad_ln1_bias: float32 [128], replicated
- grad_qkv_weight: float32 [128, 384], replicated
- grad_attn_out: float32 [128, 128], replicated
- grad_ln2_gain: float32 [128], replicated
- grad_ln2_bias: float32 [128], replicated
- grad_mlp_in: float32 [128, 512], replicated
- grad_mlp_out: float32 [512, 128], replicated
- rms: float32 [3], replicated
The draws below stay inside these ranges and needn't reach their ends.
Inputs may be any that keep to these rules, and one draw needn't show every extreme that they name: `proprio_mask`: frame 0 of every step is real. `token_valid`: token 0 of every sample is valid.
All inputs are finite; a program needn't handle non-finite values.
Results may differ from the reference program's by a relative error of at most 0.02.
The reference program's roundings to bfloat16 on the way count: a program that leaves them out, or rounds other values in their place, can miss the bound.
Values may be sent and summed in bfloat16 or wider, within the bound.
A program may use at most 256 MiB of HBM per device.

```python
import math
import jax
import jax.numpy as jnp
from jax import lax

D = 128
HEADS = 8
HEAD = 16
FF = 512
NQ = 16
FEAT = 512
PROP = 32
GRID = 8
PT = 16
STEPS = 2
SEQ = 64
SAMPLES = 2048
N_DP = 16
N_MOD = 2


def draw_vision_grid(key, part):
    key = jax.random.fold_in(key, 37)
    least = GRID // 2 + 1
    sides = jax.random.randint(key, (SAMPLES, STEPS, 2), least, GRID + 1)
    sides = sides.at[0, 0, :].set(GRID)
    sides = sides.at[SAMPLES - 1, STEPS - 1, :].set(least)
    return sides.astype(jnp.int32)


def draw_proprio_mask(key, part):
    key = jax.random.fold_in(key, 11)
    values = jax.random.randint(key, (SAMPLES, STEPS, PT), 0, 4)
    marks = jnp.minimum(values, 1)
    return marks.at[:, :, 0].set(1).astype(jnp.int32)


def draw_token_valid(key, part):
    key = jax.random.fold_in(key, 23)
    values = jax.random.randint(key, (SAMPLES, SEQ), 0, 4)
    marks = jnp.minimum(values, 1)
    return marks.at[:, 0].set(1).astype(jnp.int32)


def with_ends(entries, stream_key, low, high):
    longest = entries.shape.index(max(entries.shape))
    spots = []
    for shift in (0, 1):
        where = [jax.random.randint(jax.random.fold_in(stream_key, axis), (), 0, length) for axis, length in enumerate(entries.shape)]
        where[longest] = (where[longest] + shift) % entries.shape[longest]
        spots.append(tuple(where))
    return entries.at[spots[0]].set(low).at[spots[1]].set(high)


def shard_levels(own_key, extent, pieces, smallest, top_value):
    factor_of, own = 1.0, jax.random.fold_in(own_key, 6)
    for axis_at, parts in pieces:
        draws = jnp.exp(jax.random.uniform(jax.random.fold_in(own, axis_at), (parts,), jnp.float32, smallest / len(pieces), top_value / len(pieces)))
        factor_of = factor_of * jnp.repeat(draws, extent[axis_at] // parts).reshape([-1 if axis == axis_at else 1 for axis in range(len(extent))])
    return factor_of


def bell_draw(own_key, shape, scale, most, cuts=(), kind=jnp.bfloat16):
    values = scale * jax.random.normal(own_key, shape, jnp.float32)
    if cuts:
        values = values * shard_levels(own_key, shape, cuts, -0.22, 0.18)
    return jnp.clip(values, -most, most).astype(kind)


def setup_inputs(seed: int = 0) -> dict:
    seeds = jax.random.split(jax.random.key(seed), 27)
    return {
        "vision_feats": bell_draw(seeds[0], (SAMPLES, STEPS, GRID * GRID, FEAT), 1.0, 6.0, ((0, 16), (3, 2))),
        "vision_grid": draw_vision_grid(jax.random.fold_in(seeds[26], 71), 0),
        "proprio": bell_draw(seeds[2], (SAMPLES, STEPS, PT, PROP), 1.0, 6.0, ((0, 32),)),
        "proprio_mask": draw_proprio_mask(jax.random.fold_in(seeds[26], 71), 0),
        "token_valid": draw_token_valid(jax.random.fold_in(seeds[26], 71), 0),
        "mix_weight": with_ends(jax.random.randint(seeds[5], (SAMPLES,), 1, 5), jax.random.fold_in(seeds[5], 1), 1, 4).astype(jnp.int32),
        "out_cot": bell_draw(seeds[6], (SAMPLES, SEQ, D), 1.0, 6.0, ((0, 32),)),
        "feat_proj": bell_draw(seeds[7], (FEAT, D), FEAT ** -0.5, 0.25, ((0, 2),)),
        "vis_query": bell_draw(seeds[8], (NQ, D), 1.0, 6.0),
        "vis_wq": bell_draw(seeds[9], (D, D), D ** -0.5, 0.5),
        "vis_kv": bell_draw(seeds[10], (D, 2 * D), D ** -0.5, 0.5),
        "vis_wo": bell_draw(seeds[11], (D, D), (D // 8) ** -0.5, 1.5),
        "prop_w1": bell_draw(seeds[12], (PROP, D), PROP ** -0.5, 1.0),
        "prop_w2": bell_draw(seeds[13], (D, D), D ** -0.5, 0.5),
        "prop_query": bell_draw(seeds[14], (NQ, D), 1.0, 6.0),
        "prop_wq": bell_draw(seeds[15], (D, D), D ** -0.5, 0.5),
        "prop_kv": bell_draw(seeds[16], (D, 2 * D), D ** -0.5, 0.5),
        "prop_wo": bell_draw(seeds[17], (D, D), (D // 8) ** -0.5, 1.5),
        "ln1_gain": jnp.clip(1.0 + 0.18 * jax.random.normal(seeds[18], (D,), jnp.float32), 0.099609375, 1.8984375).astype(jnp.bfloat16),
        "ln1_bias": bell_draw(seeds[19], (D,), 0.5, 3.0),
        "qkv_weight": bell_draw(seeds[20], (D, 3 * D), D ** -0.5, 0.5),
        "attn_out": bell_draw(seeds[21], (D, D), (D // 8) ** -0.5, 1.5),
        "ln2_gain": jnp.clip(1.0 + 0.18 * jax.random.normal(seeds[22], (D,), jnp.float32), 0.099609375, 1.8984375).astype(jnp.bfloat16),
        "ln2_bias": bell_draw(seeds[23], (D,), 0.5, 3.0),
        "mlp_in": bell_draw(seeds[24], (D, FF), D ** -0.5, 0.5),
        "mlp_out": bell_draw(seeds[25], (FF, D), FF ** -0.5, 0.25),
    }


@jax.custom_vjp
def low(v):
    return lax.optimization_barrier(v.astype(jnp.bfloat16)).astype(jnp.float32)

@jax.custom_vjp
def low_back(v):
    return v

def low_keep(v):
    return (low(v), None)

def low_pass(kept, grad):
    return (grad,)

def back_keep(v):
    return (v, None)

def back_low(kept, grad):
    return (low(grad),)
low.defvjp(low_keep, low_pass)
low_back.defvjp(back_keep, back_low)

def product(left, right):
    return jnp.matmul(left, right, precision=lax.Precision.HIGHEST)

def attend(query, keys, values, key_keep):
    full_shape = query.shape
    query_heads = query.reshape(query.shape[:-1] + (HEADS, HEAD))
    key_heads = keys.reshape(keys.shape[:-1] + (HEADS, HEAD))
    value_heads = values.reshape(values.shape[:-1] + (HEADS, HEAD))
    scores = jnp.einsum('...qhd,...khd->...hqk', query_heads, key_heads, precision=lax.Precision.HIGHEST) / math.sqrt(HEAD)
    scores = jnp.where(key_keep[..., None, None, :] > 0, scores, -1e+30)
    peak_score = lax.optimization_barrier(jnp.max(scores, axis=-1, keepdims=True))
    weights = jnp.exp(scores - peak_score)
    weights = low(weights / lax.optimization_barrier(jnp.sum(weights, axis=-1, keepdims=True)))
    mixed = jnp.einsum('...hqk,...khd->...qhd', weights, value_heads, precision=lax.Precision.HIGHEST)
    return mixed.reshape(full_shape)

def layer_norm(values, gain, shift):
    centered = values - lax.optimization_barrier(jnp.mean(values, axis=-1, keepdims=True))
    spread = lax.optimization_barrier(jnp.mean(centered * centered, axis=-1, keepdims=True))
    return centered * lax.rsqrt(spread + 1e-05) * gain + shift

def cross_stem(tokens, learned, w_query, w_kv, w_out, key_keep):
    width = learned.shape[1]
    query = low_back(low(product(learned, w_query)))
    key_value = low_back(low(product(tokens, w_kv)))
    query = jnp.broadcast_to(query, tokens.shape[:-2] + query.shape)
    mixed = attend(query, key_value[..., :width], key_value[..., width:], key_keep)
    return low_back(product(low(mixed), w_out))

def forward(tok_sum, prop_frames, weights_f, vis_keep, prop_keep, tok_keep):
    vis_query, vis_wq, vis_kv, vis_wo, prop_w1, prop_w2, prop_query, prop_wq, prop_kv, prop_wo, ln1_gain, ln1_bias, qkv_weight, attn_out, ln2_gain, ln2_bias, mlp_in, mlp_out = weights_f
    width = vis_query.shape[1]
    tokens = low_back(low(tok_sum))
    vision_lat = cross_stem(tokens, vis_query, vis_wq, vis_kv, vis_wo, vis_keep)
    hidden = low(jax.nn.silu(product(prop_frames, prop_w1)))
    prop_tokens = low_back(low(product(hidden, prop_w2)))
    prop_lat = cross_stem(prop_tokens, prop_query, prop_wq, prop_kv, prop_wo, prop_keep)
    samples = vision_lat.shape[0]
    stream = jnp.stack([vision_lat, prop_lat], axis=2).reshape(samples, -1, width)
    normed = low(layer_norm(stream, ln1_gain, ln1_bias))
    qkv_all = low_back(low(product(normed, qkv_weight)))
    mixed = attend(qkv_all[..., :width], qkv_all[..., width:2 * width], qkv_all[..., 2 * width:], tok_keep)
    attn_branch = low_back(product(low(mixed), attn_out))
    middle = stream + attn_branch
    normed_two = low(layer_norm(middle, ln2_gain, ln2_bias))
    up_proj = low_back(product(normed_two, mlp_in))
    activated = low(jax.nn.gelu(up_proj))
    mlp_branch = low_back(product(activated, mlp_out))
    output = middle + mlp_branch
    valid = tok_keep[..., None]
    statistics = jnp.stack([jnp.sum(output * output * valid), jnp.sum(attn_branch * attn_branch * valid), jnp.sum(mlp_branch * mlp_branch * valid), jnp.sum(tok_keep)])
    return (output, statistics)

def make_masks(vision_grid, proprio_mask, token_valid):
    slots = jnp.arange(GRID * GRID, dtype=jnp.int32)
    rows_ok = (slots // GRID)[None, None, :] < vision_grid[..., 0:1]
    cols_ok = (slots % GRID)[None, None, :] < vision_grid[..., 1:2]
    vis_keep = (rows_ok & cols_ok).astype(jnp.float32)
    return (vis_keep, proprio_mask.astype(jnp.float32), token_valid.astype(jnp.float32))

def reference(vision_feats, vision_grid, proprio, proprio_mask, token_valid, mix_weight, out_cot, feat_proj, vis_query, vis_wq, vis_kv, vis_wo, prop_w1, prop_w2, prop_query, prop_wq, prop_kv, prop_wo, ln1_gain, ln1_bias, qkv_weight, attn_out, ln2_gain, ln2_bias, mlp_in, mlp_out):
    weights_f = tuple((item.astype(jnp.float32) for item in (vis_query, vis_wq, vis_kv, vis_wo, prop_w1, prop_w2, prop_query, prop_wq, prop_kv, prop_wo, ln1_gain, ln1_bias, qkv_weight, attn_out, ln2_gain, ln2_bias, mlp_in, mlp_out)))
    block = FEAT // N_MOD
    proj_blocks = feat_proj.astype(jnp.float32).reshape(N_MOD, block, D)
    group_count = N_DP

    def regroup(array):
        return array.reshape((group_count, SAMPLES // group_count) + array.shape[1:])
    group_data = tuple((regroup(item) for item in (vision_feats, vision_grid, proprio, proprio_mask, token_valid, mix_weight, out_cot)))

    def group_step(running, data):
        feats, grid_sizes, frames, frame_mask, tok_mask, mixing, cotangent = data
        vis_keep, prop_keep, tok_keep = make_masks(grid_sizes, frame_mask, tok_mask)

        def whole_pass(feats_f, frames_f, proj_f, weights_in):
            split = feats_f.reshape(feats_f.shape[:-1] + (N_MOD, block))
            partial_terms = jnp.einsum('stvmf,mfd->stvmd', split, proj_f, precision=lax.Precision.HIGHEST)
            tok_sum = lax.optimization_barrier(jnp.sum(low(partial_terms), axis=3))
            return forward(tok_sum, frames_f, weights_in, vis_keep, prop_keep, tok_keep)
        output, pull, statistics = jax.vjp(whole_pass, feats.astype(jnp.float32), frames.astype(jnp.float32), proj_blocks, weights_f, has_aux=True)
        cot_seed = cotangent.astype(jnp.float32) * mixing.astype(jnp.float32)[:, None, None]
        grad_feats, grad_frames, grad_proj, grad_weights = pull(cot_seed)
        running = (running[0] + grad_proj, jax.tree.map(lambda total, extra: total + extra, running[1], grad_weights), running[2] + statistics)
        return (running, (output.astype(jnp.bfloat16), grad_feats.astype(jnp.bfloat16), grad_frames.astype(jnp.bfloat16)))
    start = (jnp.zeros_like(proj_blocks), jax.tree.map(jnp.zeros_like, weights_f), jnp.zeros((4,), jnp.float32))
    running, results = lax.scan(group_step, start, group_data)
    grad_proj, grads, statistics = running
    output = results[0].reshape(SAMPLES, SEQ, D)
    grad_vision = results[1].reshape(vision_feats.shape)
    grad_proprio = results[2].reshape(proprio.shape)
    rms = jnp.sqrt(statistics[:3] / (statistics[3] * D))
    return (output, grad_vision, grad_proprio, grad_proj.reshape(FEAT, D), grads[0], grads[1], grads[2], grads[3], grads[4], grads[5], grads[6], grads[7], grads[8], grads[9], grads[10], grads[11], grads[12], grads[13], grads[14], grads[15], grads[16], grads[17], rms)
```

```python
import functools
import math

import jax
import jax.numpy as jnp
from jax import lax
from jax.experimental import pallas as pl
from jax.experimental.pallas import tpu as pltpu
from jax.sharding import PartitionSpec as P

HEADS = 8
HEAD = 16
WIDTH = 128
NEG = -1e30
BF = jnp.bfloat16
F32 = jnp.float32
VMEM_LIMIT = 60 * 2**20

R_WIN, R_WOUT, R_Q, R_KV, R_AO = 0, 512, 1024, 1152, 1408
R_SWO, R_VKV, R_PKV, R_W2, R_W1 = 1536, 1792, 2048, 2304, 2432
R_QV, R_QP, R_LN, R_STAT, R_END = 2464, 2480, 2496, 2500, 2560


def nn(a, b):
    return lax.dot_general(a, b, (((1,), (0,)), ((), ())), preferred_element_type=F32)


def nt(a, b):
    return lax.dot_general(a, b, (((1,), (1,)), ((), ())), preferred_element_type=F32)


def cat(items, axis):
    return jnp.concatenate(items, axis=axis)


def lane_iota(rows, lanes):
    return lax.broadcasted_iota(jnp.int32, (rows, lanes), 1)


def head_expand(value, masks):
    rows, lanes = value.shape
    out = []
    for h in range(HEADS):
        mask = cat([cat([masks[h]] * (rows // 16), 0)] * (lanes // WIDTH), 1)
        out.append(value * mask)
    return cat(out, 0)


def head_select(full):
    rows, lanes = full.shape[0] // HEADS, full.shape[1]
    head = (lane_iota(rows, lanes) & (WIDTH - 1)) >> 4
    out = full[:rows]
    for h in range(1, HEADS):
        out = jnp.where(head == h, full[h * rows : (h + 1) * rows], out)
    return out


def softmax_rows(scores):
    peak = jnp.max(scores, axis=1, keepdims=True)
    weights = jnp.exp(scores - peak)
    return weights * (1.0 / jnp.sum(weights, axis=1, keepdims=True))


def softmax_grad(weights, grad):
    return weights * (grad - jnp.sum(weights * grad, axis=1, keepdims=True))


def mean_rows(value):
    return jnp.sum(value, axis=0, keepdims=True) * (1.0 / value.shape[0])


def norm_rows(value):
    centered = value - mean_rows(value)
    scale = lax.rsqrt(mean_rows(centered * centered) + 1e-05)
    return centered * scale, scale


def norm_rows_grad(grad, hat, scale):
    return scale * (grad - mean_rows(grad) - hat * mean_rows(grad * hat))


def spread_keys(left, low_half, high_half):
    turned = cat([left[:, 64:], left[:, :64]], 1)
    zero = jnp.zeros((HEAD, WIDTH), BF)
    out = []
    for group in range(2):
        rows = []
        for s in range(2):
            for local in range(4):
                h = group * 4 + local
                part = slice(h * HEAD, (h + 1) * HEAD)
                source = left if (s == local % 2) else turned
                block = source[part] * (high_half if local % 2 else low_half)
                rows.append(cat([block, zero] if local < 2 else [zero, block], 1))
        out.append(cat(rows, 0))
    return out


def mix_keys(spread, weights, first):
    out = []
    for group in range(2):
        full = nn(spread[group], weights[group * 256 : (group + 1) * 256])
        out.append(jnp.where(first, full[:64], full[64:]))
    return cat(out, 0)


def stem_queries(query, w_query, masks):
    value = nn(query, w_query).astype(BF)
    return head_expand(value * jnp.asarray(0.25, BF), masks)


def block_kernel(
    grid_ref, po, pr, frames, aux, cot,
    vis_query, vis_wq, vis_kv, vis_wo, prop_w1, prop_w2, prop_query, prop_wq, prop_kv, prop_wo,
    ln, qkv_w, attn_out, mlp_in, mlp_out,
    out, dtok_ref, dframes, acc,
    masks_ref, qv_ref, qp_ref, wqkv_t, ao_t, win_t, wout_t, stem_t, ln_ref,
    gv_ref, gp_ref, lnacc, stat,
):
    step = pl.program_id(0)

    @pl.when(step == 0)
    def _():
        lane = lane_iota(16, WIDTH) >> 4
        for h in range(HEADS):
            masks_ref[h] = jnp.where(lane == h, 1.0, 0.0).astype(BF)
        masks = [masks_ref[h] for h in range(HEADS)]
        qv_ref[...] = stem_queries(vis_query[...], vis_wq[...], masks)
        qp_ref[...] = stem_queries(prop_query[...], prop_wq[...], masks)
        wqkv_t[...] = qkv_w[...].T
        ao_t[...] = attn_out[...].T
        win_t[...] = mlp_in[...].T
        wout_t[...] = mlp_out[...].T
        stem_t[:, :WIDTH] = vis_wo[...].T
        stem_t[:, WIDTH:] = prop_wo[...].T
        for j in range(4):
            ln_ref[j] = jnp.broadcast_to(ln[j : j + 1, :], (WIDTH, WIDTH)).T
        acc[...] = jnp.zeros_like(acc)
        gv_ref[...] = jnp.zeros_like(gv_ref)
        gp_ref[...] = jnp.zeros_like(gp_ref)
        lnacc[...] = jnp.zeros_like(lnacc)
        stat[...] = jnp.zeros_like(stat)

    masks = [masks_ref[h] for h in range(HEADS)]
    qv, qp = qv_ref[...], qp_ref[...]
    lane = lane_iota(HEAD, WIDTH)
    low_half = jnp.where(lane < 64, 1.0, 0.0).astype(BF)
    high_half = jnp.where(lane < 64, 0.0, 1.0).astype(BF)
    first = lane_iota(64, WIDTH) < 64
    low_tall = cat([low_half] * 8, 0)
    high_tall = cat([high_half] * 8, 0)

    tok = (po[...].astype(F32) + pr[...].astype(F32)).astype(BF)
    vkv = nn(tok, vis_kv[...]).astype(BF)
    vk, vv = vkv[:, :WIDTH], vkv[:, WIDTH:]
    slot = lax.broadcasted_iota(jnp.int32, (64, WIDTH), 0)
    slot_row, slot_col = slot >> 3, slot & 7
    bias = []
    for st in range(8):
        s, t = step * 4 + st // 2, st % 2
        keep = (slot_row < grid_ref[s, t, 0]) & (slot_col < grid_ref[s, t, 1])
        bias.append(jnp.where(keep, 0.0, NEG))
    vp = softmax_rows(nt(vk, qv).reshape(8, 64, WIDTH) + cat(bias, 0).reshape(8, 64, WIDTH))
    vpb = vp.reshape(512, WIDTH).astype(BF)
    vpt = vpb.T
    zero64 = jnp.zeros((64, WIDTH), BF)
    vmixed = []
    for j in range(4):
        pair = slice(128 * j, 128 * j + 128)
        block = vv[pair]
        spread = cat([cat([block[:64], zero64], 0), cat([zero64, block[64:]], 0)], 1)
        both = head_select(nn(vpt[:, pair], spread)).astype(BF)
        vmixed += [both[:, :WIDTH], both[:, WIDTH:]]

    fr = frames[...]
    pre = nn(fr, prop_w1[...])
    gate = jax.nn.sigmoid(pre)
    hidden = (pre * gate).astype(BF)
    ptok = nn(hidden, prop_w2[...]).astype(BF)
    pkv = nn(ptok, prop_kv[...]).astype(BF)
    pk, pv = pkv[:, :WIDTH], pkv[:, WIDTH:]
    pbias = jnp.broadcast_to(aux[0, 3:4, :WIDTH], (WIDTH, WIDTH)).T
    pp = softmax_rows((nt(pk, qp) + pbias).reshape(8, 16, WIDTH))
    ppb = pp.reshape(WIDTH, WIDTH).astype(BF)
    ppt = ppb.T
    zero16 = jnp.zeros((HEAD, WIDTH), BF)
    spread = cat(
        [cat([pv[16 * j : 16 * j + 16] if j == st else zero16 for j in range(8)], 0) for st in range(8)], 1
    )
    pm = head_select(nn(ppt, spread)).astype(BF)

    rows = []
    for st in range(8):
        rows.append(cat([vmixed[st], zero16], 1))
        rows.append(cat([zero16, pm[:, WIDTH * st : WIDTH * st + WIDTH]], 1))
    mixed_ext = cat(rows, 0)
    x = nt(stem_t[...], mixed_ext)
    g1, b1, g2, b2 = [cat([ln_ref[j]] * 2, 1) for j in range(4)]
    hat1, scale1 = norm_rows(x)
    n1 = (hat1 * g1 + b1).astype(BF)
    qkv = nn(wqkv_t[...], n1).astype(BF)
    qt, kt, vt = qkv[:WIDTH] * jnp.asarray(0.25, BF), qkv[WIDTH : 2 * WIDTH], qkv[2 * WIDTH :]
    kn, vn = kt.T, vt.T
    weights, weights_b, query_bd, mixed_t = [], [], [], []
    for p in range(2):
        pair = slice(128 * p, 128 * p + 128)
        column = jnp.broadcast_to(aux[0, 2:3, pair], (WIDTH, WIDTH)).T
        tbias = jnp.where(first, column[:64], column[64:])
        qbd = cat([qt[:, pair] * low_tall, qt[:, pair] * high_tall], 0)
        keys = cat([kn[128 * p : 128 * p + 64], kn[128 * p + 64 : 128 * p + 128]], 1)
        scores = nn(head_expand(keys, masks), qbd).reshape(8, 64, WIDTH) + tbias[None]
        w = softmax_rows(scores)
        wb = w.reshape(512, WIDTH).astype(BF)
        weights.append(w)
        weights_b.append(wb)
        query_bd.append(qbd)
        mixed_t.append(mix_keys(spread_keys(vt[:, pair], low_half, high_half), wb, first).astype(BF))
    mixed = cat(mixed_t, 1)
    branch = nn(ao_t[...], mixed)
    middle = x + branch
    hat2, scale2 = norm_rows(middle)
    n2 = (hat2 * g2 + b2).astype(BF)
    up = nn(win_t[...], n2)
    square = up * up
    c = math.sqrt(2.0 / math.pi)
    h = 0.5 + 0.5 * jnp.tanh(up * (c + (c * 0.044715) * square))
    act = up * h
    slope = h + act * (1.0 - h) * (2 * c + (6 * c * 0.044715) * square)
    act_b = act.astype(BF)
    mlp = nn(wout_t[...], act_b)
    final = middle + mlp
    out[...] = final.astype(BF).T
    valid, mix = aux[0, 0:1, :], aux[0, 1:2, :]
    for j, value in enumerate((final, branch, mlp)):
        stat[j : j + 1, :] += jnp.sum(value * value, axis=0, keepdims=True) * valid
    stat[3:4, :] += valid

    seed = cot[...].T.astype(F32) * mix
    dmlp = seed.astype(BF)
    acc[R_WOUT : R_WOUT + 512] += nt(act_b, dmlp)
    dup = (nn(mlp_out[...], dmlp) * slope).astype(BF)
    acc[R_WIN : R_WIN + 512] += nt(dup, n2)
    dn2 = nn(mlp_in[...], dup)
    fold = lambda v: v[:, :WIDTH] + v[:, WIDTH:]
    lnacc[2] += fold(dn2 * hat2)
    lnacc[3] += fold(dn2)
    dmid = seed + norm_rows_grad(dn2 * g2, hat2, scale2)
    dbranch = dmid.astype(BF)
    acc[R_AO : R_AO + WIDTH] += nt(mixed, dbranch)
    dmixed = nn(attn_out[...], dbranch).astype(BF)
    dq, dkv = [], []
    for p in range(2):
        pair = slice(128 * p, 128 * p + 128)
        dbd = cat([dmixed[:, pair] * low_tall, dmixed[:, pair] * high_tall], 0)
        values = cat([vn[128 * p : 128 * p + 64], vn[128 * p + 64 : 128 * p + 128]], 1)
        dw = nn(head_expand(values, masks), dbd).reshape(8, 64, WIDTH)
        ds = softmax_grad(weights[p], dw).reshape(512, WIDTH).astype(BF)
        dv = head_select(nt(weights_b[p], dbd)).astype(BF)
        dk = head_select(nt(ds, query_bd[p])).astype(BF)
        dq.append((mix_keys(spread_keys(kt[:, pair], low_half, high_half), ds, first) * 0.25).astype(BF))
        dkv.append(cat([dk[:, :WIDTH], dv[:, :WIDTH]], 1))
        dkv.append(cat([dk[:, WIDTH:], dv[:, WIDTH:]], 1))
    dq, dkv = cat(dq, 1), cat(dkv, 0)
    acc[R_Q : R_Q + WIDTH] += nt(n1, dq)
    grad = nn(n1, dkv)
    acc[R_KV : R_KV + WIDTH] += grad[:, :WIDTH]
    acc[R_KV + WIDTH : R_KV + 2 * WIDTH] += grad[:, WIDTH:]
    dn1 = nn(qkv_w[:, :WIDTH], dq) + nt(qkv_w[:, WIDTH:], dkv)
    lnacc[0] += fold(dn1 * hat1)
    lnacc[1] += fold(dn1)
    dx = (dmid + norm_rows_grad(dn1 * g1, hat1, scale1)).astype(BF)

    grad = nn(dx, mixed_ext)
    acc[R_SWO : R_SWO + WIDTH] += grad[:, :WIDTH]
    acc[R_SWO + WIDTH : R_SWO + 2 * WIDTH] += grad[:, WIDTH:]
    dstem = nn(dx.T, stem_t[...]).astype(BF)
    dw, dv, pdw, pdv = [], [], [], []
    for st in range(8):
        spread = head_expand(dstem[32 * st : 32 * st + 16, :WIDTH], masks)
        dw.append(nt(vv[64 * st : 64 * st + 64], spread))
        dv.append(nn(vpb[64 * st : 64 * st + 64], spread))
        spread = head_expand(dstem[32 * st + 16 : 32 * st + 32, WIDTH:], masks)
        pdw.append(nt(pv[16 * st : 16 * st + 16], spread))
        pdv.append(nn(ppb[16 * st : 16 * st + 16], spread))
    ds = softmax_grad(vp, cat(dw, 0).reshape(8, 64, WIDTH)).reshape(512, WIDTH).astype(BF)
    dkv = cat([nn(ds, qv).astype(BF), cat(dv, 0).astype(BF)], 1)
    dtok_ref[...] = nt(dkv, vis_kv[...]).astype(BF)
    grad = nn(tok.T, dkv)
    acc[R_VKV : R_VKV + WIDTH] += grad[:, :WIDTH]
    acc[R_VKV + WIDTH : R_VKV + 2 * WIDTH] += grad[:, WIDTH:]
    gv_ref[...] += nn(ds.T, vk)

    ds = softmax_grad(pp, cat(pdw, 0).reshape(8, 16, WIDTH)).reshape(WIDTH, WIDTH).astype(BF)
    dkv = cat([nn(ds, qp).astype(BF), cat(pdv, 0).astype(BF)], 1)
    dptok = nt(dkv, prop_kv[...]).astype(BF)
    grad = nn(ptok.T, dkv)
    acc[R_PKV : R_PKV + WIDTH] += grad[:, :WIDTH]
    acc[R_PKV + WIDTH : R_PKV + 2 * WIDTH] += grad[:, WIDTH:]
    gp_ref[...] += nn(ds.T, pk)
    acc[R_W2 : R_W2 + WIDTH] += nn(hidden.T, dptok)
    dhidden = nt(dptok, prop_w2[...])
    dpre = (dhidden * (gate * (1.0 + pre * (1.0 - gate)))).astype(BF)
    acc[R_W1 : R_W1 + 32] += nn(fr.T, dpre)
    dframes[...] = nt(dpre, prop_w1[...]).astype(BF)

    @pl.when(step == pl.num_programs(0) - 1)
    def _():
        acc[R_QV : R_QV + 16] = head_select(gv_ref[...]) * 0.25
        acc[R_QP : R_QP + 16] = head_select(gp_ref[...]) * 0.25
        for j in range(4):
            acc[R_LN + j : R_LN + j + 1] = jnp.sum(lnacc[j].T, axis=0, keepdims=True)
            acc[R_STAT + j : R_STAT + j + 1] = stat[j : j + 1, :WIDTH] + stat[j : j + 1, WIDTH:]


def whole(shape):
    return pl.BlockSpec(shape, lambda i, *_: (0,) * len(shape))


def block_call(grid_sizes, po, pr, frames, aux, cot, weights):
    steps = aux.shape[0]
    row = lambda i, *_: (i, 0)
    in_specs = [
        pl.BlockSpec(memory_space=pltpu.SMEM),
        pl.BlockSpec((512, WIDTH), row),
        pl.BlockSpec((512, WIDTH), row),
        pl.BlockSpec((128, frames.shape[1]), row),
        pl.BlockSpec((1, 8, 256), lambda i: (i, 0, 0)),
        pl.BlockSpec((256, WIDTH), row),
    ] + [whole(w.shape) for w in weights]
    out_shape = (
        jax.ShapeDtypeStruct((256 * steps, WIDTH), BF),
        jax.ShapeDtypeStruct((512 * steps, WIDTH), BF),
        jax.ShapeDtypeStruct((128 * steps, frames.shape[1]), BF),
        jax.ShapeDtypeStruct((R_END, WIDTH), F32),
    )
    out_specs = (
        pl.BlockSpec((256, WIDTH), row),
        pl.BlockSpec((512, WIDTH), row),
        pl.BlockSpec((128, frames.shape[1]), row),
        whole((R_END, WIDTH)),
    )
    scratch = [
        pltpu.VMEM((8, 16, WIDTH), BF),
        pltpu.VMEM((128, WIDTH), BF),
        pltpu.VMEM((128, WIDTH), BF),
        pltpu.VMEM((384, WIDTH), BF),
        pltpu.VMEM((128, WIDTH), BF),
        pltpu.VMEM((512, WIDTH), BF),
        pltpu.VMEM((128, 512), BF),
        pltpu.VMEM((128, 256), BF),
        pltpu.VMEM((4, WIDTH, WIDTH), F32),
        pltpu.VMEM((WIDTH, WIDTH), F32),
        pltpu.VMEM((WIDTH, WIDTH), F32),
        pltpu.VMEM((4, WIDTH, WIDTH), F32),
        pltpu.VMEM((8, 256), F32),
    ]
    return pl.pallas_call(
        block_kernel,
        grid=(steps,),
        in_specs=in_specs,
        out_specs=out_specs,
        out_shape=out_shape,
        scratch_shapes=scratch,
        compiler_params=pltpu.CompilerParams(vmem_limit_bytes=VMEM_LIMIT),
        name="stems_trunk",
    )(grid_sizes, po, pr, frames, aux, cot, *weights)


def make_aux(proprio_mask, token_valid, mix_weight):
    samples, seq = token_valid.shape
    steps = samples // 4
    valid = token_valid.reshape(steps, 1, 4 * seq).astype(F32)
    mix = jnp.broadcast_to(mix_weight.astype(F32)[:, None], (samples, seq)).reshape(steps, 1, 4 * seq)
    vbias = jnp.where(valid > 0, 0.0, NEG)
    pbias = jnp.where(proprio_mask.reshape(steps, 1, -1) > 0, 0.0, NEG)
    pbias = jnp.concatenate([pbias, jnp.zeros_like(pbias)], axis=2)
    rest = jnp.zeros((steps, 4, 4 * seq), F32)
    return jnp.concatenate([valid, mix, vbias, pbias, rest], axis=1)


def project_kernel(half, feats, proj, out):
    out[...] = nn(feats[...], proj[...]).astype(BF)


def project_call(half, feats, proj):
    rows, channels = feats.shape[0] // 2, feats.shape[1]
    steps = 8
    return pl.pallas_call(
        project_kernel,
        grid_spec=pltpu.PrefetchScalarGridSpec(
            num_scalar_prefetch=1,
            grid=(steps,),
            in_specs=[
                pl.BlockSpec((rows // steps, channels), lambda i, half: (half[0] * steps + i, 0)),
                whole(proj.shape),
            ],
            out_specs=pl.BlockSpec((rows // steps, WIDTH), lambda i, half: (i, 0)),
        ),
        out_shape=jax.ShapeDtypeStruct((rows, WIDTH), BF),
        compiler_params=pltpu.CompilerParams(vmem_limit_bytes=VMEM_LIMIT),
        cost_estimate=pl.CostEstimate(
            flops=2 * rows * channels * WIDTH, bytes_accessed=2 * rows * (channels + WIDTH), transcendentals=0
        ),
        name="project",
    )(half, feats, proj)


def feature_kernel(half, dtok, feats, proj, before, gsum_before, grad, gsum):
    @pl.when(pl.program_id(0) == 0)
    def _():
        gsum[...] = gsum_before[...]

    d = dtok[...]
    grad[...] = nt(d, proj[...]).astype(BF)
    gsum[...] += nn(d.T, feats[...])


def feature_kernel_first(half, dtok, feats, proj, grad, gsum):
    @pl.when(pl.program_id(0) == 0)
    def _():
        gsum[...] = jnp.zeros_like(gsum)

    d = dtok[...]
    grad[...] = nt(d, proj[...]).astype(BF)
    gsum[...] += nn(d.T, feats[...])


def feature_call(half, dtok, feats, proj, before=None):
    rows, channels = feats.shape[0] // 2, feats.shape[1]
    steps = 8
    in_specs = [
        pl.BlockSpec((rows // steps, WIDTH), lambda i, half: (i, 0)),
        pl.BlockSpec((rows // steps, channels), lambda i, half: (half[0] * steps + i, 0)),
        whole(proj.shape),
    ]
    args = (half, dtok, feats, proj)
    if before is not None:
        in_specs += [pl.BlockSpec(memory_space=pl.ANY), whole((WIDTH, channels))]
        args += tuple(before)
    return pl.pallas_call(
        feature_kernel_first if before is None else feature_kernel,
        grid_spec=pltpu.PrefetchScalarGridSpec(
            num_scalar_prefetch=1,
            grid=(steps,),
            in_specs=in_specs,
            out_specs=(
                pl.BlockSpec((rows // steps, channels), lambda i, half: (half[0] * steps + i, 0)),
                whole((WIDTH, channels)),
            ),
        ),
        out_shape=(
            jax.ShapeDtypeStruct((2 * rows, channels), BF),
            jax.ShapeDtypeStruct((WIDTH, channels), F32),
        ),
        input_output_aliases={} if before is None else {4: 0},
        compiler_params=pltpu.CompilerParams(vmem_limit_bytes=VMEM_LIMIT),
        cost_estimate=pl.CostEstimate(
            flops=4 * rows * channels * WIDTH, bytes_accessed=2 * rows * (2 * channels + WIDTH), transcendentals=0
        ),
        name="features",
    )(*args)


def unpack_kernel(
    total, gfeat, vis_query, vis_wq, prop_query, prop_wq,
    o_feat, o_vq, o_vwq, o_vkv, o_vwo, o_w1, o_w2, o_pq, o_pwq, o_pkv, o_pwo,
    o_g1, o_b1, o_qkv, o_ao, o_g2, o_b2, o_in, o_out, o_rms,
):
    def rows(start, count):
        return total[start : start + count]

    o_feat[...] = gfeat[...].T
    for o_query, o_w, query, w, start in (
        (o_vq, o_vwq, vis_query, vis_wq, R_QV),
        (o_pq, o_pwq, prop_query, prop_wq, R_QP),
    ):
        grad = rows(start, 16).astype(BF)
        o_query[...] = nt(grad, w[...])
        o_w[...] = lax.dot_general(
            query[...], grad, (((0,), (0,)), ((), ())), preferred_element_type=F32
        )
    for o, start in ((o_vkv, R_VKV), (o_pkv, R_PKV)):
        o[:, :WIDTH] = rows(start, WIDTH)
        o[:, WIDTH:] = rows(start + WIDTH, WIDTH)
    o_vwo[...] = rows(R_SWO, WIDTH).T
    o_pwo[...] = rows(R_SWO + WIDTH, WIDTH).T
    o_w1[...] = rows(R_W1, 32)
    o_w2[...] = rows(R_W2, WIDTH)
    for j in range(3):
        o_qkv[:, WIDTH * j : WIDTH * j + WIDTH] = rows(R_Q + WIDTH * j, WIDTH)
    o_ao[...] = rows(R_AO, WIDTH)
    o_in[...] = rows(R_WIN, 512).T
    o_out[...] = rows(R_WOUT, 512)
    for j, o in enumerate((o_g1, o_b1, o_g2, o_b2)):
        o[...] = rows(R_LN + j, 1)
    sums = jnp.sum(rows(R_STAT, 4), axis=1, keepdims=True)
    o_rms[...] = jnp.broadcast_to(jnp.sqrt(sums / (sums[3:4] * WIDTH)), (4, WIDTH))


def unpack_call(total, gfeat, vis_query, vis_wq, prop_query, prop_wq):
    shapes = [
        (gfeat.shape[1], WIDTH), (16, WIDTH), (WIDTH, WIDTH), (WIDTH, 256), (WIDTH, WIDTH), (32, WIDTH),
        (WIDTH, WIDTH), (16, WIDTH), (WIDTH, WIDTH), (WIDTH, 256), (WIDTH, WIDTH), (1, WIDTH), (1, WIDTH),
        (WIDTH, 384), (WIDTH, WIDTH), (1, WIDTH), (1, WIDTH), (WIDTH, 512), (512, WIDTH), (4, WIDTH),
    ]
    return pl.pallas_call(
        unpack_kernel,
        out_shape=[jax.ShapeDtypeStruct(s, F32) for s in shapes],
        compiler_params=pltpu.CompilerParams(vmem_limit_bytes=VMEM_LIMIT),
        name="unpack",
    )(total, gfeat, vis_query, vis_wq, prop_query, prop_wq)


def per_device(
    vision_feats, vision_grid, proprio, proprio_mask, token_valid, mix_weight, out_cot, feat_proj,
    vis_query, vis_wq, vis_kv, vis_wo, prop_w1, prop_w2, prop_query, prop_wq, prop_kv, prop_wo,
    ln1_gain, ln1_bias, qkv_weight, attn_out, ln2_gain, ln2_bias, mlp_in, mlp_out,
):
    me = lax.axis_index("mod").astype(jnp.int32)
    own, other = me.reshape(1), (1 - me).reshape(1)
    swap = [(0, 1), (1, 0)]
    feats = vision_feats.reshape(-1, vision_feats.shape[3])
    sent = project_call(other, feats, feat_proj)
    received = lax.ppermute(sent, "mod", swap)
    kept = project_call(own, feats, feat_proj)
    aux = make_aux(proprio_mask, token_valid, mix_weight)
    ln = jnp.stack([ln1_gain, ln1_bias, ln2_gain, ln2_bias]).astype(F32)
    weights = (
        vis_query, vis_wq, vis_kv, vis_wo, prop_w1, prop_w2, prop_query, prop_wq, prop_kv, prop_wo,
        ln, qkv_weight, attn_out, mlp_in, mlp_out,
    )
    frames = proprio.reshape(-1, proprio.shape[3])
    output, dtok, dframes, acc = block_call(
        vision_grid, kept, received, frames, aux, out_cot.reshape(-1, WIDTH), weights
    )
    dtok_other = lax.ppermute(dtok, "mod", swap)
    part = feature_call(own, dtok, feats, feat_proj)
    grad_vision, gfeat = feature_call(other, dtok_other, feats, feat_proj, part)
    total = lax.psum(acc, ("dp", "mod"))
    gfeat = lax.psum(gfeat, "dp")
    outs = unpack_call(total, gfeat, vis_query, vis_wq, prop_query, prop_wq)
    vectors = {11, 12, 15, 16}
    outs = [o.reshape(WIDTH) if j in vectors else o for j, o in enumerate(outs)]
    return (
        output.reshape(out_cot.shape),
        grad_vision.reshape(vision_feats.shape),
        dframes.reshape(proprio.shape),
        *outs[:-1],
        outs[-1][:3, 0],
    )


def solution(mesh):
    both = ("dp", "mod")
    return jax.shard_map(
        per_device,
        mesh=mesh,
        in_specs=(
            P("dp", None, None, "mod"),
            P(both, None, None),
            P(both, None, None, None),
            P(both, None, None),
            P(both, None),
            P(both),
            P(both, None, None),
            P("mod", None),
        ) + (P(),) * 18,
        out_specs=(
            P(both, None, None),
            P("dp", None, None, "mod"),
            P(both, None, None, None),
            P("mod", None),
        ) + (P(),) * 19,
        check_vma=False,
    )
```

```python
import functools
import math

import jax
import jax.numpy as jnp
from jax import lax
from jax.experimental import pallas as pl
from jax.experimental.pallas import tpu as pltpu
from jax.sharding import PartitionSpec as P

HEADS = 8
HEAD = 16
WIDTH = 128
NEG = -1e30
BF = jnp.bfloat16
F32 = jnp.float32
VMEM_LIMIT = 60 * 2**20

R_WIN, R_WOUT, R_Q, R_KV, R_AO = 0, 512, 1024, 1152, 1408
R_SWO, R_VKV, R_PKV, R_W2, R_W1 = 1536, 1792, 2048, 2304, 2432
R_QV, R_QP, R_LN, R_STAT, R_END = 2464, 2480, 2496, 2500, 2560


def nn(a, b):
    return lax.dot_general(a, b, (((1,), (0,)), ((), ())), preferred_element_type=F32)


def nt(a, b):
    return lax.dot_general(a, b, (((1,), (1,)), ((), ())), preferred_element_type=F32)


def cat(items, axis):
    return jnp.concatenate(items, axis=axis)


def lane_iota(rows, lanes):
    return lax.broadcasted_iota(jnp.int32, (rows, lanes), 1)


def head_expand(value, masks):
    rows, lanes = value.shape
    out = []
    for h in range(HEADS):
        mask = cat([cat([masks[h]] * (rows // 16), 0)] * (lanes // WIDTH), 1)
        out.append(value * mask)
    return cat(out, 0)


def head_select(full):
    rows, lanes = full.shape[0] // HEADS, full.shape[1]
    head = (lane_iota(rows, lanes) & (WIDTH - 1)) >> 4
    out = full[:rows]
    for h in range(1, HEADS):
        out = jnp.where(head == h, full[h * rows : (h + 1) * rows], out)
    return out


def softmax_rows(scores):
    peak = jnp.max(scores, axis=1, keepdims=True)
    weights = jnp.exp(scores - peak)
    return weights * (1.0 / jnp.sum(weights, axis=1, keepdims=True))


def softmax_grad(weights, grad):
    return weights * (grad - jnp.sum(weights * grad, axis=1, keepdims=True))


def mean_rows(value):
    return jnp.sum(value, axis=0, keepdims=True) * (1.0 / value.shape[0])


def norm_rows(value):
    centered = value - mean_rows(value)
    scale = lax.rsqrt(mean_rows(centered * centered) + 1e-05)
    return centered * scale, scale


def norm_rows_grad(grad, hat, scale):
    return scale * (grad - mean_rows(grad) - hat * mean_rows(grad * hat))


def spread_keys(left, low_half, high_half):
    turned = cat([left[:, 64:], left[:, :64]], 1)
    zero = jnp.zeros((HEAD, WIDTH), BF)
    out = []
    for group in range(2):
        rows = []
        for s in range(2):
            for local in range(4):
                h = group * 4 + local
                part = slice(h * HEAD, (h + 1) * HEAD)
                source = left if (s == local % 2) else turned
                block = source[part] * (high_half if local % 2 else low_half)
                rows.append(cat([block, zero] if local < 2 else [zero, block], 1))
        out.append(cat(rows, 0))
    return out


def mix_keys(spread, weights, first):
    out = []
    for group in range(2):
        full = nn(spread[group], weights[group * 256 : (group + 1) * 256])
        out.append(jnp.where(first, full[:64], full[64:]))
    return cat(out, 0)


def stem_queries(query, w_query, masks):
    value = nn(query, w_query).astype(BF)
    return head_expand(value * jnp.asarray(0.25, BF), masks)


def block_kernel(
    grid_ref, po, pr, frames, aux, cot,
    vis_query, vis_wq, vis_kv, vis_wo, prop_w1, prop_w2, prop_query, prop_wq, prop_kv, prop_wo,
    ln, qkv_w, attn_out, mlp_in, mlp_out,
    out, dtok_ref, dframes, acc,
    masks_ref, qv_ref, qp_ref, wqkv_t, ao_t, win_t, wout_t, stem_t, ln_ref,
    gv_ref, gp_ref, lnacc, stat,
):
    step = pl.program_id(0)

    @pl.when(step == 0)
    def _():
        lane = lane_iota(16, WIDTH) >> 4
        for h in range(HEADS):
            masks_ref[h] = jnp.where(lane == h, 1.0, 0.0).astype(BF)
        masks = [masks_ref[h] for h in range(HEADS)]
        qv_ref[...] = stem_queries(vis_query[...], vis_wq[...], masks)
        qp_ref[...] = stem_queries(prop_query[...], prop_wq[...], masks)
        wqkv_t[...] = qkv_w[...].T
        ao_t[...] = attn_out[...].T
        win_t[...] = mlp_in[...].T
        wout_t[...] = mlp_out[...].T
        stem_t[:, :WIDTH] = vis_wo[...].T
        stem_t[:, WIDTH:] = prop_wo[...].T
        for j in range(4):
            ln_ref[j] = jnp.broadcast_to(ln[j : j + 1, :], (WIDTH, WIDTH)).T
        acc[...] = jnp.zeros_like(acc)
        gv_ref[...] = jnp.zeros_like(gv_ref)
        gp_ref[...] = jnp.zeros_like(gp_ref)
        lnacc[...] = jnp.zeros_like(lnacc)
        stat[...] = jnp.zeros_like(stat)

    masks = [masks_ref[h] for h in range(HEADS)]
    qv, qp = qv_ref[...], qp_ref[...]
    lane = lane_iota(HEAD, WIDTH)
    low_half = jnp.where(lane < 64, 1.0, 0.0).astype(BF)
    high_half = jnp.where(lane < 64, 0.0, 1.0).astype(BF)
    first = lane_iota(64, WIDTH) < 64
    low_tall = cat([low_half] * 8, 0)
    high_tall = cat([high_half] * 8, 0)

    tok = (po[...].astype(F32) + pr[...].astype(F32)).astype(BF)
    vkv = nn(tok, vis_kv[...]).astype(BF)
    vk, vv = vkv[:, :WIDTH], vkv[:, WIDTH:]
    slot = lax.broadcasted_iota(jnp.int32, (64, WIDTH), 0)
    slot_row, slot_col = slot >> 3, slot & 7
    bias = []
    for st in range(8):
        s, t = step * 4 + st // 2, st % 2
        keep = (slot_row < grid_ref[s, t, 0]) & (slot_col < grid_ref[s, t, 1])
        bias.append(jnp.where(keep, 0.0, NEG))
    vp = softmax_rows(nt(vk, qv).reshape(8, 64, WIDTH) + cat(bias, 0).reshape(8, 64, WIDTH))
    vpb = vp.reshape(512, WIDTH).astype(BF)
    vpt = vpb.T
    zero64 = jnp.zeros((64, WIDTH), BF)
    vmixed = []
    for j in range(4):
        pair = slice(128 * j, 128 * j + 128)
        block = vv[pair]
        spread = cat([cat([block[:64], zero64], 0), cat([zero64, block[64:]], 0)], 1)
        both = head_select(nn(vpt[:, pair], spread)).astype(BF)
        vmixed += [both[:, :WIDTH], both[:, WIDTH:]]

    fr = frames[...]
    pre = nn(fr, prop_w1[...])
    gate = jax.nn.sigmoid(pre)
    hidden = (pre * gate).astype(BF)
    ptok = nn(hidden, prop_w2[...]).astype(BF)
    pkv = nn(ptok, prop_kv[...]).astype(BF)
    pk, pv = pkv[:, :WIDTH], pkv[:, WIDTH:]
    pbias = jnp.broadcast_to(aux[0, 3:4, :WIDTH], (WIDTH, WIDTH)).T
    pp = softmax_rows((nt(pk, qp) + pbias).reshape(8, 16, WIDTH))
    ppb = pp.reshape(WIDTH, WIDTH).astype(BF)
    ppt = ppb.T
    zero16 = jnp.zeros((HEAD, WIDTH), BF)
    spread = cat(
        [cat([pv[16 * j : 16 * j + 16] if j == st else zero16 for j in range(8)], 0) for st in range(8)], 1
    )
    pm = head_select(nn(ppt, spread)).astype(BF)

    rows = []
    for st in range(8):
        rows.append(cat([vmixed[st], zero16], 1))
        rows.append(cat([zero16, pm[:, WIDTH * st : WIDTH * st + WIDTH]], 1))
    mixed_ext = cat(rows, 0)
    x = nt(stem_t[...], mixed_ext)
    g1, b1, g2, b2 = [cat([ln_ref[j]] * 2, 1) for j in range(4)]
    hat1, scale1 = norm_rows(x)
    n1 = (hat1 * g1 + b1).astype(BF)
    qkv = nn(wqkv_t[...], n1).astype(BF)
    qt, kt, vt = qkv[:WIDTH] * jnp.asarray(0.25, BF), qkv[WIDTH : 2 * WIDTH], qkv[2 * WIDTH :]
    kn, vn = kt.T, vt.T
    weights, weights_b, query_bd, mixed_t = [], [], [], []
    for p in range(2):
        pair = slice(128 * p, 128 * p + 128)
        column = jnp.broadcast_to(aux[0, 2:3, pair], (WIDTH, WIDTH)).T
        tbias = jnp.where(first, column[:64], column[64:])
        qbd = cat([qt[:, pair] * low_tall, qt[:, pair] * high_tall], 0)
        keys = cat([kn[128 * p : 128 * p + 64], kn[128 * p + 64 : 128 * p + 128]], 1)
        scores = nn(head_expand(keys, masks), qbd).reshape(8, 64, WIDTH) + tbias[None]
        w = softmax_rows(scores)
        wb = w.reshape(512, WIDTH).astype(BF)
        weights.append(w)
        weights_b.append(wb)
        query_bd.append(qbd)
        mixed_t.append(mix_keys(spread_keys(vt[:, pair], low_half, high_half), wb, first).astype(BF))
    mixed = cat(mixed_t, 1)
    branch = nn(ao_t[...], mixed)
    middle = x + branch
    hat2, scale2 = norm_rows(middle)
    n2 = (hat2 * g2 + b2).astype(BF)
    up = nn(win_t[...], n2)
    square = up * up
    c = math.sqrt(2.0 / math.pi)
    h = 0.5 + 0.5 * jnp.tanh(up * (c + (c * 0.044715) * square))
    act = up * h
    slope = h + act * (1.0 - h) * (2 * c + (6 * c * 0.044715) * square)
    act_b = act.astype(BF)
    mlp = nn(wout_t[...], act_b)
    final = middle + mlp
    out[...] = final.astype(BF).T
    valid, mix = aux[0, 0:1, :], aux[0, 1:2, :]
    for j, value in enumerate((final, branch, mlp)):
        stat[j : j + 1, :] += jnp.sum(value * value, axis=0, keepdims=True) * valid
    stat[3:4, :] += valid

    seed = cot[...].T.astype(F32) * mix
    dmlp = seed.astype(BF)
    acc[R_WOUT : R_WOUT + 512] += nt(act_b, dmlp)
    dup = (nn(mlp_out[...], dmlp) * slope).astype(BF)
    acc[R_WIN : R_WIN + 512] += nt(dup, n2)
    dn2 = nn(mlp_in[...], dup)
    fold = lambda v: v[:, :WIDTH] + v[:, WIDTH:]
    lnacc[2] += fold(dn2 * hat2)
    lnacc[3] += fold(dn2)
    dmid = seed + norm_rows_grad(dn2 * g2, hat2, scale2)
    dbranch = dmid.astype(BF)
    acc[R_AO : R_AO + WIDTH] += nt(mixed, dbranch)
    dmixed = nn(attn_out[...], dbranch).astype(BF)
    dq, dkv = [], []
    for p in range(2):
        pair = slice(128 * p, 128 * p + 128)
        dbd = cat([dmixed[:, pair] * low_tall, dmixed[:, pair] * high_tall], 0)
        values = cat([vn[128 * p : 128 * p + 64], vn[128 * p + 64 : 128 * p + 128]], 1)
        dw = nn(head_expand(values, masks), dbd).reshape(8, 64, WIDTH)
        ds = softmax_grad(weights[p], dw).reshape(512, WIDTH).astype(BF)
        dv = head_select(nt(weights_b[p], dbd)).astype(BF)
        dk = head_select(nt(ds, query_bd[p])).astype(BF)
        dq.append((mix_keys(spread_keys(kt[:, pair], low_half, high_half), ds, first) * 0.25).astype(BF))
        dkv.append(cat([dk[:, :WIDTH], dv[:, :WIDTH]], 1))
        dkv.append(cat([dk[:, WIDTH:], dv[:, WIDTH:]], 1))
    dq, dkv = cat(dq, 1), cat(dkv, 0)
    acc[R_Q : R_Q + WIDTH] += nt(n1, dq)
    grad = nn(n1, dkv)
    acc[R_KV : R_KV + WIDTH] += grad[:, :WIDTH]
    acc[R_KV + WIDTH : R_KV + 2 * WIDTH] += grad[:, WIDTH:]
    dn1 = nn(qkv_w[:, :WIDTH], dq) + nt(qkv_w[:, WIDTH:], dkv)
    lnacc[0] += fold(dn1 * hat1)
    lnacc[1] += fold(dn1)
    dx = (dmid + norm_rows_grad(dn1 * g1, hat1, scale1)).astype(BF)

    grad = nn(dx, mixed_ext)
    acc[R_SWO : R_SWO + WIDTH] += grad[:, :WIDTH]
    acc[R_SWO + WIDTH : R_SWO + 2 * WIDTH] += grad[:, WIDTH:]
    dstem = nn(dx.T, stem_t[...]).astype(BF)
    dw, dv, pdw, pdv = [], [], [], []
    for st in range(8):
        spread = head_expand(dstem[32 * st : 32 * st + 16, :WIDTH], masks)
        dw.append(nt(vv[64 * st : 64 * st + 64], spread))
        dv.append(nn(vpb[64 * st : 64 * st + 64], spread))
        spread = head_expand(dstem[32 * st + 16 : 32 * st + 32, WIDTH:], masks)
        pdw.append(nt(pv[16 * st : 16 * st + 16], spread))
        pdv.append(nn(ppb[16 * st : 16 * st + 16], spread))
    ds = softmax_grad(vp, cat(dw, 0).reshape(8, 64, WIDTH)).reshape(512, WIDTH).astype(BF)
    dkv = cat([nn(ds, qv).astype(BF), cat(dv, 0).astype(BF)], 1)
    dtok_ref[...] = nt(dkv, vis_kv[...]).astype(BF)
    grad = nn(tok.T, dkv)
    acc[R_VKV : R_VKV + WIDTH] += grad[:, :WIDTH]
    acc[R_VKV + WIDTH : R_VKV + 2 * WIDTH] += grad[:, WIDTH:]
    gv_ref[...] += nn(ds.T, vk)

    ds = softmax_grad(pp, cat(pdw, 0).reshape(8, 16, WIDTH)).reshape(WIDTH, WIDTH).astype(BF)
    dkv = cat([nn(ds, qp).astype(BF), cat(pdv, 0).astype(BF)], 1)
    dptok = nt(dkv, prop_kv[...]).astype(BF)
    grad = nn(ptok.T, dkv)
    acc[R_PKV : R_PKV + WIDTH] += grad[:, :WIDTH]
    acc[R_PKV + WIDTH : R_PKV + 2 * WIDTH] += grad[:, WIDTH:]
    gp_ref[...] += nn(ds.T, pk)
    acc[R_W2 : R_W2 + WIDTH] += nn(hidden.T, dptok)
    dhidden = nt(dptok, prop_w2[...])
    dpre = (dhidden * (gate * (1.0 + pre * (1.0 - gate)))).astype(BF)
    acc[R_W1 : R_W1 + 32] += nn(fr.T, dpre)
    dframes[...] = nt(dpre, prop_w1[...]).astype(BF)

    @pl.when(step == pl.num_programs(0) - 1)
    def _():
        acc[R_QV : R_QV + 16] = head_select(gv_ref[...]) * 0.25
        acc[R_QP : R_QP + 16] = head_select(gp_ref[...]) * 0.25
        for j in range(4):
            acc[R_LN + j : R_LN + j + 1] = jnp.sum(lnacc[j].T, axis=0, keepdims=True)
            acc[R_STAT + j : R_STAT + j + 1] = stat[j : j + 1, :WIDTH] + stat[j : j + 1, WIDTH:]


def whole(shape):
    return pl.BlockSpec(shape, lambda i, *_: (0,) * len(shape))


def block_call(grid_sizes, po, pr, frames, aux, cot, weights):
    steps = aux.shape[0]
    row = lambda i, *_: (i, 0)
    in_specs = [
        pl.BlockSpec(memory_space=pltpu.SMEM),
        pl.BlockSpec((512, WIDTH), row),
        pl.BlockSpec((512, WIDTH), row),
        pl.BlockSpec((128, frames.shape[1]), row),
        pl.BlockSpec((1, 8, 256), lambda i: (i, 0, 0)),
        pl.BlockSpec((256, WIDTH), row),
    ] + [whole(w.shape) for w in weights]
    out_shape = (
        jax.ShapeDtypeStruct((256 * steps, WIDTH), BF),
        jax.ShapeDtypeStruct((512 * steps, WIDTH), BF),
        jax.ShapeDtypeStruct((128 * steps, frames.shape[1]), BF),
        jax.ShapeDtypeStruct((R_END, WIDTH), F32),
    )
    out_specs = (
        pl.BlockSpec((256, WIDTH), row),
        pl.BlockSpec((512, WIDTH), row),
        pl.BlockSpec((128, frames.shape[1]), row),
        whole((R_END, WIDTH)),
    )
    scratch = [
        pltpu.VMEM((8, 16, WIDTH), BF),
        pltpu.VMEM((128, WIDTH), BF),
        pltpu.VMEM((128, WIDTH), BF),
        pltpu.VMEM((384, WIDTH), BF),
        pltpu.VMEM((128, WIDTH), BF),
        pltpu.VMEM((512, WIDTH), BF),
        pltpu.VMEM((128, 512), BF),
        pltpu.VMEM((128, 256), BF),
        pltpu.VMEM((4, WIDTH, WIDTH), F32),
        pltpu.VMEM((WIDTH, WIDTH), F32),
        pltpu.VMEM((WIDTH, WIDTH), F32),
        pltpu.VMEM((4, WIDTH, WIDTH), F32),
        pltpu.VMEM((8, 256), F32),
    ]
    return pl.pallas_call(
        block_kernel,
        grid=(steps,),
        in_specs=in_specs,
        out_specs=out_specs,
        out_shape=out_shape,
        scratch_shapes=scratch,
        compiler_params=pltpu.CompilerParams(vmem_limit_bytes=VMEM_LIMIT),
        name="stems_trunk",
    )(grid_sizes, po, pr, frames, aux, cot, *weights)


def make_aux(proprio_mask, token_valid, mix_weight):
    samples, seq = token_valid.shape
    steps = samples // 4
    valid = token_valid.reshape(steps, 1, 4 * seq).astype(F32)
    mix = jnp.broadcast_to(mix_weight.astype(F32)[:, None], (samples, seq)).reshape(steps, 1, 4 * seq)
    vbias = jnp.where(valid > 0, 0.0, NEG)
    pbias = jnp.where(proprio_mask.reshape(steps, 1, -1) > 0, 0.0, NEG)
    pbias = jnp.concatenate([pbias, jnp.zeros_like(pbias)], axis=2)
    rest = jnp.zeros((steps, 4, 4 * seq), F32)
    return jnp.concatenate([valid, mix, vbias, pbias, rest], axis=1)


def project_kernel(half, feats, proj, out):
    out[...] = nn(feats[...], proj[...]).astype(BF)


def project_call(half, feats, proj):
    rows, channels = feats.shape[0] // 2, feats.shape[1]
    steps = 8
    return pl.pallas_call(
        project_kernel,
        grid_spec=pltpu.PrefetchScalarGridSpec(
            num_scalar_prefetch=1,
            grid=(steps,),
            in_specs=[
                pl.BlockSpec((rows // steps, channels), lambda i, half: (half[0] * steps + i, 0)),
                whole(proj.shape),
            ],
            out_specs=pl.BlockSpec((rows // steps, WIDTH), lambda i, half: (i, 0)),
        ),
        out_shape=jax.ShapeDtypeStruct((rows, WIDTH), BF),
        compiler_params=pltpu.CompilerParams(vmem_limit_bytes=VMEM_LIMIT),
        cost_estimate=pl.CostEstimate(
            flops=2 * rows * channels * WIDTH, bytes_accessed=2 * rows * (channels + WIDTH), transcendentals=0
        ),
        name="project",
    )(half, feats, proj)


def feature_kernel(half, dtok, feats, proj, before, gsum_before, grad, gsum):
    @pl.when(pl.program_id(0) == 0)
    def _():
        gsum[...] = gsum_before[...]

    d = dtok[...]
    grad[...] = nt(d, proj[...]).astype(BF)
    gsum[...] += nn(d.T, feats[...])


def feature_kernel_first(half, dtok, feats, proj, grad, gsum):
    @pl.when(pl.program_id(0) == 0)
    def _():
        gsum[...] = jnp.zeros_like(gsum)

    d = dtok[...]
    grad[...] = nt(d, proj[...]).astype(BF)
    gsum[...] += nn(d.T, feats[...])


def feature_call(half, dtok, feats, proj, before=None):
    rows, channels = feats.shape[0] // 2, feats.shape[1]
    steps = 8
    in_specs = [
        pl.BlockSpec((rows // steps, WIDTH), lambda i, half: (i, 0)),
        pl.BlockSpec((rows // steps, channels), lambda i, half: (half[0] * steps + i, 0)),
        whole(proj.shape),
    ]
    args = (half, dtok, feats, proj)
    if before is not None:
        in_specs += [pl.BlockSpec(memory_space=pl.ANY), whole((WIDTH, channels))]
        args += tuple(before)
    return pl.pallas_call(
        feature_kernel_first if before is None else feature_kernel,
        grid_spec=pltpu.PrefetchScalarGridSpec(
            num_scalar_prefetch=1,
            grid=(steps,),
            in_specs=in_specs,
            out_specs=(
                pl.BlockSpec((rows // steps, channels), lambda i, half: (half[0] * steps + i, 0)),
                whole((WIDTH, channels)),
            ),
        ),
        out_shape=(
            jax.ShapeDtypeStruct((2 * rows, channels), BF),
            jax.ShapeDtypeStruct((WIDTH, channels), F32),
        ),
        input_output_aliases={} if before is None else {4: 0},
        compiler_params=pltpu.CompilerParams(vmem_limit_bytes=VMEM_LIMIT),
        cost_estimate=pl.CostEstimate(
            flops=4 * rows * channels * WIDTH, bytes_accessed=2 * rows * (2 * channels + WIDTH), transcendentals=0
        ),
        name="features",
    )(*args)


def unpack_kernel(
    total, gfeat, vis_query, vis_wq, prop_query, prop_wq,
    o_feat, o_vq, o_vwq, o_vkv, o_vwo, o_w1, o_w2, o_pq, o_pwq, o_pkv, o_pwo,
    o_g1, o_b1, o_qkv, o_ao, o_g2, o_b2, o_in, o_out, o_rms,
):
    def rows(start, count):
        return total[start : start + count].astype(F32)

    o_feat[...] = gfeat[...].astype(F32).T
    for o_query, o_w, query, w, start in (
        (o_vq, o_vwq, vis_query, vis_wq, R_QV),
        (o_pq, o_pwq, prop_query, prop_wq, R_QP),
    ):
        grad = rows(start, 16).astype(BF)
        o_query[...] = nt(grad, w[...])
        o_w[...] = lax.dot_general(
            query[...], grad, (((0,), (0,)), ((), ())), preferred_element_type=F32
        )
    for o, start in ((o_vkv, R_VKV), (o_pkv, R_PKV)):
        o[:, :WIDTH] = rows(start, WIDTH)
        o[:, WIDTH:] = rows(start + WIDTH, WIDTH)
    o_vwo[...] = rows(R_SWO, WIDTH).T
    o_pwo[...] = rows(R_SWO + WIDTH, WIDTH).T
    o_w1[...] = rows(R_W1, 32)
    o_w2[...] = rows(R_W2, WIDTH)
    for j in range(3):
        o_qkv[:, WIDTH * j : WIDTH * j + WIDTH] = rows(R_Q + WIDTH * j, WIDTH)
    o_ao[...] = rows(R_AO, WIDTH)
    o_in[...] = rows(R_WIN, 512).T
    o_out[...] = rows(R_WOUT, 512)
    small = rows(R_LN, 16)
    for j, o in enumerate((o_g1, o_b1, o_g2, o_b2)):
        o[...] = small[j : j + 1]
    sums = jnp.sum(small[R_STAT - R_LN : R_STAT - R_LN + 4], axis=1, keepdims=True)
    o_rms[...] = jnp.broadcast_to(jnp.sqrt(sums / (sums[3:4] * WIDTH)), (4, WIDTH))


def unpack_call(total, gfeat, vis_query, vis_wq, prop_query, prop_wq):
    shapes = [
        (gfeat.shape[1], WIDTH), (16, WIDTH), (WIDTH, WIDTH), (WIDTH, 256), (WIDTH, WIDTH), (32, WIDTH),
        (WIDTH, WIDTH), (16, WIDTH), (WIDTH, WIDTH), (WIDTH, 256), (WIDTH, WIDTH), (1, WIDTH), (1, WIDTH),
        (WIDTH, 384), (WIDTH, WIDTH), (1, WIDTH), (1, WIDTH), (WIDTH, 512), (512, WIDTH), (4, WIDTH),
    ]
    return pl.pallas_call(
        unpack_kernel,
        out_shape=[jax.ShapeDtypeStruct(s, F32) for s in shapes],
        compiler_params=pltpu.CompilerParams(vmem_limit_bytes=VMEM_LIMIT),
        name="unpack",
    )(total, gfeat, vis_query, vis_wq, prop_query, prop_wq)


def reduce_kernel(n, chunk, acc, gfeat, total, gsum, send_a, recv_a, send_b, recv_b, reduced, gathered, recv_d, sem_a, sem_b, sem_c, sem_d):
    me, core = lax.axis_index("dp"), lax.axis_index("mod")
    mesh = pl.DeviceIdType.MESH
    partner = (me, 1 - core)
    half = R_END // 2
    channels = gfeat.shape[1]

    barrier = pltpu.get_barrier_semaphore()
    pl.semaphore_signal(barrier, inc=1, device_id=partner, device_id_type=mesh)

    def greet(k, carry):
        pl.semaphore_signal(barrier, inc=1, device_id=(lax.rem(me + k, n), core), device_id_type=mesh)
        return carry

    lax.fori_loop(1, n, greet, 0)
    pl.semaphore_wait(barrier, n)

    theirs = pl.ds(pl.multiple_of((1 - core) * half, 16), half)
    mine = pl.ds(pl.multiple_of(core * half, 16), half)
    send_a[...] = acc[theirs].astype(BF)
    copy = pltpu.make_async_remote_copy(
        src_ref=send_a, dst_ref=recv_a, send_sem=sem_a.at[0], recv_sem=sem_a.at[1],
        device_id=partner, device_id_type=mesh,
    )
    copy.start()
    for j in range(channels // WIDTH):
        start = half + WIDTH * j
        send_b[start : start + WIDTH] = gfeat[:, WIDTH * j : WIDTH * j + WIDTH].astype(BF)
    used = half + WIDTH * (channels // WIDTH)
    if used < n * chunk:
        send_b[used:] = jnp.zeros((n * chunk - used, WIDTH), BF)
    copy.wait()
    send_b[:half] = (acc[mine] + recv_a[...].astype(F32)).astype(BF)

    def scatter(k):
        peer = lax.rem(me + k, n)
        return pltpu.make_async_remote_copy(
            src_ref=send_b.at[pl.ds(pl.multiple_of(peer * chunk, 16), chunk)],
            dst_ref=recv_b.at[k - 1],
            send_sem=sem_b.at[0, k - 1], recv_sem=sem_b.at[1, k - 1],
            device_id=(peer, core), device_id_type=mesh,
        )

    def gather(k):
        peer = lax.rem(me + k, n)
        return pltpu.make_async_remote_copy(
            src_ref=reduced,
            dst_ref=gathered.at[pl.ds(pl.multiple_of(me * chunk, 16), chunk)],
            send_sem=sem_c.at[0, k - 1], recv_sem=sem_c.at[1, k - 1],
            device_id=(peer, core), device_id_type=mesh,
        )

    def start(make):
        def body(k, carry):
            make(k).start()
            return carry

        lax.fori_loop(1, n, body, 0)

    def finish(make):
        def body(k, carry):
            make(k).wait()
            return carry

        lax.fori_loop(1, n, body, 0)

    own = pl.ds(pl.multiple_of(me * chunk, 16), chunk)
    start(scatter)
    finish(scatter)
    result = send_b[own].astype(F32)
    result = lax.fori_loop(0, n - 1, lambda k, value: value + recv_b[k].astype(F32), result)
    reduced[...] = result.astype(BF)
    start(gather)
    gathered[own] = reduced[...]
    finish(gather)

    copy = pltpu.make_async_remote_copy(
        src_ref=gathered.at[pl.ds(0, half)], dst_ref=recv_d, send_sem=sem_d.at[0], recv_sem=sem_d.at[1],
        device_id=partner, device_id_type=mesh,
    )
    copy.start()
    total[mine] = gathered[:half]
    for j in range(channels // WIDTH):
        start_row = half + WIDTH * j
        gsum[:, WIDTH * j : WIDTH * j + WIDTH] = gathered[start_row : start_row + WIDTH]
    copy.wait()
    total[theirs] = recv_d[...]


def reduce_call(acc, gfeat, n):
    half = R_END // 2
    rows = half + WIDTH * (gfeat.shape[1] // WIDTH)
    chunk = 16 * -(-rows // (16 * n))
    vmem = pl.BlockSpec(memory_space=pltpu.VMEM)
    return pl.pallas_call(
        functools.partial(reduce_kernel, n, chunk),
        out_shape=(jax.ShapeDtypeStruct(acc.shape, BF), jax.ShapeDtypeStruct(gfeat.shape, BF)),
        in_specs=[vmem, vmem],
        out_specs=(vmem, vmem),
        scratch_shapes=[
            pltpu.VMEM((half, WIDTH), BF),
            pltpu.VMEM((half, WIDTH), BF),
            pltpu.VMEM((n * chunk, WIDTH), BF),
            pltpu.VMEM((n - 1, chunk, WIDTH), BF),
            pltpu.VMEM((chunk, WIDTH), BF),
            pltpu.VMEM((n * chunk, WIDTH), BF),
            pltpu.VMEM((half, WIDTH), BF),
            pltpu.SemaphoreType.DMA((2,)),
            pltpu.SemaphoreType.DMA((2, n - 1)),
            pltpu.SemaphoreType.DMA((2, n - 1)),
            pltpu.SemaphoreType.DMA((2,)),
        ],
        compiler_params=pltpu.CompilerParams(
            collective_id=0, has_side_effects=True, vmem_limit_bytes=VMEM_LIMIT
        ),
        name="reduce",
    )(acc, gfeat)


def per_device(
    vision_feats, vision_grid, proprio, proprio_mask, token_valid, mix_weight, out_cot, feat_proj,
    vis_query, vis_wq, vis_kv, vis_wo, prop_w1, prop_w2, prop_query, prop_wq, prop_kv, prop_wo,
    ln1_gain, ln1_bias, qkv_weight, attn_out, ln2_gain, ln2_bias, mlp_in, mlp_out,
):
    me = lax.axis_index("mod").astype(jnp.int32)
    own, other = me.reshape(1), (1 - me).reshape(1)
    swap = [(0, 1), (1, 0)]
    feats = vision_feats.reshape(-1, vision_feats.shape[3])
    sent = project_call(other, feats, feat_proj)
    received = lax.ppermute(sent, "mod", swap)
    kept = project_call(own, feats, feat_proj)
    aux = make_aux(proprio_mask, token_valid, mix_weight)
    ln = jnp.stack([ln1_gain, ln1_bias, ln2_gain, ln2_bias]).astype(F32)
    weights = (
        vis_query, vis_wq, vis_kv, vis_wo, prop_w1, prop_w2, prop_query, prop_wq, prop_kv, prop_wo,
        ln, qkv_weight, attn_out, mlp_in, mlp_out,
    )
    frames = proprio.reshape(-1, proprio.shape[3])
    output, dtok, dframes, acc = block_call(
        vision_grid, kept, received, frames, aux, out_cot.reshape(-1, WIDTH), weights
    )
    dtok_other = lax.ppermute(dtok, "mod", swap)
    part = feature_call(own, dtok, feats, feat_proj)
    grad_vision, gfeat = feature_call(other, dtok_other, feats, feat_proj, part)
    total, gfeat = reduce_call(acc, gfeat, lax.axis_size("dp"))
    outs = unpack_call(total, gfeat, vis_query, vis_wq, prop_query, prop_wq)
    vectors = {11, 12, 15, 16}
    outs = [o.reshape(WIDTH) if j in vectors else o for j, o in enumerate(outs)]
    return (
        output.reshape(out_cot.shape),
        grad_vision.reshape(vision_feats.shape),
        dframes.reshape(proprio.shape),
        *outs[:-1],
        outs[-1][:3, 0],
    )


def solution(mesh):
    both = ("dp", "mod")
    return jax.shard_map(
        per_device,
        mesh=mesh,
        in_specs=(
            P("dp", None, None, "mod"),
            P(both, None, None),
            P(both, None, None, None),
            P(both, None, None),
            P(both, None),
            P(both),
            P(both, None, None),
            P("mod", None),
        ) + (P(),) * 18,
        out_specs=(
            P(both, None, None),
            P("dp", None, None, "mod"),
            P(both, None, None, None),
            P("mod", None),
        ) + (P(),) * 19,
        check_vma=False,
    )
```

```python
import functools
import math

import jax
import jax.numpy as jnp
from jax import lax
from jax.experimental import pallas as pl
from jax.experimental.pallas import tpu as pltpu
from jax.sharding import PartitionSpec as P

HEADS = 8
HEAD = 16
WIDTH = 128
NEG = -1e30
BF = jnp.bfloat16
F32 = jnp.float32
VMEM_LIMIT = 60 * 2**20
CHAINS = 4

R_WIN, R_WOUT, R_Q, R_KV, R_AO = 0, 512, 1024, 1152, 1408
R_SWO, R_VKV, R_PKV, R_W2, R_W1 = 1536, 1792, 2048, 2304, 2432
R_QV, R_QP, R_LN, R_STAT, R_END = 2464, 2480, 2496, 2500, 2560


def nn(a, b):
    return lax.dot_general(a, b, (((1,), (0,)), ((), ())), preferred_element_type=F32)


def nt(a, b):
    return lax.dot_general(a, b, (((1,), (1,)), ((), ())), preferred_element_type=F32)


def cat(items, axis):
    return jnp.concatenate(items, axis=axis)


def lane_iota(rows, lanes):
    return lax.broadcasted_iota(jnp.int32, (rows, lanes), 1)


def head_expand(value, masks):
    rows, lanes = value.shape
    out = []
    for h in range(HEADS):
        mask = cat([cat([masks[h]] * (rows // 16), 0)] * (lanes // WIDTH), 1)
        out.append(value * mask)
    return cat(out, 0)


def head_select(full):
    rows, lanes = full.shape[0] // HEADS, full.shape[1]
    head = (lane_iota(rows, lanes) & (WIDTH - 1)) >> 4
    out = full[:rows]
    for h in range(1, HEADS):
        out = jnp.where(head == h, full[h * rows : (h + 1) * rows], out)
    return out


def softmax_rows(scores):
    peak = jnp.max(scores, axis=1, keepdims=True)
    weights = jnp.exp(scores - peak)
    return weights * (1.0 / jnp.sum(weights, axis=1, keepdims=True))


def softmax_grad(weights, grad):
    return weights * (grad - jnp.sum(weights * grad, axis=1, keepdims=True))


def mean_rows(value):
    return jnp.sum(value, axis=0, keepdims=True) * (1.0 / value.shape[0])


def norm_rows(value):
    centered = value - mean_rows(value)
    scale = lax.rsqrt(mean_rows(centered * centered) + 1e-05)
    return centered * scale, scale


def norm_rows_grad(grad, hat, scale):
    return scale * (grad - mean_rows(grad) - hat * mean_rows(grad * hat))


def spread_keys(left, low_half, high_half):
    turned = cat([left[:, 64:], left[:, :64]], 1)
    zero = jnp.zeros((HEAD, WIDTH), BF)
    out = []
    for group in range(2):
        rows = []
        for s in range(2):
            for local in range(4):
                h = group * 4 + local
                part = slice(h * HEAD, (h + 1) * HEAD)
                source = left if (s == local % 2) else turned
                block = source[part] * (high_half if local % 2 else low_half)
                rows.append(cat([block, zero] if local < 2 else [zero, block], 1))
        out.append(cat(rows, 0))
    return out


def mix_keys(spread, weights, first):
    out = []
    for group in range(2):
        full = nn(spread[group], weights[group * 256 : (group + 1) * 256])
        out.append(jnp.where(first, full[:64], full[64:]))
    return cat(out, 0)


def stem_queries(query, w_query, masks):
    value = nn(query, w_query).astype(BF)
    return head_expand(value * jnp.asarray(0.25, BF), masks)


def block_kernel(
    half, grid_ref, feats, pr, frames, aux, cot, proj,
    vis_query, vis_wq, vis_kv, vis_wo, prop_w1, prop_w2, prop_query, prop_wq, prop_kv, prop_wo,
    ln, qkv_w, attn_out, mlp_in, mlp_out,
    out, grad_feats, dtok_ref, dframes, acc, gsum,
    masks_ref, qv_ref, qp_ref, wqkv_t, ao_t, win_t, wout_t, stem_t, ln_ref,
    gv_ref, gp_ref, lnacc, stat,
):
    step = pl.program_id(0)

    @pl.when(step == 0)
    def _():
        lane = lane_iota(16, WIDTH) >> 4
        for h in range(HEADS):
            masks_ref[h] = jnp.where(lane == h, 1.0, 0.0).astype(BF)
        masks = [masks_ref[h] for h in range(HEADS)]
        qv_ref[...] = stem_queries(vis_query[...], vis_wq[...], masks)
        qp_ref[...] = stem_queries(prop_query[...], prop_wq[...], masks)
        wqkv_t[...] = qkv_w[...].T
        ao_t[...] = attn_out[...].T
        win_t[...] = mlp_in[...].T
        wout_t[...] = mlp_out[...].T
        stem_t[:, :WIDTH] = vis_wo[...].T
        stem_t[:, WIDTH:] = prop_wo[...].T
        for j in range(4):
            ln_ref[j] = jnp.broadcast_to(ln[j : j + 1, :], (WIDTH, WIDTH)).T
        acc[...] = jnp.zeros_like(acc)
        gsum[...] = jnp.zeros_like(gsum)
        gv_ref[...] = jnp.zeros_like(gv_ref)
        gp_ref[...] = jnp.zeros_like(gp_ref)
        lnacc[...] = jnp.zeros_like(lnacc)
        stat[...] = jnp.zeros_like(stat)

    masks = [masks_ref[h] for h in range(HEADS)]
    qv, qp = qv_ref[...], qp_ref[...]
    lane = lane_iota(HEAD, WIDTH)
    low_half = jnp.where(lane < 64, 1.0, 0.0).astype(BF)
    high_half = jnp.where(lane < 64, 0.0, 1.0).astype(BF)
    first = lane_iota(64, WIDTH) < 64
    low_tall = cat([low_half] * 8, 0)
    high_tall = cat([high_half] * 8, 0)


    def chain(g):
        slots = slice(512 * g, 512 * g + 512)
        kept = nn(feats[slots], proj[...]).astype(BF)
        tok = (kept.astype(F32) + pr[slots].astype(F32)).astype(BF)
        vkv = nn(tok, vis_kv[...]).astype(BF)
        vk, vv = vkv[:, :WIDTH], vkv[:, WIDTH:]
        slot = lax.broadcasted_iota(jnp.int32, (64, WIDTH), 0)
        slot_row, slot_col = slot >> 3, slot & 7
        bias = []
        for st in range(8):
            s, t = (step * CHAINS + g) * 4 + st // 2, st % 2
            keep = (slot_row < grid_ref[2 * t, s]) & (slot_col < grid_ref[2 * t + 1, s])
            bias.append(jnp.where(keep, 0.0, NEG))
        yield
        vp = softmax_rows(nt(vk, qv).reshape(8, 64, WIDTH) + cat(bias, 0).reshape(8, 64, WIDTH))
        vpb = vp.reshape(512, WIDTH).astype(BF)
        yield
        vpt = vpb.T
        zero64 = jnp.zeros((64, WIDTH), BF)
        vmixed = []
        for j in range(4):
            pair = slice(128 * j, 128 * j + 128)
            block = vv[pair]
            spread = cat([cat([block[:64], zero64], 0), cat([zero64, block[64:]], 0)], 1)
            both = head_select(nn(vpt[:, pair], spread)).astype(BF)
            vmixed += [both[:, :WIDTH], both[:, WIDTH:]]

        yield
        fr = frames[128 * g : 128 * g + 128]
        pre = nn(fr, prop_w1[...])
        gate = jax.nn.sigmoid(pre)
        hidden = (pre * gate).astype(BF)
        ptok = nn(hidden, prop_w2[...]).astype(BF)
        pkv = nn(ptok, prop_kv[...]).astype(BF)
        pk, pv = pkv[:, :WIDTH], pkv[:, WIDTH:]
        pbias = jnp.broadcast_to(aux[g, 3:4, :WIDTH], (WIDTH, WIDTH)).T
        yield
        pp = softmax_rows((nt(pk, qp) + pbias).reshape(8, 16, WIDTH))
        ppb = pp.reshape(WIDTH, WIDTH).astype(BF)
        ppt = ppb.T
        zero16 = jnp.zeros((HEAD, WIDTH), BF)
        spread = cat(
            [cat([pv[16 * j : 16 * j + 16] if j == st else zero16 for j in range(8)], 0) for st in range(8)], 1
        )
        pm = head_select(nn(ppt, spread)).astype(BF)

        yield
        rows = []
        for st in range(8):
            rows.append(cat([vmixed[st], zero16], 1))
            rows.append(cat([zero16, pm[:, WIDTH * st : WIDTH * st + WIDTH]], 1))
        mixed_ext = cat(rows, 0)
        x = nt(stem_t[...], mixed_ext)
        g1, b1, g2, b2 = [cat([ln_ref[j]] * 2, 1) for j in range(4)]
        hat1, scale1 = norm_rows(x)
        n1 = (hat1 * g1 + b1).astype(BF)
        yield
        qkv = nn(wqkv_t[...], n1).astype(BF)
        qt, kt, vt = qkv[:WIDTH] * jnp.asarray(0.25, BF), qkv[WIDTH : 2 * WIDTH], qkv[2 * WIDTH :]
        kn, vn = kt.T, vt.T
        yield
        weights, weights_b, query_bd, mixed_t = [], [], [], []
        for p in range(2):
            pair = slice(128 * p, 128 * p + 128)
            column = jnp.broadcast_to(aux[g, 2:3, pair], (WIDTH, WIDTH)).T
            tbias = jnp.where(first, column[:64], column[64:])
            qbd = cat([qt[:, pair] * low_tall, qt[:, pair] * high_tall], 0)
            keys = cat([kn[128 * p : 128 * p + 64], kn[128 * p + 64 : 128 * p + 128]], 1)
            scores = nn(head_expand(keys, masks), qbd).reshape(8, 64, WIDTH) + tbias[None]
            yield
            w = softmax_rows(scores)
            yield
            wb = w.reshape(512, WIDTH).astype(BF)
            weights.append(w)
            weights_b.append(wb)
            query_bd.append(qbd)
            mixed_t.append(mix_keys(spread_keys(vt[:, pair], low_half, high_half), wb, first).astype(BF))
        mixed = cat(mixed_t, 1)
        yield
        branch = nn(ao_t[...], mixed)
        middle = x + branch
        hat2, scale2 = norm_rows(middle)
        n2 = (hat2 * g2 + b2).astype(BF)
        yield
        up = nn(win_t[...], n2)
        yield
        square = up * up
        c = math.sqrt(2.0 / math.pi)
        h = 0.5 + 0.5 * jnp.tanh(up * (c + (c * 0.044715) * square))
        act = up * h
        slope = h + act * (1.0 - h) * (2 * c + (6 * c * 0.044715) * square)
        act_b = act.astype(BF)
        yield
        mlp = nn(wout_t[...], act_b)
        final = middle + mlp
        out[256 * g : 256 * g + 256] = final.astype(BF).T
        valid, mix = aux[g, 0:1, :], aux[g, 1:2, :]
        for j, value in enumerate((final, branch, mlp)):
            stat[j : j + 1, :] += jnp.sum(value * value, axis=0, keepdims=True) * valid
        stat[3:4, :] += valid

        yield
        seed = cot[256 * g : 256 * g + 256].T.astype(F32) * mix
        dmlp = seed.astype(BF)
        acc[R_WOUT : R_WOUT + 512] += nt(act_b, dmlp)
        dup = (nn(mlp_out[...], dmlp) * slope).astype(BF)
        acc[R_WIN : R_WIN + 512] += nt(dup, n2)
        yield
        dn2 = nn(mlp_in[...], dup)
        fold = lambda v: v[:, :WIDTH] + v[:, WIDTH:]
        lnacc[2] += fold(dn2 * hat2)
        lnacc[3] += fold(dn2)
        dmid = seed + norm_rows_grad(dn2 * g2, hat2, scale2)
        dbranch = dmid.astype(BF)
        acc[R_AO : R_AO + WIDTH] += nt(mixed, dbranch)
        yield
        dmixed = nn(attn_out[...], dbranch).astype(BF)
        yield
        dq, dkv = [], []
        for p in range(2):
            pair = slice(128 * p, 128 * p + 128)
            dbd = cat([dmixed[:, pair] * low_tall, dmixed[:, pair] * high_tall], 0)
            values = cat([vn[128 * p : 128 * p + 64], vn[128 * p + 64 : 128 * p + 128]], 1)
            dw = nn(head_expand(values, masks), dbd).reshape(8, 64, WIDTH)
            yield
            ds = softmax_grad(weights[p], dw).reshape(512, WIDTH).astype(BF)
            dv = head_select(nt(weights_b[p], dbd)).astype(BF)
            dk = head_select(nt(ds, query_bd[p])).astype(BF)
            dq.append((mix_keys(spread_keys(kt[:, pair], low_half, high_half), ds, first) * 0.25).astype(BF))
            dkv.append(cat([dk[:, :WIDTH], dv[:, :WIDTH]], 1))
            dkv.append(cat([dk[:, WIDTH:], dv[:, WIDTH:]], 1))
        dq, dkv = cat(dq, 1), cat(dkv, 0)
        yield
        acc[R_Q : R_Q + WIDTH] += nt(n1, dq)
        grad = nn(n1, dkv)
        acc[R_KV : R_KV + WIDTH] += grad[:, :WIDTH]
        acc[R_KV + WIDTH : R_KV + 2 * WIDTH] += grad[:, WIDTH:]
        dn1 = nn(qkv_w[:, :WIDTH], dq) + nt(qkv_w[:, WIDTH:], dkv)
        lnacc[0] += fold(dn1 * hat1)
        lnacc[1] += fold(dn1)
        dx = (dmid + norm_rows_grad(dn1 * g1, hat1, scale1)).astype(BF)

        yield
        grad = nn(dx, mixed_ext)
        acc[R_SWO : R_SWO + WIDTH] += grad[:, :WIDTH]
        acc[R_SWO + WIDTH : R_SWO + 2 * WIDTH] += grad[:, WIDTH:]
        dstem = nn(dx.T, stem_t[...]).astype(BF)
        dw, dv, pdw, pdv = [], [], [], []
        for st in range(8):
            spread = head_expand(dstem[32 * st : 32 * st + 16, :WIDTH], masks)
            dw.append(nt(vv[64 * st : 64 * st + 64], spread))
            dv.append(nn(vpb[64 * st : 64 * st + 64], spread))
            spread = head_expand(dstem[32 * st + 16 : 32 * st + 32, WIDTH:], masks)
            pdw.append(nt(pv[16 * st : 16 * st + 16], spread))
            pdv.append(nn(ppb[16 * st : 16 * st + 16], spread))
        yield
        ds = softmax_grad(vp, cat(dw, 0).reshape(8, 64, WIDTH)).reshape(512, WIDTH).astype(BF)
        dkv = cat([nn(ds, qv).astype(BF), cat(dv, 0).astype(BF)], 1)
        dtok = nt(dkv, vis_kv[...]).astype(BF)
        dtok_ref[slots] = dtok
        grad_feats[slots] = nt(dtok, proj[...]).astype(BF)
        gsum[...] += nn(dtok.T, feats[slots])
        grad = nn(tok.T, dkv)
        acc[R_VKV : R_VKV + WIDTH] += grad[:, :WIDTH]
        acc[R_VKV + WIDTH : R_VKV + 2 * WIDTH] += grad[:, WIDTH:]
        gv_ref[...] += nn(ds.T, vk)

        yield
        ds = softmax_grad(pp, cat(pdw, 0).reshape(8, 16, WIDTH)).reshape(WIDTH, WIDTH).astype(BF)
        dkv = cat([nn(ds, qp).astype(BF), cat(pdv, 0).astype(BF)], 1)
        dptok = nt(dkv, prop_kv[...]).astype(BF)
        grad = nn(ptok.T, dkv)
        acc[R_PKV : R_PKV + WIDTH] += grad[:, :WIDTH]
        acc[R_PKV + WIDTH : R_PKV + 2 * WIDTH] += grad[:, WIDTH:]
        gp_ref[...] += nn(ds.T, pk)
        yield
        acc[R_W2 : R_W2 + WIDTH] += nn(hidden.T, dptok)
        dhidden = nt(dptok, prop_w2[...])
        dpre = (dhidden * (gate * (1.0 + pre * (1.0 - gate)))).astype(BF)
        acc[R_W1 : R_W1 + 32] += nn(fr.T, dpre)
        dframes[128 * g : 128 * g + 128] = nt(dpre, prop_w1[...]).astype(BF)

        yield

    live = [chain(g) for g in range(CHAINS)]
    while live:
        for one in list(live):
            if next(one, live) is live:
                live.remove(one)

    @pl.when(step == pl.num_programs(0) - 1)
    def _():
        acc[R_QV : R_QV + 16] = head_select(gv_ref[...]) * 0.25
        acc[R_QP : R_QP + 16] = head_select(gp_ref[...]) * 0.25
        for j in range(4):
            acc[R_LN + j : R_LN + j + 1] = jnp.sum(lnacc[j].T, axis=0, keepdims=True)
            acc[R_STAT + j : R_STAT + j + 1] = stat[j : j + 1, :WIDTH] + stat[j : j + 1, WIDTH:]


def whole(shape):
    return pl.BlockSpec(shape, lambda i, *_: (0,) * len(shape))


def block_call(half, grid_sizes, feats, received, frames, aux, cot, proj, weights):
    steps = aux.shape[0] // CHAINS
    channels = feats.shape[1]
    row = lambda i, *_: (i, 0)
    own = lambda i, half, _: (half[0] * steps + i, 0)
    in_specs = [
        pl.BlockSpec((512 * CHAINS, channels), own),
        pl.BlockSpec((512 * CHAINS, WIDTH), row),
        pl.BlockSpec((128 * CHAINS, frames.shape[1]), row),
        pl.BlockSpec((CHAINS, 8, 256), lambda i, *_: (i, 0, 0)),
        pl.BlockSpec((256 * CHAINS, WIDTH), row),
        whole(proj.shape),
    ] + [whole(w.shape) for w in weights]
    out_shape = (
        jax.ShapeDtypeStruct((256 * CHAINS * steps, WIDTH), BF),
        jax.ShapeDtypeStruct(feats.shape, BF),
        jax.ShapeDtypeStruct((512 * CHAINS * steps, WIDTH), BF),
        jax.ShapeDtypeStruct((128 * CHAINS * steps, frames.shape[1]), BF),
        jax.ShapeDtypeStruct((R_END, WIDTH), F32),
        jax.ShapeDtypeStruct((WIDTH, channels), F32),
    )
    out_specs = (
        pl.BlockSpec((256 * CHAINS, WIDTH), row),
        pl.BlockSpec((512 * CHAINS, channels), own),
        pl.BlockSpec((512 * CHAINS, WIDTH), row),
        pl.BlockSpec((128 * CHAINS, frames.shape[1]), row),
        whole((R_END, WIDTH)),
        whole((WIDTH, channels)),
    )
    scratch = [
        pltpu.VMEM((8, 16, WIDTH), BF),
        pltpu.VMEM((128, WIDTH), BF),
        pltpu.VMEM((128, WIDTH), BF),
        pltpu.VMEM((384, WIDTH), BF),
        pltpu.VMEM((128, WIDTH), BF),
        pltpu.VMEM((512, WIDTH), BF),
        pltpu.VMEM((128, 512), BF),
        pltpu.VMEM((128, 256), BF),
        pltpu.VMEM((4, WIDTH, WIDTH), F32),
        pltpu.VMEM((WIDTH, WIDTH), F32),
        pltpu.VMEM((WIDTH, WIDTH), F32),
        pltpu.VMEM((4, WIDTH, WIDTH), F32),
        pltpu.VMEM((8, 256), F32),
    ]
    return pl.pallas_call(
        block_kernel,
        grid_spec=pltpu.PrefetchScalarGridSpec(
            num_scalar_prefetch=2,
            grid=(steps,),
            in_specs=in_specs,
            out_specs=out_specs,
            scratch_shapes=scratch,
        ),
        out_shape=out_shape,
        compiler_params=pltpu.CompilerParams(vmem_limit_bytes=VMEM_LIMIT),
        name="stems_trunk",
    )(half, grid_sizes, feats, received, frames, aux, cot, proj, *weights)


def make_aux(proprio_mask, token_valid, mix_weight):
    samples, seq = token_valid.shape
    steps = samples // 4
    valid = token_valid.reshape(steps, 1, 4 * seq).astype(F32)
    mix = jnp.broadcast_to(mix_weight.astype(F32)[:, None], (samples, seq)).reshape(steps, 1, 4 * seq)
    vbias = jnp.where(valid > 0, 0.0, NEG)
    pbias = jnp.where(proprio_mask.reshape(steps, 1, -1) > 0, 0.0, NEG)
    pbias = jnp.concatenate([pbias, jnp.zeros_like(pbias)], axis=2)
    rest = jnp.zeros((steps, 4, 4 * seq), F32)
    return jnp.concatenate([valid, mix, vbias, pbias, rest], axis=1)

PROJECT_STEPS = 4
FEATURE_STEPS = 4


def project_kernel(half, feats, proj, out):
    out[...] = nn(feats[...], proj[...]).astype(BF)


def project_call(half, feats, proj):
    rows, channels = feats.shape[0] // 2, feats.shape[1]
    steps = PROJECT_STEPS
    return pl.pallas_call(
        project_kernel,
        grid_spec=pltpu.PrefetchScalarGridSpec(
            num_scalar_prefetch=1,
            grid=(steps,),
            in_specs=[
                pl.BlockSpec((rows // steps, channels), lambda i, half: (half[0] * steps + i, 0)),
                whole(proj.shape),
            ],
            out_specs=pl.BlockSpec((rows // steps, WIDTH), lambda i, half: (i, 0)),
        ),
        out_shape=jax.ShapeDtypeStruct((rows, WIDTH), BF),
        compiler_params=pltpu.CompilerParams(vmem_limit_bytes=VMEM_LIMIT),
        cost_estimate=pl.CostEstimate(
            flops=2 * rows * channels * WIDTH, bytes_accessed=2 * rows * (channels + WIDTH), transcendentals=0
        ),
        name="project",
    )(half, feats, proj)


def feature_kernel(half, dtok, feats, proj, before, gsum_before, grad, gsum):
    @pl.when(pl.program_id(0) == 0)
    def _():
        gsum[...] = gsum_before[...]

    d = dtok[...]
    grad[...] = nt(d, proj[...]).astype(BF)
    gsum[...] += nn(d.T, feats[...])


def feature_call(half, dtok, feats, proj, grad, gsum):
    rows, channels = feats.shape[0] // 2, feats.shape[1]
    steps = FEATURE_STEPS
    return pl.pallas_call(
        feature_kernel,
        grid_spec=pltpu.PrefetchScalarGridSpec(
            num_scalar_prefetch=1,
            grid=(steps,),
            in_specs=[
                pl.BlockSpec((rows // steps, WIDTH), lambda i, half: (i, 0)),
                pl.BlockSpec((rows // steps, channels), lambda i, half: (half[0] * steps + i, 0)),
                whole(proj.shape),
                pl.BlockSpec(memory_space=pl.ANY),
                whole((WIDTH, channels)),
            ],
            out_specs=(
                pl.BlockSpec((rows // steps, channels), lambda i, half: (half[0] * steps + i, 0)),
                whole((WIDTH, channels)),
            ),
        ),
        out_shape=(
            jax.ShapeDtypeStruct((2 * rows, channels), BF),
            jax.ShapeDtypeStruct((WIDTH, channels), F32),
        ),
        input_output_aliases={4: 0},
        compiler_params=pltpu.CompilerParams(vmem_limit_bytes=VMEM_LIMIT),
        name="features",
    )(half, dtok, feats, proj, grad, gsum)


def unpack_kernel(
    total, gfeat, vis_query, vis_wq, prop_query, prop_wq,
    o_feat, o_vq, o_vwq, o_vkv, o_vwo, o_w1, o_w2, o_pq, o_pwq, o_pkv, o_pwo,
    o_g1, o_b1, o_qkv, o_ao, o_g2, o_b2, o_in, o_out, o_rms,
):
    def rows(start, count):
        return total[start : start + count].astype(F32)

    o_feat[...] = gfeat[...].astype(F32).T
    for o_query, o_w, query, w, start in (
        (o_vq, o_vwq, vis_query, vis_wq, R_QV),
        (o_pq, o_pwq, prop_query, prop_wq, R_QP),
    ):
        grad = rows(start, 16).astype(BF)
        o_query[...] = nt(grad, w[...])
        o_w[...] = lax.dot_general(
            query[...], grad, (((0,), (0,)), ((), ())), preferred_element_type=F32
        )
    for o, start in ((o_vkv, R_VKV), (o_pkv, R_PKV)):
        o[:, :WIDTH] = rows(start, WIDTH)
        o[:, WIDTH:] = rows(start + WIDTH, WIDTH)
    o_vwo[...] = rows(R_SWO, WIDTH).T
    o_pwo[...] = rows(R_SWO + WIDTH, WIDTH).T
    o_w1[...] = rows(R_W1, 32)
    o_w2[...] = rows(R_W2, WIDTH)
    for j in range(3):
        o_qkv[:, WIDTH * j : WIDTH * j + WIDTH] = rows(R_Q + WIDTH * j, WIDTH)
    o_ao[...] = rows(R_AO, WIDTH)
    o_in[...] = rows(R_WIN, 512).T
    o_out[...] = rows(R_WOUT, 512)
    small = rows(R_LN, 16)
    for j, o in enumerate((o_g1, o_b1, o_g2, o_b2)):
        o[...] = small[j : j + 1]
    sums = jnp.sum(small[R_STAT - R_LN : R_STAT - R_LN + 4], axis=1, keepdims=True)
    o_rms[...] = jnp.broadcast_to(jnp.sqrt(sums / (sums[3:4] * WIDTH)), (4, WIDTH))


def unpack_call(total, gfeat, vis_query, vis_wq, prop_query, prop_wq):
    shapes = [
        (gfeat.shape[1], WIDTH), (16, WIDTH), (WIDTH, WIDTH), (WIDTH, 256), (WIDTH, WIDTH), (32, WIDTH),
        (WIDTH, WIDTH), (16, WIDTH), (WIDTH, WIDTH), (WIDTH, 256), (WIDTH, WIDTH), (1, WIDTH), (1, WIDTH),
        (WIDTH, 384), (WIDTH, WIDTH), (1, WIDTH), (1, WIDTH), (WIDTH, 512), (512, WIDTH), (4, WIDTH),
    ]
    return pl.pallas_call(
        unpack_kernel,
        out_shape=[jax.ShapeDtypeStruct(s, F32) for s in shapes],
        compiler_params=pltpu.CompilerParams(vmem_limit_bytes=VMEM_LIMIT),
        name="unpack",
    )(total, gfeat, vis_query, vis_wq, prop_query, prop_wq)


def reduce_kernel(n, chunk, acc, gfeat, total, gsum, send_a, recv_a, send_b, recv_b, reduced, gathered, recv_d, sem_a, sem_b, sem_c, sem_d):
    me, core = lax.axis_index("dp"), lax.axis_index("mod")
    mesh = pl.DeviceIdType.MESH
    partner = (me, 1 - core)
    half = R_END // 2
    channels = gfeat.shape[1]

    barrier = pltpu.get_barrier_semaphore()
    pl.semaphore_signal(barrier, inc=1, device_id=partner, device_id_type=mesh)

    def greet(k, carry):
        pl.semaphore_signal(barrier, inc=1, device_id=(lax.rem(me + k, n), core), device_id_type=mesh)
        return carry

    lax.fori_loop(1, n, greet, 0)
    pl.semaphore_wait(barrier, n)

    theirs = pl.ds(pl.multiple_of((1 - core) * half, 16), half)
    mine = pl.ds(pl.multiple_of(core * half, 16), half)
    send_a[...] = acc[theirs].astype(BF)
    copy = pltpu.make_async_remote_copy(
        src_ref=send_a, dst_ref=recv_a, send_sem=sem_a.at[0], recv_sem=sem_a.at[1],
        device_id=partner, device_id_type=mesh,
    )
    copy.start()
    for j in range(channels // WIDTH):
        start = half + WIDTH * j
        send_b[start : start + WIDTH] = gfeat[:, WIDTH * j : WIDTH * j + WIDTH].astype(BF)
    used = half + WIDTH * (channels // WIDTH)
    if used < n * chunk:
        send_b[used:] = jnp.zeros((n * chunk - used, WIDTH), BF)
    copy.wait()
    send_b[:half] = (acc[mine] + recv_a[...].astype(F32)).astype(BF)

    def scatter(k):
        peer = lax.rem(me + k, n)
        return pltpu.make_async_remote_copy(
            src_ref=send_b.at[pl.ds(pl.multiple_of(peer * chunk, 16), chunk)],
            dst_ref=recv_b.at[k - 1],
            send_sem=sem_b.at[0, k - 1], recv_sem=sem_b.at[1, k - 1],
            device_id=(peer, core), device_id_type=mesh,
        )

    def gather(k):
        peer = lax.rem(me + k, n)
        return pltpu.make_async_remote_copy(
            src_ref=reduced,
            dst_ref=gathered.at[pl.ds(pl.multiple_of(me * chunk, 16), chunk)],
            send_sem=sem_c.at[0, k - 1], recv_sem=sem_c.at[1, k - 1],
            device_id=(peer, core), device_id_type=mesh,
        )

    def start(make):
        def body(k, carry):
            make(k).start()
            return carry

        lax.fori_loop(1, n, body, 0)

    def finish(make):
        def body(k, carry):
            make(k).wait()
            return carry

        lax.fori_loop(1, n, body, 0)

    own = pl.ds(pl.multiple_of(me * chunk, 16), chunk)
    start(scatter)
    finish(scatter)
    result = send_b[own].astype(F32)
    result = lax.fori_loop(0, n - 1, lambda k, value: value + recv_b[k].astype(F32), result)
    reduced[...] = result.astype(BF)
    start(gather)
    gathered[own] = reduced[...]
    finish(gather)

    copy = pltpu.make_async_remote_copy(
        src_ref=gathered.at[pl.ds(0, half)], dst_ref=recv_d, send_sem=sem_d.at[0], recv_sem=sem_d.at[1],
        device_id=partner, device_id_type=mesh,
    )
    copy.start()
    total[mine] = gathered[:half]
    for j in range(channels // WIDTH):
        start_row = half + WIDTH * j
        gsum[:, WIDTH * j : WIDTH * j + WIDTH] = gathered[start_row : start_row + WIDTH]
    copy.wait()
    total[theirs] = recv_d[...]


def reduce_call(acc, gfeat, n):
    half = R_END // 2
    rows = half + WIDTH * (gfeat.shape[1] // WIDTH)
    chunk = 16 * -(-rows // (16 * n))
    vmem = pl.BlockSpec(memory_space=pltpu.VMEM)
    return pl.pallas_call(
        functools.partial(reduce_kernel, n, chunk),
        out_shape=(jax.ShapeDtypeStruct(acc.shape, BF), jax.ShapeDtypeStruct(gfeat.shape, BF)),
        in_specs=[vmem, vmem],
        out_specs=(vmem, vmem),
        scratch_shapes=[
            pltpu.VMEM((half, WIDTH), BF),
            pltpu.VMEM((half, WIDTH), BF),
            pltpu.VMEM((n * chunk, WIDTH), BF),
            pltpu.VMEM((n - 1, chunk, WIDTH), BF),
            pltpu.VMEM((chunk, WIDTH), BF),
            pltpu.VMEM((n * chunk, WIDTH), BF),
            pltpu.VMEM((half, WIDTH), BF),
            pltpu.SemaphoreType.DMA((2,)),
            pltpu.SemaphoreType.DMA((2, n - 1)),
            pltpu.SemaphoreType.DMA((2, n - 1)),
            pltpu.SemaphoreType.DMA((2,)),
        ],
        compiler_params=pltpu.CompilerParams(
            collective_id=0, has_side_effects=True, vmem_limit_bytes=VMEM_LIMIT
        ),
        name="reduce",
    )(acc, gfeat)


def per_device(
    vision_feats, vision_grid, proprio, proprio_mask, token_valid, mix_weight, out_cot, feat_proj,
    vis_query, vis_wq, vis_kv, vis_wo, prop_w1, prop_w2, prop_query, prop_wq, prop_kv, prop_wo,
    ln1_gain, ln1_bias, qkv_weight, attn_out, ln2_gain, ln2_bias, mlp_in, mlp_out,
):
    me = lax.axis_index("mod").astype(jnp.int32)
    own, other = me.reshape(1), (1 - me).reshape(1)
    swap = [(0, 1), (1, 0)]
    feats = vision_feats.reshape(-1, vision_feats.shape[3])
    sent = project_call(other, feats, feat_proj)
    received = lax.ppermute(sent, "mod", swap)
    aux = make_aux(proprio_mask, token_valid, mix_weight)
    ln = jnp.stack([ln1_gain, ln1_bias, ln2_gain, ln2_bias]).astype(F32)
    weights = (
        vis_query, vis_wq, vis_kv, vis_wo, prop_w1, prop_w2, prop_query, prop_wq, prop_kv, prop_wo,
        ln, qkv_weight, attn_out, mlp_in, mlp_out,
    )
    frames = proprio.reshape(-1, proprio.shape[3])
    grid_sizes = jnp.transpose(vision_grid, (1, 2, 0)).reshape(4, -1)
    output, grad_vision, dtok, dframes, acc, gfeat = block_call(
        own, grid_sizes, feats, received, frames, aux, out_cot.reshape(-1, WIDTH), feat_proj, weights
    )
    dtok_other = lax.ppermute(dtok, "mod", swap)
    grad_vision, gfeat = feature_call(other, dtok_other, feats, feat_proj, grad_vision, gfeat)
    total, gfeat = reduce_call(acc, gfeat, lax.axis_size("dp"))
    outs = unpack_call(total, gfeat, vis_query, vis_wq, prop_query, prop_wq)
    vectors = {11, 12, 15, 16}
    outs = [o.reshape(WIDTH) if j in vectors else o for j, o in enumerate(outs)]
    return (
        output.reshape(out_cot.shape),
        grad_vision.reshape(vision_feats.shape),
        dframes.reshape(proprio.shape),
        *outs[:-1],
        outs[-1][:3, 0],
    )


def solution(mesh):
    both = ("dp", "mod")
    return jax.shard_map(
        per_device,
        mesh=mesh,
        in_specs=(
            P("dp", None, None, "mod"),
            P(both, None, None),
            P(both, None, None, None),
            P(both, None, None),
            P(both, None),
            P(both),
            P(both, None, None),
            P("mod", None),
        ) + (P(),) * 18,
        out_specs=(
            P(both, None, None),
            P("dp", None, None, "mod"),
            P(both, None, None, None),
            P("mod", None),
        ) + (P(),) * 19,
        check_vma=False,
    )
```

```python
import functools
import math

import jax
import jax.numpy as jnp
from jax import lax
from jax.experimental import pallas as pl
from jax.experimental.pallas import tpu as pltpu
from jax.sharding import PartitionSpec as P

HEADS = 8
HEAD = 16
WIDTH = 128
NEG = -1e30
BF = jnp.bfloat16
F32 = jnp.float32
VMEM_LIMIT = 60 * 2**20
CHAINS = 4

R_WIN, R_WOUT, R_Q, R_KV, R_AO = 0, 512, 1024, 1152, 1408
R_SWO, R_VKV, R_PKV, R_W2, R_W1 = 1536, 1792, 2048, 2304, 2432
R_QV, R_QP, R_LN, R_STAT, R_END = 2464, 2480, 2496, 2500, 2560


def nn(a, b):
    return lax.dot_general(a, b, (((1,), (0,)), ((), ())), preferred_element_type=F32)


def nt(a, b):
    return lax.dot_general(a, b, (((1,), (1,)), ((), ())), preferred_element_type=F32)


def cat(items, axis):
    return jnp.concatenate(items, axis=axis)


def lane_iota(rows, lanes):
    return lax.broadcasted_iota(jnp.int32, (rows, lanes), 1)


def tile_to(mask, rows, lanes):
    return cat([cat([mask] * (rows // mask.shape[0]), 0)] * (lanes // mask.shape[1]), 1)


def head_expand(value, masks):
    return cat([value * tile_to(mask, *value.shape) for mask in masks], 0)


def head_select(full, heads, period):
    rows, lanes = full.shape[0] // heads, full.shape[1]
    head = (lane_iota(rows, lanes) & (period - 1)) >> 4
    out = full[:rows]
    for h in range(1, heads):
        out = jnp.where(head == h, full[h * rows : (h + 1) * rows], out)
    return out


def turn(value):
    out = []
    for j in range(0, value.shape[1], WIDTH):
        out += [value[:, j + 64 : j + 128], value[:, j : j + 64]]
    return cat(out, 1)


def diagonal(blocks):
    out = []
    for j, block in enumerate(blocks):
        row = [block if k == j else jnp.zeros((block.shape[0], other.shape[1]), BF) for k, other in enumerate(blocks)]
        out.append(cat(row, 1))
    return cat(out, 0)


def pair_up(parts):
    return cat([cat(parts[j : j + 2], 1) for j in range(0, 8, 2)], 0)


def unpair(value, rows):
    out = []
    for j in range(4):
        part = value[rows * j : rows * j + rows]
        out += [part[:, :WIDTH], part[:, WIDTH:]]
    return cat(out, 0)


def softmax_rows(scores):
    peak = jnp.max(scores, axis=1, keepdims=True)
    weights = jnp.exp(scores - peak)
    return weights * (1.0 / jnp.sum(weights, axis=1, keepdims=True))


def softmax_grad(weights, grad):
    return weights * (grad - jnp.sum(weights * grad, axis=1, keepdims=True))


def mean_rows(value):
    return jnp.sum(value, axis=0, keepdims=True) * (1.0 / value.shape[0])


def norm_rows(value):
    centered = value - mean_rows(value)
    scale = lax.rsqrt(mean_rows(centered * centered) + 1e-05)
    return centered * scale, scale


def norm_rows_grad(grad, hat, scale):
    return scale * (grad - mean_rows(grad) - hat * mean_rows(grad * hat))


def split_samples(value, low_half, high_half):
    out = []
    for s in range(4):
        half = tile_to(high_half if s % 2 else low_half, 64, WIDTH)
        block = value[:, WIDTH * (s // 2) : WIDTH * (s // 2) + WIDTH] * half
        zero = jnp.zeros((64, WIDTH), BF)
        out.append(cat([block, zero] if s < 2 else [zero, block], 1))
    return cat(out, 0)


def gather_heads(value, turned, group, low_half, high_half):
    low_tall, high_tall = tile_to(low_half, 64, WIDTH), tile_to(high_half, 64, WIDTH)
    out = []
    for s in (0, 2):
        even, odd = slice(64 * s, 64 * s + 64), slice(64 * s + 64, 64 * s + 128)
        left, right = (value[even], turned[odd]) if group == 0 else (turned[even], value[odd])
        out.append(left * low_tall + right * high_tall)
    return cat(out, 1)


def scatter_heads(parts, low_half, high_half):
    low_tall, high_tall = tile_to(low_half, 64, WIDTH), tile_to(high_half, 64, WIDTH)
    turned = [turn(part) for part in parts]
    out = []
    for s in range(4):
        lanes = slice(WIDTH * (s // 2), WIDTH * (s // 2) + WIDTH)
        left = (turned if s % 2 else parts)[0][:, lanes]
        right = (parts if s % 2 else turned)[1][:, lanes]
        out.append(left * low_tall + right * high_tall)
    return cat(out, 0)


def spread_keys(value, turned, group, low_half, high_half):
    zero = jnp.zeros((HEAD, WIDTH), BF)
    rows = []
    for s in range(4):
        lanes = slice(WIDTH * (s // 2), WIDTH * (s // 2) + WIDTH)
        for local in range(4):
            h = group * 4 + local
            source = value if s % 2 == local % 2 else turned
            block = source[h * HEAD : (h + 1) * HEAD, lanes] * (high_half if local % 2 else low_half)
            rows.append(cat([block, zero] if local < 2 else [zero, block], 1))
    return cat(rows, 0)


def mix_keys(value, weights, low_half, high_half, first):
    turned = turn(value)
    out = []
    for group in range(2):
        full = nn(spread_keys(value, turned, group, low_half, high_half), weights[group])
        left = jnp.where(first, full[:64, :WIDTH], full[64:128, :WIDTH])
        right = jnp.where(first, full[128:192, WIDTH:], full[192:, WIDTH:])
        out.append(cat([left, right], 1))
    return cat(out, 0)


def stem_queries(query, w_query, masks):
    value = nn(query, w_query).astype(BF)
    return head_expand(value * jnp.asarray(0.25, BF), masks)


def block_kernel(
    half, grid_ref, feats, pr, frames, aux, cot, proj,
    vis_query, vis_wq, vis_kv, vis_wo, prop_w1, prop_w2, prop_query, prop_wq, prop_kv, prop_wo,
    ln, qkv_w, attn_out, mlp_in, mlp_out,
    out, grad_feats, dtok_ref, dframes, acc, gsum,
    masks_ref, qv_ref, qp_ref, wqkv_t, ao_t, win_t, wout_t, stem_t, ln_ref,
    gv_ref, gp_ref, lnacc, stat,
):
    step = pl.program_id(0)

    @pl.when(step == 0)
    def _():
        lane = lane_iota(16, WIDTH) >> 4
        for h in range(HEADS):
            masks_ref[h] = jnp.where(lane == h, 1.0, 0.0).astype(BF)
        for h in range(4):
            masks_ref[HEADS + h] = jnp.where((lane & 3) == h, 1.0, 0.0).astype(BF)
        masks = [masks_ref[h] for h in range(HEADS)]
        qv_ref[...] = diagonal([stem_queries(vis_query[...], vis_wq[...], masks)] * 2)
        qp_ref[...] = diagonal([stem_queries(prop_query[...], prop_wq[...], masks)] * 2)
        wqkv_t[...] = qkv_w[...].T
        ao_t[...] = attn_out[...].T
        win_t[...] = mlp_in[...].T
        wout_t[...] = mlp_out[...].T
        stem_t[:, :WIDTH] = vis_wo[...].T
        stem_t[:, WIDTH:] = prop_wo[...].T
        for j in range(4):
            ln_ref[j] = jnp.broadcast_to(ln[j : j + 1, :], (WIDTH, WIDTH)).T
        acc[...] = jnp.zeros_like(acc)
        gsum[...] = jnp.zeros_like(gsum)
        gv_ref[...] = jnp.zeros_like(gv_ref)
        gp_ref[...] = jnp.zeros_like(gp_ref)
        lnacc[...] = jnp.zeros_like(lnacc)
        stat[...] = jnp.zeros_like(stat)

    masks = [masks_ref[h] for h in range(HEADS)]
    masks_group = [masks_ref[HEADS + h] for h in range(4)]
    qv, qp = qv_ref[...], qp_ref[...]
    lane = lane_iota(HEAD, WIDTH)
    low_half = jnp.where(lane < 64, 1.0, 0.0).astype(BF)
    high_half = jnp.where(lane < 64, 0.0, 1.0).astype(BF)
    first = lane_iota(64, WIDTH) < 64


    def chain(g):
        slots = slice(512 * g, 512 * g + 512)
        kept = nn(feats[slots], proj[...]).astype(BF)
        tok = (kept.astype(F32) + pr[slots].astype(F32)).astype(BF)
        vkv = nn(tok, vis_kv[...]).astype(BF)
        vk, vv = vkv[:, :WIDTH], vkv[:, WIDTH:]
        slot = lax.broadcasted_iota(jnp.int32, (64, WIDTH), 0)
        slot_row, slot_col = slot >> 3, slot & 7
        bias = []
        for st in range(8):
            s, t = (step * CHAINS + g) * 4 + st // 2, st % 2
            keep = (slot_row < grid_ref[2 * t, s]) & (slot_col < grid_ref[2 * t + 1, s])
            bias.append(jnp.where(keep, 0.0, NEG))
        bias = pair_up(bias).reshape(4, 64, 256)
        vk2 = pair_up([vk[64 * st : 64 * st + 64] for st in range(8)])
        vv2 = pair_up([vv[64 * st : 64 * st + 64] for st in range(8)])
        yield
        vp = softmax_rows(nt(vk2, qv).reshape(4, 64, 256) + bias)
        vpb = vp.reshape(256, 256).astype(BF)
        yield
        vpt = vpb.T
        vmixed = [None] * 8
        for e in range(2):
            for m in range(2):
                one, two = 4 * m + e, 4 * m + 2 + e
                spread = diagonal([vv[64 * one : 64 * one + 64], vv[64 * two : 64 * two + 64]])
                lhs = vpt[WIDTH * e : WIDTH * e + WIDTH, WIDTH * m : WIDTH * m + WIDTH]
                both = head_select(nn(lhs, spread), HEADS, WIDTH).astype(BF)
                vmixed[one], vmixed[two] = both[:, :WIDTH], both[:, WIDTH:]

        yield
        fr = frames[128 * g : 128 * g + 128]
        pre = nn(fr, prop_w1[...])
        gate = jax.nn.sigmoid(pre)
        hidden = (pre * gate).astype(BF)
        ptok = nn(hidden, prop_w2[...]).astype(BF)
        pkv = nn(ptok, prop_kv[...]).astype(BF)
        pk, pv = pkv[:, :WIDTH], pkv[:, WIDTH:]
        column = jnp.broadcast_to(aux[g, 3:4, :WIDTH], (WIDTH, WIDTH)).T
        parts = lambda v: [v[HEAD * st : HEAD * st + HEAD] for st in range(8)]
        pbias = pair_up(parts(column))
        pk2, pv2 = pair_up(parts(pk)), pair_up(parts(pv))
        yield
        pp = softmax_rows((nt(pk2, qp) + pbias).reshape(4, HEAD, 256))
        ppb = pp.reshape(64, 256).astype(BF)
        ppt = ppb.T
        pmixed = [None] * 8
        for e in range(2):
            spread = diagonal([pv[HEAD * st : HEAD * st + HEAD] for st in range(e, 8, 2)])
            both = head_select(nn(ppt[WIDTH * e : WIDTH * e + WIDTH], spread), HEADS, WIDTH).astype(BF)
            for j in range(4):
                pmixed[2 * j + e] = both[:, WIDTH * j : WIDTH * j + WIDTH]

        yield
        zero16 = jnp.zeros((HEAD, WIDTH), BF)
        rows = []
        for st in range(8):
            rows.append(cat([vmixed[st], zero16], 1))
            rows.append(cat([zero16, pmixed[st]], 1))
        mixed_ext = cat(rows, 0)
        x = nt(stem_t[...], mixed_ext)
        g1, b1, g2, b2 = [cat([ln_ref[j]] * 2, 1) for j in range(4)]
        hat1, scale1 = norm_rows(x)
        n1 = (hat1 * g1 + b1).astype(BF)
        yield
        qkv = nn(wqkv_t[...], n1).astype(BF)
        qt, kt, vt = qkv[:WIDTH] * jnp.asarray(0.25, BF), qkv[WIDTH : 2 * WIDTH], qkv[2 * WIDTH :]
        kn, vn = kt.T, vt.T
        kn_turned, vn_turned = turn(kn), turn(vn)
        yield
        weights, weights_b, query_bd = [], [], []
        tbias = []
        for p in range(2):
            column = jnp.broadcast_to(aux[g, 2:3, 128 * p : 128 * p + 128], (WIDTH, WIDTH)).T
            tbias.append(jnp.where(first, column[:64], column[64:]))
        tbias = cat(tbias, 1)[None]
        for group in range(2):
            part = slice(64 * group, 64 * group + 64)
            qbd = split_samples(qt[part], low_half, high_half)
            keys = head_expand(gather_heads(kn, kn_turned, group, low_half, high_half), masks_group)
            scores = nn(keys, qbd).reshape(4, 64, 256) + tbias
            yield
            w = softmax_rows(scores)
            weights.append(w)
            weights_b.append(w.reshape(256, 256).astype(BF))
            query_bd.append(qbd)
            yield
        mixed = mix_keys(vt, weights_b, low_half, high_half, first).astype(BF)
        yield
        branch = nn(ao_t[...], mixed)
        middle = x + branch
        hat2, scale2 = norm_rows(middle)
        n2 = (hat2 * g2 + b2).astype(BF)
        yield
        up = nn(win_t[...], n2)
        yield
        square = up * up
        c = math.sqrt(2.0 / math.pi)
        h = 0.5 + 0.5 * jnp.tanh(up * (c + (c * 0.044715) * square))
        act = up * h
        slope = h + act * (1.0 - h) * (2 * c + (6 * c * 0.044715) * square)
        act_b = act.astype(BF)
        yield
        mlp = nn(wout_t[...], act_b)
        final = middle + mlp
        out[256 * g : 256 * g + 256] = final.astype(BF).T
        valid, mix = aux[g, 0:1, :], aux[g, 1:2, :]
        for j, value in enumerate((final, branch, mlp)):
            stat[j : j + 1, :] += jnp.sum(value * value, axis=0, keepdims=True) * valid
        stat[3:4, :] += valid

        yield
        seed = cot[256 * g : 256 * g + 256].T.astype(F32) * mix
        dmlp = seed.astype(BF)
        acc[R_WOUT : R_WOUT + 512] += nt(act_b, dmlp)
        dup = (nn(mlp_out[...], dmlp) * slope).astype(BF)
        acc[R_WIN : R_WIN + 512] += nt(dup, n2)
        yield
        dn2 = nn(mlp_in[...], dup)
        fold = lambda v: v[:, :WIDTH] + v[:, WIDTH:]
        lnacc[2] += fold(dn2 * hat2)
        lnacc[3] += fold(dn2)
        dmid = seed + norm_rows_grad(dn2 * g2, hat2, scale2)
        dbranch = dmid.astype(BF)
        acc[R_AO : R_AO + WIDTH] += nt(mixed, dbranch)
        yield
        dmixed = nn(attn_out[...], dbranch).astype(BF)
        yield
        ds_all, dk, dv = [], [], []
        for group in range(2):
            part = slice(64 * group, 64 * group + 64)
            dbd = split_samples(dmixed[part], low_half, high_half)
            values = head_expand(gather_heads(vn, vn_turned, group, low_half, high_half), masks_group)
            dw = nn(values, dbd).reshape(4, 64, 256)
            yield
            ds = softmax_grad(weights[group], dw).reshape(256, 256).astype(BF)
            dv.append(head_select(nt(weights_b[group], dbd), 4, 64).astype(BF))
            dk.append(head_select(nt(ds, query_bd[group]), 4, 64).astype(BF))
            ds_all.append(ds)
        dq = (mix_keys(kt, ds_all, low_half, high_half, first) * 0.25).astype(BF)
        dkv = cat([scatter_heads(dk, low_half, high_half), scatter_heads(dv, low_half, high_half)], 1)
        yield
        acc[R_Q : R_Q + WIDTH] += nt(n1, dq)
        grad = nn(n1, dkv)
        acc[R_KV : R_KV + WIDTH] += grad[:, :WIDTH]
        acc[R_KV + WIDTH : R_KV + 2 * WIDTH] += grad[:, WIDTH:]
        dn1 = nn(qkv_w[:, :WIDTH], dq) + nt(qkv_w[:, WIDTH:], dkv)
        lnacc[0] += fold(dn1 * hat1)
        lnacc[1] += fold(dn1)
        dx = (dmid + norm_rows_grad(dn1 * g1, hat1, scale1)).astype(BF)

        yield
        grad = nn(dx, mixed_ext)
        acc[R_SWO : R_SWO + WIDTH] += grad[:, :WIDTH]
        acc[R_SWO + WIDTH : R_SWO + 2 * WIDTH] += grad[:, WIDTH:]
        dstem = nn(dx.T, stem_t[...]).astype(BF)
        dw, dv, pdw, pdv = [], [], [], []
        for st in range(8):
            j, e, r = st // 2, st % 2, 32 * st
            tall, short, lanes = slice(64 * j, 64 * j + 64), slice(HEAD * j, HEAD * j + HEAD), slice(WIDTH * e, WIDTH * e + WIDTH)
            spread = head_expand(cat([dstem[r : r + 16, :WIDTH], dstem[r + 16 : r + 32, WIDTH:]], 1), masks)
            full = nt(diagonal([vv2[tall, lanes], pv2[short, lanes]]), spread)
            dw.append(full[:64])
            pdw.append(full[64:])
            full = nn(
                diagonal([vpb[tall, lanes], ppb[short, lanes]]), cat([spread[:, :WIDTH], spread[:, WIDTH:]], 0)
            ).astype(BF)
            dv.append(full[:64])
            pdv.append(full[64:])
        yield
        ds = softmax_grad(vp, pair_up(dw).reshape(4, 64, 256)).reshape(256, 256).astype(BF)
        dkv = cat([unpair(nn(ds, qv).astype(BF), 64), cat(dv, 0)], 1)
        dtok = nt(dkv, vis_kv[...]).astype(BF)
        dtok_ref[slots] = dtok
        grad_feats[slots] = nt(dtok, proj[...]).astype(BF)
        gsum[...] += nn(dtok.T, feats[slots])
        grad = nn(tok.T, dkv)
        acc[R_VKV : R_VKV + WIDTH] += grad[:, :WIDTH]
        acc[R_VKV + WIDTH : R_VKV + 2 * WIDTH] += grad[:, WIDTH:]
        full = nn(ds.T, vk2)
        gv_ref[...] += full[:WIDTH, :WIDTH] + full[WIDTH:, WIDTH:]

        yield
        ds = softmax_grad(pp, pair_up(pdw).reshape(4, HEAD, 256)).reshape(64, 256).astype(BF)
        dkv = cat([unpair(nn(ds, qp).astype(BF), HEAD), cat(pdv, 0)], 1)
        dptok = nt(dkv, prop_kv[...]).astype(BF)
        grad = nn(ptok.T, dkv)
        acc[R_PKV : R_PKV + WIDTH] += grad[:, :WIDTH]
        acc[R_PKV + WIDTH : R_PKV + 2 * WIDTH] += grad[:, WIDTH:]
        full = nn(ds.T, pk2)
        gp_ref[...] += full[:WIDTH, :WIDTH] + full[WIDTH:, WIDTH:]
        yield
        acc[R_W2 : R_W2 + WIDTH] += nn(hidden.T, dptok)
        dhidden = nt(dptok, prop_w2[...])
        dpre = (dhidden * (gate * (1.0 + pre * (1.0 - gate)))).astype(BF)
        acc[R_W1 : R_W1 + 32] += nn(fr.T, dpre)
        dframes[128 * g : 128 * g + 128] = nt(dpre, prop_w1[...]).astype(BF)

        yield

    live = [chain(g) for g in range(CHAINS)]
    while live:
        for one in list(live):
            if next(one, live) is live:
                live.remove(one)

    @pl.when(step == pl.num_programs(0) - 1)
    def _():
        acc[R_QV : R_QV + 16] = head_select(gv_ref[...], HEADS, WIDTH) * 0.25
        acc[R_QP : R_QP + 16] = head_select(gp_ref[...], HEADS, WIDTH) * 0.25
        for j in range(4):
            acc[R_LN + j : R_LN + j + 1] = jnp.sum(lnacc[j].T, axis=0, keepdims=True)
            acc[R_STAT + j : R_STAT + j + 1] = stat[j : j + 1, :WIDTH] + stat[j : j + 1, WIDTH:]


def whole(shape):
    return pl.BlockSpec(shape, lambda i, *_: (0,) * len(shape))


def block_call(half, grid_sizes, feats, received, frames, aux, cot, proj, weights):
    steps = aux.shape[0] // CHAINS
    channels = feats.shape[1]
    row = lambda i, *_: (i, 0)
    own = lambda i, half, _: (half[0] * steps + i, 0)
    in_specs = [
        pl.BlockSpec((512 * CHAINS, channels), own),
        pl.BlockSpec((512 * CHAINS, WIDTH), row),
        pl.BlockSpec((128 * CHAINS, frames.shape[1]), row),
        pl.BlockSpec((CHAINS, 8, 256), lambda i, *_: (i, 0, 0)),
        pl.BlockSpec((256 * CHAINS, WIDTH), row),
        whole(proj.shape),
    ] + [whole(w.shape) for w in weights]
    out_shape = (
        jax.ShapeDtypeStruct((256 * CHAINS * steps, WIDTH), BF),
        jax.ShapeDtypeStruct(feats.shape, BF),
        jax.ShapeDtypeStruct((512 * CHAINS * steps, WIDTH), BF),
        jax.ShapeDtypeStruct((128 * CHAINS * steps, frames.shape[1]), BF),
        jax.ShapeDtypeStruct((R_END, WIDTH), F32),
        jax.ShapeDtypeStruct((WIDTH, channels), F32),
    )
    out_specs = (
        pl.BlockSpec((256 * CHAINS, WIDTH), row),
        pl.BlockSpec((512 * CHAINS, channels), own),
        pl.BlockSpec((512 * CHAINS, WIDTH), row),
        pl.BlockSpec((128 * CHAINS, frames.shape[1]), row),
        whole((R_END, WIDTH)),
        whole((WIDTH, channels)),
    )
    scratch = [
        pltpu.VMEM((12, 16, WIDTH), BF),
        pltpu.VMEM((256, 256), BF),
        pltpu.VMEM((256, 256), BF),
        pltpu.VMEM((384, WIDTH), BF),
        pltpu.VMEM((128, WIDTH), BF),
        pltpu.VMEM((512, WIDTH), BF),
        pltpu.VMEM((128, 512), BF),
        pltpu.VMEM((128, 256), BF),
        pltpu.VMEM((4, WIDTH, WIDTH), F32),
        pltpu.VMEM((WIDTH, WIDTH), F32),
        pltpu.VMEM((WIDTH, WIDTH), F32),
        pltpu.VMEM((4, WIDTH, WIDTH), F32),
        pltpu.VMEM((8, 256), F32),
    ]
    return pl.pallas_call(
        block_kernel,
        grid_spec=pltpu.PrefetchScalarGridSpec(
            num_scalar_prefetch=2,
            grid=(steps,),
            in_specs=in_specs,
            out_specs=out_specs,
            scratch_shapes=scratch,
        ),
        out_shape=out_shape,
        compiler_params=pltpu.CompilerParams(vmem_limit_bytes=VMEM_LIMIT),
        name="stems_trunk",
    )(half, grid_sizes, feats, received, frames, aux, cot, proj, *weights)


def make_aux(proprio_mask, token_valid, mix_weight):
    samples, seq = token_valid.shape
    steps = samples // 4
    valid = token_valid.reshape(steps, 1, 4 * seq).astype(F32)
    mix = jnp.broadcast_to(mix_weight.astype(F32)[:, None], (samples, seq)).reshape(steps, 1, 4 * seq)
    vbias = jnp.where(valid > 0, 0.0, NEG)
    pbias = jnp.where(proprio_mask.reshape(steps, 1, -1) > 0, 0.0, NEG)
    pbias = jnp.concatenate([pbias, jnp.zeros_like(pbias)], axis=2)
    rest = jnp.zeros((steps, 4, 4 * seq), F32)
    return jnp.concatenate([valid, mix, vbias, pbias, rest], axis=1)

PROJECT_STEPS = 4
FEATURE_STEPS = 4


def project_kernel(half, feats, proj, out):
    out[...] = nn(feats[...], proj[...]).astype(BF)


def project_call(half, feats, proj):
    rows, channels = feats.shape[0] // 2, feats.shape[1]
    steps = PROJECT_STEPS
    return pl.pallas_call(
        project_kernel,
        grid_spec=pltpu.PrefetchScalarGridSpec(
            num_scalar_prefetch=1,
            grid=(steps,),
            in_specs=[
                pl.BlockSpec((rows // steps, channels), lambda i, half: (half[0] * steps + i, 0)),
                whole(proj.shape),
            ],
            out_specs=pl.BlockSpec((rows // steps, WIDTH), lambda i, half: (i, 0)),
        ),
        out_shape=jax.ShapeDtypeStruct((rows, WIDTH), BF),
        compiler_params=pltpu.CompilerParams(vmem_limit_bytes=VMEM_LIMIT),
        cost_estimate=pl.CostEstimate(
            flops=2 * rows * channels * WIDTH, bytes_accessed=2 * rows * (channels + WIDTH), transcendentals=0
        ),
        name="project",
    )(half, feats, proj)


def unpack_kernel(
    half, dother, proj, before, total, gfeat, vis_query, vis_wq, prop_query, prop_wq,
    o_vision, o_feat, o_vq, o_vwq, o_vkv, o_vwo, o_w1, o_w2, o_pq, o_pwq, o_pkv, o_pwo,
    o_g1, o_b1, o_qkv, o_ao, o_g2, o_b2, o_in, o_out, o_rms,
):
    o_vision[...] = nt(dother[...], proj[...]).astype(BF)

    @pl.when(pl.program_id(0) == 0)
    def _():
        def rows(start, count):
            return total[start : start + count].astype(F32)

        o_feat[...] = gfeat[...].astype(F32).T
        for o_query, o_w, query, w, start in (
            (o_vq, o_vwq, vis_query, vis_wq, R_QV),
            (o_pq, o_pwq, prop_query, prop_wq, R_QP),
        ):
            grad = rows(start, 16).astype(BF)
            o_query[...] = nt(grad, w[...])
            o_w[...] = lax.dot_general(
                query[...], grad, (((0,), (0,)), ((), ())), preferred_element_type=F32
            )
        for o, start in ((o_vkv, R_VKV), (o_pkv, R_PKV)):
            o[:, :WIDTH] = rows(start, WIDTH)
            o[:, WIDTH:] = rows(start + WIDTH, WIDTH)
        o_vwo[...] = rows(R_SWO, WIDTH).T
        o_pwo[...] = rows(R_SWO + WIDTH, WIDTH).T
        o_w1[...] = rows(R_W1, 32)
        o_w2[...] = rows(R_W2, WIDTH)
        for j in range(3):
            o_qkv[:, WIDTH * j : WIDTH * j + WIDTH] = rows(R_Q + WIDTH * j, WIDTH)
        o_ao[...] = rows(R_AO, WIDTH)
        o_in[...] = rows(R_WIN, 512).T
        o_out[...] = rows(R_WOUT, 512)
        small = rows(R_LN, 16)
        for j, o in enumerate((o_g1, o_b1, o_g2, o_b2)):
            o[...] = small[j : j + 1]
        sums = jnp.sum(small[R_STAT - R_LN : R_STAT - R_LN + 4], axis=1, keepdims=True)
        o_rms[...] = jnp.broadcast_to(jnp.sqrt(sums / (sums[3:4] * WIDTH)), (4, WIDTH))


def unpack_call(half, dother, proj, grad_vision, total, gfeat, vis_query, vis_wq, prop_query, prop_wq):
    rows, channels = dother.shape[0], proj.shape[0]
    steps = FEATURE_STEPS
    shapes = [
        (gfeat.shape[1], WIDTH), (16, WIDTH), (WIDTH, WIDTH), (WIDTH, 256), (WIDTH, WIDTH), (32, WIDTH),
        (WIDTH, WIDTH), (16, WIDTH), (WIDTH, WIDTH), (WIDTH, 256), (WIDTH, WIDTH), (1, WIDTH), (1, WIDTH),
        (WIDTH, 384), (WIDTH, WIDTH), (1, WIDTH), (1, WIDTH), (WIDTH, 512), (512, WIDTH), (4, WIDTH),
    ]
    args = (proj, grad_vision, total, gfeat, vis_query, vis_wq, prop_query, prop_wq)
    return pl.pallas_call(
        unpack_kernel,
        grid_spec=pltpu.PrefetchScalarGridSpec(
            num_scalar_prefetch=1,
            grid=(steps,),
            in_specs=[pl.BlockSpec((rows // steps, WIDTH), lambda i, half: (i, 0)), whole(proj.shape)]
            + [pl.BlockSpec(memory_space=pl.ANY)]
            + [whole(a.shape) for a in args[2:]],
            out_specs=[pl.BlockSpec((rows // steps, channels), lambda i, half: (half[0] * steps + i, 0))]
            + [whole(s) for s in shapes],
        ),
        out_shape=[jax.ShapeDtypeStruct(grad_vision.shape, BF)] + [jax.ShapeDtypeStruct(s, F32) for s in shapes],
        input_output_aliases={3: 0},
        compiler_params=pltpu.CompilerParams(vmem_limit_bytes=VMEM_LIMIT),
        name="unpack",
    )(half, dother, *args)


def finish_kernel(
    n, chunk, gchunk, acc, gsum, dtok, feats, total, gout, dother,
    fbuf, send_a, recv_a, send_b, recv_b, reduced, gathered, recv_d, send_g, recv_g, reduced_g, gathered_g,
    sem_t, sem_f, sem_a, sem_b, sem_c, sem_d, sem_bg, sem_cg,
):
    me, core = lax.axis_index("dp"), lax.axis_index("mod")
    mesh = pl.DeviceIdType.MESH
    partner = (me, 1 - core)
    half = R_END // 2
    slots, channels = fbuf.shape
    piece = slots // FEATURE_STEPS

    def remote(src, dst, send_sem, recv_sem, device):
        return pltpu.make_async_remote_copy(
            src_ref=src, dst_ref=dst, send_sem=send_sem, recv_sem=recv_sem, device_id=device, device_id_type=mesh
        )

    def rows(index, count):
        return pl.ds(pl.multiple_of(index * count, 16), count)

    barrier = pltpu.get_barrier_semaphore()
    pl.semaphore_signal(barrier, inc=1, device_id=partner, device_id_type=mesh)

    def greet(k, carry):
        pl.semaphore_signal(barrier, inc=1, device_id=(lax.rem(me + k, n), core), device_id_type=mesh)
        return carry

    lax.fori_loop(1, n, greet, 0)
    pl.semaphore_wait(barrier, n)

    send_a[...] = acc[rows(1 - core, half)].astype(BF)
    copy_a = remote(send_a, recv_a, sem_a.at[0], sem_a.at[1], partner)
    copy_a.start()
    tokens, features = [], []
    for j in range(FEATURE_STEPS):
        part = pl.ds(piece * j, piece)
        tokens.append(remote(dtok.at[part], dother.at[part], sem_t.at[0, j], sem_t.at[1, j], partner))
        tokens[j].start()
        start_row = pl.multiple_of((1 - core) * slots + piece * j, 16)
        features.append(pltpu.make_async_copy(feats.at[pl.ds(start_row, piece)], fbuf.at[part], sem_f.at[j]))
        features[j].start()
    if half < n * chunk:
        send_b[half:] = jnp.zeros((n * chunk - half, WIDTH), BF)
    copy_a.wait()
    send_b[:half] = (acc[rows(core, half)] + recv_a[...].astype(F32)).astype(BF)

    def scatter(k):
        peer = lax.rem(me + k, n)
        return remote(
            send_b.at[rows(peer, chunk)], recv_b.at[k - 1], sem_b.at[0, k - 1], sem_b.at[1, k - 1], (peer, core)
        )

    def gather(k):
        peer = lax.rem(me + k, n)
        return remote(
            reduced, gathered.at[rows(me, chunk)], sem_c.at[0, k - 1], sem_c.at[1, k - 1], (peer, core)
        )

    def scatter_g(k):
        peer = lax.rem(me + k, n)
        return remote(
            send_g.at[rows(peer, gchunk)], recv_g.at[k - 1], sem_bg.at[0, k - 1], sem_bg.at[1, k - 1], (peer, core)
        )

    def gather_g(k):
        peer = lax.rem(me + k, n)
        return remote(
            reduced_g, gathered_g.at[rows(me, gchunk)], sem_cg.at[0, k - 1], sem_cg.at[1, k - 1], (peer, core)
        )

    def forward(k):
        owner = rows(lax.rem(me + n - k, n), chunk)
        return remote(gathered.at[owner], recv_d.at[owner], sem_d.at[0, k], sem_d.at[1, k], partner)

    def each(first, step):
        def body(k, carry):
            step(k)
            return carry

        lax.fori_loop(first, n, body, 0)

    each(1, lambda k: scatter(k).start())

    grad = gsum[...]
    for j in range(FEATURE_STEPS):
        tokens[j].wait()
        features[j].wait()
        part = slice(piece * j, piece * j + piece)
        grad = grad + nn(dother[part].T, fbuf[part])
    used = WIDTH * (channels // WIDTH)
    for j in range(channels // WIDTH):
        send_g[WIDTH * j : WIDTH * j + WIDTH] = grad[:, WIDTH * j : WIDTH * j + WIDTH].astype(BF)
    if used < n * gchunk:
        send_g[used:] = jnp.zeros((n * gchunk - used, WIDTH), BF)
    each(1, lambda k: scatter_g(k).start())

    each(1, lambda k: scatter(k).wait())
    value = send_b[rows(me, chunk)].astype(F32)
    value = lax.fori_loop(0, n - 1, lambda k, v: v + recv_b[k].astype(F32), value)
    reduced[...] = value.astype(BF)
    gathered[rows(me, chunk)] = reduced[...]
    each(1, lambda k: gather(k).start())
    forward(0).start()

    each(1, lambda k: scatter_g(k).wait())
    value = send_g[rows(me, gchunk)].astype(F32)
    value = lax.fori_loop(0, n - 1, lambda k, v: v + recv_g[k].astype(F32), value)
    reduced_g[...] = value.astype(BF)
    gathered_g[rows(me, gchunk)] = reduced_g[...]
    each(1, lambda k: gather_g(k).start())

    def pass_on(k):
        gather(k).wait()
        forward(k).start()

    each(1, pass_on)
    total[rows(core, half)] = gathered[:half]
    each(1, lambda k: gather_g(k).wait())
    for j in range(channels // WIDTH):
        gout[:, WIDTH * j : WIDTH * j + WIDTH] = gathered_g[WIDTH * j : WIDTH * j + WIDTH]
    each(0, lambda k: forward(k).wait())
    total[rows(1 - core, half)] = recv_d[:half]


def finish_call(acc, gsum, dtok, feats, n):
    slots, channels = dtok.shape[0], feats.shape[1]
    half = R_END // 2
    chunk = 16 * -(-half // (16 * n))
    gchunk = 16 * -(-channels // (16 * n))
    vmem = pl.BlockSpec(memory_space=pltpu.VMEM)
    hbm = pl.BlockSpec(memory_space=pl.ANY)
    dma = pltpu.SemaphoreType.DMA
    return pl.pallas_call(
        functools.partial(finish_kernel, n, chunk, gchunk),
        out_shape=(
            jax.ShapeDtypeStruct(acc.shape, BF),
            jax.ShapeDtypeStruct(gsum.shape, BF),
            jax.ShapeDtypeStruct(dtok.shape, BF),
        ),
        in_specs=[vmem, vmem, hbm, hbm],
        out_specs=(vmem, vmem, vmem),
        scratch_shapes=[
            pltpu.VMEM((slots, channels), BF),
            pltpu.VMEM((half, WIDTH), BF),
            pltpu.VMEM((half, WIDTH), BF),
            pltpu.VMEM((n * chunk, WIDTH), BF),
            pltpu.VMEM((n - 1, chunk, WIDTH), BF),
            pltpu.VMEM((chunk, WIDTH), BF),
            pltpu.VMEM((n * chunk, WIDTH), BF),
            pltpu.VMEM((n * chunk, WIDTH), BF),
            pltpu.VMEM((n * gchunk, WIDTH), BF),
            pltpu.VMEM((n - 1, gchunk, WIDTH), BF),
            pltpu.VMEM((gchunk, WIDTH), BF),
            pltpu.VMEM((n * gchunk, WIDTH), BF),
            dma((2, FEATURE_STEPS)),
            dma((FEATURE_STEPS,)),
            dma((2,)),
            dma((2, n - 1)),
            dma((2, n - 1)),
            dma((2, n)),
            dma((2, n - 1)),
            dma((2, n - 1)),
        ],
        compiler_params=pltpu.CompilerParams(
            collective_id=0, has_side_effects=True, vmem_limit_bytes=VMEM_LIMIT
        ),
        name="finish",
    )(acc, gsum, dtok, feats)


def per_device(
    vision_feats, vision_grid, proprio, proprio_mask, token_valid, mix_weight, out_cot, feat_proj,
    vis_query, vis_wq, vis_kv, vis_wo, prop_w1, prop_w2, prop_query, prop_wq, prop_kv, prop_wo,
    ln1_gain, ln1_bias, qkv_weight, attn_out, ln2_gain, ln2_bias, mlp_in, mlp_out,
):
    me = lax.axis_index("mod").astype(jnp.int32)
    own, other = me.reshape(1), (1 - me).reshape(1)
    swap = [(0, 1), (1, 0)]
    feats = vision_feats.reshape(-1, vision_feats.shape[3])
    sent = project_call(other, feats, feat_proj)
    received = lax.ppermute(sent, "mod", swap)
    aux = make_aux(proprio_mask, token_valid, mix_weight)
    ln = jnp.stack([ln1_gain, ln1_bias, ln2_gain, ln2_bias]).astype(F32)
    weights = (
        vis_query, vis_wq, vis_kv, vis_wo, prop_w1, prop_w2, prop_query, prop_wq, prop_kv, prop_wo,
        ln, qkv_weight, attn_out, mlp_in, mlp_out,
    )
    frames = proprio.reshape(-1, proprio.shape[3])
    grid_sizes = jnp.transpose(vision_grid, (1, 2, 0)).reshape(4, -1)
    output, grad_vision, dtok, dframes, acc, gfeat = block_call(
        own, grid_sizes, feats, received, frames, aux, out_cot.reshape(-1, WIDTH), feat_proj, weights
    )
    total, gfeat, dother = finish_call(acc, gfeat, dtok, feats, lax.axis_size("dp"))
    grad_vision, *outs = unpack_call(
        other, dother, feat_proj, grad_vision, total, gfeat, vis_query, vis_wq, prop_query, prop_wq
    )
    vectors = {11, 12, 15, 16}
    outs = [o.reshape(WIDTH) if j in vectors else o for j, o in enumerate(outs)]
    return (
        output.reshape(out_cot.shape),
        grad_vision.reshape(vision_feats.shape),
        dframes.reshape(proprio.shape),
        *outs[:-1],
        outs[-1][:3, 0],
    )


def solution(mesh):
    both = ("dp", "mod")
    return jax.shard_map(
        per_device,
        mesh=mesh,
        in_specs=(
            P("dp", None, None, "mod"),
            P(both, None, None),
            P(both, None, None, None),
            P(both, None, None),
            P(both, None),
            P(both),
            P(both, None, None),
            P("mod", None),
        ) + (P(),) * 18,
        out_specs=(
            P(both, None, None),
            P("dp", None, None, "mod"),
            P(both, None, None, None),
            P("mod", None),
        ) + (P(),) * 19,
        check_vma=False,
    )
```

```python
import functools
import math

import jax
import jax.numpy as jnp
from jax import lax
from jax.experimental import pallas as pl
from jax.experimental.pallas import tpu as pltpu
from jax.sharding import PartitionSpec as P

HEADS = 8
HEAD = 16
WIDTH = 128
PROP = 32
NEG = -1e30
BF = jnp.bfloat16
F32 = jnp.float32
VMEM_LIMIT = 60 * 2**20
CHAINS = 8
FF_PART = 256

R_WIN, R_WOUT, R_Q, R_KV, R_AO = 0, 512, 1024, 1152, 1408
R_SWO, R_VKV, R_PKV, R_W2, R_W1 = 1536, 1792, 2048, 2304, 2432
R_QV, R_QP, R_LN, R_STAT, R_END = 2464, 2480, 2496, 2500, 2560


def nn(a, b):
    return lax.dot_general(a, b, (((1,), (0,)), ((), ())), preferred_element_type=F32)


def nt(a, b):
    return lax.dot_general(a, b, (((1,), (1,)), ((), ())), preferred_element_type=F32)


def cat(items, axis):
    return jnp.concatenate(items, axis=axis)


def lane_iota(rows, lanes):
    return lax.broadcasted_iota(jnp.int32, (rows, lanes), 1)


def tile_to(mask, rows, lanes):
    return cat([cat([mask] * (rows // mask.shape[0]), 0)] * (lanes // mask.shape[1]), 1)


def head_expand(value, masks):
    return cat([value * tile_to(mask, *value.shape) for mask in masks], 0)


def head_select(full, heads, period):
    rows, lanes = full.shape[0] // heads, full.shape[1]
    head = (lane_iota(rows, lanes) & (period - 1)) >> 4
    out = full[:rows]
    for h in range(1, heads):
        out = jnp.where(head == h, full[h * rows : (h + 1) * rows], out)
    return out


def turn(value):
    out = []
    for j in range(0, value.shape[1], WIDTH):
        out += [value[:, j + 64 : j + 128], value[:, j : j + 64]]
    return cat(out, 1)


def diagonal(blocks):
    out = []
    for j, block in enumerate(blocks):
        row = [block if k == j else jnp.zeros((block.shape[0], other.shape[1]), BF) for k, other in enumerate(blocks)]
        out.append(cat(row, 1))
    return cat(out, 0)


def pair_up(parts):
    return cat([cat(parts[j : j + 2], 1) for j in range(0, 8, 2)], 0)


def unpair(value, rows):
    out = []
    for j in range(4):
        part = value[rows * j : rows * j + rows]
        out += [part[:, :WIDTH], part[:, WIDTH:]]
    return cat(out, 0)


def softmax_rows(scores):
    peak = jnp.max(scores, axis=1, keepdims=True)
    weights = jnp.exp(scores - peak)
    return weights * (1.0 / jnp.sum(weights, axis=1, keepdims=True))


def softmax_grad(weights, grad):
    return weights * (grad - jnp.sum(weights * grad, axis=1, keepdims=True))


def mean_rows(value):
    return jnp.sum(value, axis=0, keepdims=True) * (1.0 / value.shape[0])


def norm_rows(value):
    centered = value - mean_rows(value)
    scale = lax.rsqrt(mean_rows(centered * centered) + 1e-05)
    return centered * scale, scale


def norm_rows_grad(grad, hat, scale):
    return scale * (grad - mean_rows(grad) - hat * mean_rows(grad * hat))


def split_samples(value, low_half, high_half):
    out = []
    for s in range(4):
        half = tile_to(high_half if s % 2 else low_half, 64, WIDTH)
        block = value[:, WIDTH * (s // 2) : WIDTH * (s // 2) + WIDTH] * half
        zero = jnp.zeros((64, WIDTH), BF)
        out.append(cat([block, zero] if s < 2 else [zero, block], 1))
    return cat(out, 0)


def gather_heads(value, turned, group, low_half, high_half):
    low_tall, high_tall = tile_to(low_half, 64, WIDTH), tile_to(high_half, 64, WIDTH)
    out = []
    for s in (0, 2):
        even, odd = slice(64 * s, 64 * s + 64), slice(64 * s + 64, 64 * s + 128)
        left, right = (value[even], turned[odd]) if group == 0 else (turned[even], value[odd])
        out.append(left * low_tall + right * high_tall)
    return cat(out, 1)


def scatter_heads(parts, low_half, high_half):
    low_tall, high_tall = tile_to(low_half, 64, WIDTH), tile_to(high_half, 64, WIDTH)
    turned = [turn(part) for part in parts]
    out = []
    for s in range(4):
        lanes = slice(WIDTH * (s // 2), WIDTH * (s // 2) + WIDTH)
        left = (turned if s % 2 else parts)[0][:, lanes]
        right = (parts if s % 2 else turned)[1][:, lanes]
        out.append(left * low_tall + right * high_tall)
    return cat(out, 0)


def spread_keys(value, turned, group, low_half, high_half):
    zero = jnp.zeros((HEAD, WIDTH), BF)
    rows = []
    for s in range(4):
        lanes = slice(WIDTH * (s // 2), WIDTH * (s // 2) + WIDTH)
        for local in range(4):
            h = group * 4 + local
            source = value if s % 2 == local % 2 else turned
            block = source[h * HEAD : (h + 1) * HEAD, lanes] * (high_half if local % 2 else low_half)
            rows.append(cat([block, zero] if local < 2 else [zero, block], 1))
    return cat(rows, 0)


def mix_keys(value, weights, low_half, high_half, first):
    turned = turn(value)
    out = []
    for group in range(2):
        full = nn(spread_keys(value, turned, group, low_half, high_half), weights[group])
        left = jnp.where(first, full[:64, :WIDTH], full[64:128, :WIDTH])
        right = jnp.where(first, full[128:192, WIDTH:], full[192:, WIDTH:])
        out.append(cat([left, right], 1))
    return cat(out, 0)


def stem_queries(query, w_query, masks):
    value = nn(query, w_query).astype(BF)
    return head_expand(value * jnp.asarray(0.25, BF), masks)


def block_kernel(
    half, grid_ref, feats, pr, frames, aux, cot, proj,
    vis_query, vis_wq, vis_kv, vis_wo, prop_w1, prop_w2, prop_query, prop_wq, prop_kv, prop_wo,
    ln, qkv_w, attn_out, mlp_in, mlp_out,
    out, grad_feats, dtok_ref, dframes, acc_out, gsum,
    masks_ref, qv_ref, qp_ref, wqkv_t, ao_t, win_t, wout_t, stem_t, ln_ref,
    gv_ref, gp_ref, lnacc, stat, acc, fr_ref, df_ref,
):
    step = pl.program_id(0)

    @pl.when(step == 0)
    def _():
        lane = lane_iota(16, WIDTH) >> 4
        for h in range(HEADS):
            masks_ref[h] = jnp.where(lane == h, 1.0, 0.0).astype(BF)
        for h in range(4):
            masks_ref[HEADS + h] = jnp.where((lane & 3) == h, 1.0, 0.0).astype(BF)
        masks = [masks_ref[h] for h in range(HEADS)]
        qv_ref[...] = diagonal([stem_queries(vis_query[...], vis_wq[...], masks)] * 2)
        qp_ref[...] = diagonal([stem_queries(prop_query[...], prop_wq[...], masks)] * 2)
        wqkv_t[...] = qkv_w[...].T
        ao_t[...] = attn_out[...].T
        win_t[...] = mlp_in[...].T
        wout_t[...] = mlp_out[...].T
        stem_t[:, :WIDTH] = vis_wo[...].T
        stem_t[:, WIDTH:] = prop_wo[...].T
        for j in range(4):
            ln_ref[j] = jnp.broadcast_to(ln[j : j + 1, :], (WIDTH, WIDTH)).T
        for j in range(frames.shape[0] // PROP):
            block = frames[PROP * j : PROP * j + PROP].astype(F32).T
            fr_ref[pl.ds(j, block.shape[0], stride=frames.shape[0] // PROP)] = block
        acc[...] = jnp.zeros_like(acc)
        gsum[...] = jnp.zeros_like(gsum)
        gv_ref[...] = jnp.zeros_like(gv_ref)
        gp_ref[...] = jnp.zeros_like(gp_ref)
        lnacc[...] = jnp.zeros_like(lnacc)
        stat[...] = jnp.zeros_like(stat)

    masks = [masks_ref[h] for h in range(HEADS)]
    masks_group = [masks_ref[HEADS + h] for h in range(4)]
    qv, qp = qv_ref[...], qp_ref[...]
    lane = lane_iota(HEAD, WIDTH)
    low_half = jnp.where(lane < 64, 1.0, 0.0).astype(BF)
    high_half = jnp.where(lane < 64, 0.0, 1.0).astype(BF)
    first = lane_iota(64, WIDTH) < 64


    def chain(g):
        slots = slice(512 * g, 512 * g + 512)
        kept = nn(feats[slots], proj[...]).astype(BF)
        tok = (kept.astype(F32) + pr[slots].astype(F32)).astype(BF)
        vkv = nn(tok, vis_kv[...]).astype(BF)
        vk, vv = vkv[:, :WIDTH], vkv[:, WIDTH:]
        slot = lax.broadcasted_iota(jnp.int32, (64, WIDTH), 0)
        slot_row, slot_col = slot >> 3, slot & 7
        bias = []
        for st in range(8):
            s, t = (step * CHAINS + g) * 4 + st // 2, st % 2
            keep = (slot_row < grid_ref[2 * t, s]) & (slot_col < grid_ref[2 * t + 1, s])
            bias.append(jnp.where(keep, 0.0, NEG))
        bias = pair_up(bias).reshape(4, 64, 256)
        vk2 = pair_up([vk[64 * st : 64 * st + 64] for st in range(8)])
        vv2 = pair_up([vv[64 * st : 64 * st + 64] for st in range(8)])
        yield
        vp = softmax_rows(nt(vk2, qv).reshape(4, 64, 256) + bias)
        vpb = vp.reshape(256, 256).astype(BF)
        yield
        vpt = vpb.T
        vmixed = [None] * 8
        for e in range(2):
            for m in range(2):
                one, two = 4 * m + e, 4 * m + 2 + e
                spread = diagonal([vv[64 * one : 64 * one + 64], vv[64 * two : 64 * two + 64]])
                lhs = vpt[WIDTH * e : WIDTH * e + WIDTH, WIDTH * m : WIDTH * m + WIDTH]
                both = head_select(nn(lhs, spread), HEADS, WIDTH).astype(BF)
                vmixed[one], vmixed[two] = both[:, :WIDTH], both[:, WIDTH:]

        yield
        fr_rows = pl.ds(pl.multiple_of((step * CHAINS + g) * 128, 128), 128)
        fr = fr_ref[fr_rows].astype(BF)
        pre = nn(fr, prop_w1[...])
        gate = jax.nn.sigmoid(pre)
        hidden = (pre * gate).astype(BF)
        ptok = nn(hidden, prop_w2[...]).astype(BF)
        pkv = nn(ptok, prop_kv[...]).astype(BF)
        pk, pv = pkv[:, :WIDTH], pkv[:, WIDTH:]
        column = jnp.broadcast_to(aux[g, 3:4, :WIDTH], (WIDTH, WIDTH)).T
        parts = lambda v: [v[HEAD * st : HEAD * st + HEAD] for st in range(8)]
        pbias = pair_up(parts(column))
        pk2, pv2 = pair_up(parts(pk)), pair_up(parts(pv))
        yield
        pp = softmax_rows((nt(pk2, qp) + pbias).reshape(4, HEAD, 256))
        ppb = pp.reshape(64, 256).astype(BF)
        ppt = ppb.T
        pmixed = [None] * 8
        for e in range(2):
            spread = diagonal([pv[HEAD * st : HEAD * st + HEAD] for st in range(e, 8, 2)])
            both = head_select(nn(ppt[WIDTH * e : WIDTH * e + WIDTH], spread), HEADS, WIDTH).astype(BF)
            for j in range(4):
                pmixed[2 * j + e] = both[:, WIDTH * j : WIDTH * j + WIDTH]

        yield
        zero16 = jnp.zeros((HEAD, WIDTH), BF)
        rows = []
        for st in range(8):
            rows.append(cat([vmixed[st], zero16], 1))
            rows.append(cat([zero16, pmixed[st]], 1))
        mixed_ext = cat(rows, 0)
        x = nt(stem_t[...], mixed_ext)
        g1, b1, g2, b2 = [cat([ln_ref[j]] * 2, 1) for j in range(4)]
        hat1, scale1 = norm_rows(x)
        n1 = (hat1 * g1 + b1).astype(BF)
        yield
        qkv = nn(wqkv_t[...], n1).astype(BF)
        qt, kt, vt = qkv[:WIDTH] * jnp.asarray(0.25, BF), qkv[WIDTH : 2 * WIDTH], qkv[2 * WIDTH :]
        kn, vn = kt.T, vt.T
        kn_turned, vn_turned = turn(kn), turn(vn)
        yield
        weights, weights_b, query_bd = [], [], []
        tbias = []
        for p in range(2):
            column = jnp.broadcast_to(aux[g, 2:3, 128 * p : 128 * p + 128], (WIDTH, WIDTH)).T
            tbias.append(jnp.where(first, column[:64], column[64:]))
        tbias = cat(tbias, 1)[None]
        for group in range(2):
            part = slice(64 * group, 64 * group + 64)
            qbd = split_samples(qt[part], low_half, high_half)
            keys = head_expand(gather_heads(kn, kn_turned, group, low_half, high_half), masks_group)
            scores = nn(keys, qbd).reshape(4, 64, 256) + tbias
            yield
            w = softmax_rows(scores)
            weights.append(w)
            weights_b.append(w.reshape(256, 256).astype(BF))
            query_bd.append(qbd)
            yield
        mixed = mix_keys(vt, weights_b, low_half, high_half, first).astype(BF)
        yield
        branch = nn(ao_t[...], mixed)
        middle = x + branch
        hat2, scale2 = norm_rows(middle)
        n2 = (hat2 * g2 + b2).astype(BF)
        yield
        c = math.sqrt(2.0 / math.pi)
        seed = cot[256 * g : 256 * g + 256].T.astype(F32) * aux[g, 1:2, :]
        dmlp = seed.astype(BF)
        mlp, dn2, act_all, dup_all = 0.0, 0.0, [], []
        for j in range(512 // FF_PART):
            part = slice(FF_PART * j, FF_PART * j + FF_PART)
            up = nn(win_t[part], n2)
            yield
            square = up * up
            h = 0.5 + 0.5 * jnp.tanh(up * (c + (c * 0.044715) * square))
            act = up * h
            slope = h + act * (1.0 - h) * (2 * c + (6 * c * 0.044715) * square)
            act_b = act.astype(BF)
            mlp = mlp + nn(wout_t[:, part], act_b)
            dup = (nn(mlp_out[part], dmlp) * slope).astype(BF)
            yield
            dn2 = dn2 + nn(mlp_in[:, part], dup)
            acc[R_WOUT + FF_PART * j : R_WOUT + FF_PART * j + FF_PART] += nt(act_b, dmlp)
            acc[R_WIN + FF_PART * j : R_WIN + FF_PART * j + FF_PART] += nt(dup, n2)
            yield
        final = middle + mlp
        out[256 * g : 256 * g + 256] = final.astype(BF).T
        valid = aux[g, 0:1, :]
        for j, value in enumerate((final, branch, mlp)):
            stat[j : j + 1, :] += jnp.sum(value * value, axis=0, keepdims=True) * valid
        stat[3:4, :] += valid

        yield
        fold = lambda v: v[:, :WIDTH] + v[:, WIDTH:]
        lnacc[2] += fold(dn2 * hat2)
        lnacc[3] += fold(dn2)
        dmid = seed + norm_rows_grad(dn2 * g2, hat2, scale2)
        dbranch = dmid.astype(BF)
        acc[R_AO : R_AO + WIDTH] += nt(mixed, dbranch)
        yield
        dmixed = nn(attn_out[...], dbranch).astype(BF)
        yield
        ds_all, dk, dv = [], [], []
        for group in range(2):
            part = slice(64 * group, 64 * group + 64)
            dbd = split_samples(dmixed[part], low_half, high_half)
            values = head_expand(gather_heads(vn, vn_turned, group, low_half, high_half), masks_group)
            dw = nn(values, dbd).reshape(4, 64, 256)
            yield
            ds = softmax_grad(weights[group], dw).reshape(256, 256).astype(BF)
            dv.append(head_select(nt(weights_b[group], dbd), 4, 64).astype(BF))
            dk.append(head_select(nt(ds, query_bd[group]), 4, 64).astype(BF))
            ds_all.append(ds)
        dq = (mix_keys(kt, ds_all, low_half, high_half, first) * 0.25).astype(BF)
        dkv = cat([scatter_heads(dk, low_half, high_half), scatter_heads(dv, low_half, high_half)], 1)
        yield
        acc[R_Q : R_Q + WIDTH] += nt(n1, dq)
        grad = nn(n1, dkv)
        acc[R_KV : R_KV + WIDTH] += grad[:, :WIDTH]
        acc[R_KV + WIDTH : R_KV + 2 * WIDTH] += grad[:, WIDTH:]
        dn1 = nn(qkv_w[:, :WIDTH], dq) + nt(qkv_w[:, WIDTH:], dkv)
        lnacc[0] += fold(dn1 * hat1)
        lnacc[1] += fold(dn1)
        dx = (dmid + norm_rows_grad(dn1 * g1, hat1, scale1)).astype(BF)

        yield
        grad = nn(dx, mixed_ext)
        acc[R_SWO : R_SWO + WIDTH] += grad[:, :WIDTH]
        acc[R_SWO + WIDTH : R_SWO + 2 * WIDTH] += grad[:, WIDTH:]
        dstem = nn(dx.T, stem_t[...]).astype(BF)
        dw, dv, pdw, pdv = [], [], [], []
        for st in range(8):
            j, e, r = st // 2, st % 2, 32 * st
            tall, short, lanes = slice(64 * j, 64 * j + 64), slice(HEAD * j, HEAD * j + HEAD), slice(WIDTH * e, WIDTH * e + WIDTH)
            spread = head_expand(cat([dstem[r : r + 16, :WIDTH], dstem[r + 16 : r + 32, WIDTH:]], 1), masks)
            full = nt(diagonal([vv2[tall, lanes], pv2[short, lanes]]), spread)
            dw.append(full[:64])
            pdw.append(full[64:])
            full = nn(
                diagonal([vpb[tall, lanes], ppb[short, lanes]]), cat([spread[:, :WIDTH], spread[:, WIDTH:]], 0)
            ).astype(BF)
            dv.append(full[:64])
            pdv.append(full[64:])
        yield
        ds = softmax_grad(vp, pair_up(dw).reshape(4, 64, 256)).reshape(256, 256).astype(BF)
        dkv = cat([unpair(nn(ds, qv).astype(BF), 64), cat(dv, 0)], 1)
        dtok = nt(dkv, vis_kv[...]).astype(BF)
        dtok_ref[slots] = dtok
        grad_feats[slots] = nt(dtok, proj[...]).astype(BF)
        gsum[...] += nn(dtok.T, feats[slots])
        grad = nn(tok.T, dkv)
        acc[R_VKV : R_VKV + WIDTH] += grad[:, :WIDTH]
        acc[R_VKV + WIDTH : R_VKV + 2 * WIDTH] += grad[:, WIDTH:]
        full = nn(ds.T, vk2)
        gv_ref[...] += full[:WIDTH, :WIDTH] + full[WIDTH:, WIDTH:]

        yield
        ds = softmax_grad(pp, pair_up(pdw).reshape(4, HEAD, 256)).reshape(64, 256).astype(BF)
        dkv = cat([unpair(nn(ds, qp).astype(BF), HEAD), cat(pdv, 0)], 1)
        dptok = nt(dkv, prop_kv[...]).astype(BF)
        grad = nn(ptok.T, dkv)
        acc[R_PKV : R_PKV + WIDTH] += grad[:, :WIDTH]
        acc[R_PKV + WIDTH : R_PKV + 2 * WIDTH] += grad[:, WIDTH:]
        full = nn(ds.T, pk2)
        gp_ref[...] += full[:WIDTH, :WIDTH] + full[WIDTH:, WIDTH:]
        yield
        acc[R_W2 : R_W2 + WIDTH] += nn(hidden.T, dptok)
        dhidden = nt(dptok, prop_w2[...])
        dpre = (dhidden * (gate * (1.0 + pre * (1.0 - gate)))).astype(BF)
        acc[R_W1 : R_W1 + 32] += nn(fr.T, dpre)
        df_ref[fr_rows] = nt(dpre, prop_w1[...])

        yield

    live = [(g // 2 * 6, chain(g)) for g in range(CHAINS)]
    tick = 0
    while live:
        for one in list(live):
            if tick >= one[0] and next(one[1], live) is live:
                live.remove(one)
        tick += 1

    @pl.when(step == pl.num_programs(0) - 1)
    def _():
        acc[R_QV : R_QV + 16] = head_select(gv_ref[...], HEADS, WIDTH) * 0.25
        acc[R_QP : R_QP + 16] = head_select(gp_ref[...], HEADS, WIDTH) * 0.25
        for j in range(4):
            acc[R_LN + j : R_LN + j + 1] = jnp.sum(lnacc[j].T, axis=0, keepdims=True)
            acc[R_STAT + j : R_STAT + j + 1] = stat[j : j + 1, :WIDTH] + stat[j : j + 1, WIDTH:]
        acc_out[...] = acc[...].astype(BF)
        for j in range(frames.shape[0] // PROP):
            block = df_ref[pl.ds(j, frames.shape[1], stride=frames.shape[0] // PROP)]
            dframes[PROP * j : PROP * j + PROP] = block.T.astype(BF)


def whole(shape):
    return pl.BlockSpec(shape, lambda i, *_: (0,) * len(shape))


def block_call(half, grid_sizes, feats, received, frames, aux, cot, proj, weights):
    steps = aux.shape[0] // CHAINS
    channels = feats.shape[1]
    row = lambda i, *_: (i, 0)
    own = lambda i, half, _: (half[0] * steps + i, 0)
    in_specs = [
        pl.BlockSpec((512 * CHAINS, channels), own),
        pl.BlockSpec((512 * CHAINS, WIDTH), row),
        whole(frames.shape),
        pl.BlockSpec((CHAINS, 8, 256), lambda i, *_: (i, 0, 0)),
        pl.BlockSpec((256 * CHAINS, WIDTH), row),
        whole(proj.shape),
    ] + [whole(w.shape) for w in weights]
    out_shape = (
        jax.ShapeDtypeStruct((256 * CHAINS * steps, WIDTH), BF),
        jax.ShapeDtypeStruct(feats.shape, BF),
        jax.ShapeDtypeStruct((512 * CHAINS * steps, WIDTH), BF),
        jax.ShapeDtypeStruct(frames.shape, BF),
        jax.ShapeDtypeStruct((R_END, WIDTH), BF),
        jax.ShapeDtypeStruct((WIDTH, channels), F32),
    )
    out_specs = (
        pl.BlockSpec((256 * CHAINS, WIDTH), row),
        pl.BlockSpec((512 * CHAINS, channels), own),
        pl.BlockSpec((512 * CHAINS, WIDTH), row),
        whole(frames.shape),
        whole((R_END, WIDTH)),
        whole((WIDTH, channels)),
    )
    scratch = [
        pltpu.VMEM((12, 16, WIDTH), BF),
        pltpu.VMEM((256, 256), BF),
        pltpu.VMEM((256, 256), BF),
        pltpu.VMEM((384, WIDTH), BF),
        pltpu.VMEM((128, WIDTH), BF),
        pltpu.VMEM((512, WIDTH), BF),
        pltpu.VMEM((128, 512), BF),
        pltpu.VMEM((128, 256), BF),
        pltpu.VMEM((4, WIDTH, WIDTH), F32),
        pltpu.VMEM((WIDTH, WIDTH), F32),
        pltpu.VMEM((WIDTH, WIDTH), F32),
        pltpu.VMEM((4, WIDTH, WIDTH), F32),
        pltpu.VMEM((8, 256), F32),
        pltpu.VMEM((R_END, WIDTH), F32),
        pltpu.VMEM((frames.shape[0] // PROP * frames.shape[1], PROP), F32),
        pltpu.VMEM((frames.shape[0] // PROP * frames.shape[1], PROP), F32),
    ]
    return pl.pallas_call(
        block_kernel,
        grid_spec=pltpu.PrefetchScalarGridSpec(
            num_scalar_prefetch=2,
            grid=(steps,),
            in_specs=in_specs,
            out_specs=out_specs,
            scratch_shapes=scratch,
        ),
        out_shape=out_shape,
        compiler_params=pltpu.CompilerParams(vmem_limit_bytes=VMEM_LIMIT),
        name="stems_trunk",
    )(half, grid_sizes, feats, received, frames, aux, cot, proj, *weights)


def make_aux(proprio_mask, token_valid, mix_weight):
    samples, seq = token_valid.shape
    steps = samples // 4
    valid = token_valid.reshape(steps, 1, 4 * seq).astype(F32)
    mix = jnp.broadcast_to(mix_weight.astype(F32)[:, None], (samples, seq)).reshape(steps, 1, 4 * seq)
    vbias = jnp.where(valid > 0, 0.0, NEG)
    pbias = jnp.where(proprio_mask.reshape(steps, 1, -1) > 0, 0.0, NEG)
    pbias = jnp.concatenate([pbias, jnp.zeros_like(pbias)], axis=2)
    rest = jnp.zeros((steps, 4, 4 * seq), F32)
    return jnp.concatenate([valid, mix, vbias, pbias, rest], axis=1)

PROJECT_STEPS = 4
FEATURE_STEPS = 4


def project_kernel(half, feats, proj, out):
    out[...] = nn(feats[...], proj[...]).astype(BF)


def project_call(half, feats, proj):
    rows, channels = feats.shape[0] // 2, feats.shape[1]
    steps = PROJECT_STEPS
    return pl.pallas_call(
        project_kernel,
        grid_spec=pltpu.PrefetchScalarGridSpec(
            num_scalar_prefetch=1,
            grid=(steps,),
            in_specs=[
                pl.BlockSpec((rows // steps, channels), lambda i, half: (half[0] * steps + i, 0)),
                whole(proj.shape),
            ],
            out_specs=pl.BlockSpec((rows // steps, WIDTH), lambda i, half: (i, 0)),
        ),
        out_shape=jax.ShapeDtypeStruct((rows, WIDTH), BF),
        compiler_params=pltpu.CompilerParams(vmem_limit_bytes=VMEM_LIMIT),
        cost_estimate=pl.CostEstimate(
            flops=2 * rows * channels * WIDTH, bytes_accessed=2 * rows * (channels + WIDTH), transcendentals=0
        ),
        name="project",
    )(half, feats, proj)


def unpack_kernel(
    chunk, dother, proj, total, vis_query, vis_wq, prop_query, prop_wq, before,
    o_vision, o_feat, o_vq, o_vwq, o_vkv, o_vwo, o_w1, o_w2, o_pq, o_pwq, o_pkv, o_pwo,
    o_g1, o_b1, o_qkv, o_ao, o_g2, o_b2, o_in, o_out, o_rms, vision, sems,
):
    core = lax.axis_index("mod")
    slots, channels = vision.shape
    piece = slots // FEATURE_STEPS
    copies = []
    for j in range(FEATURE_STEPS):
        part = pl.ds(piece * j, piece)
        vision[part] = nt(dother[part], proj[...]).astype(BF)
        start = pl.multiple_of((1 - core) * slots + piece * j, 16)
        copies.append(pltpu.make_async_copy(vision.at[part], o_vision.at[pl.ds(start, piece)], sems.at[j]))
        copies[j].start()

    n = total.shape[1]
    halves = [total[j, :, :chunk].reshape(n * chunk, WIDTH) for j in range(2)]
    half = R_END // 2

    def rows(start, count):
        source, at = halves[start // half], start % half
        return source[at : at + count].astype(F32)

    gsum = total[core, :, chunk:].reshape(n * (total.shape[2] - chunk), WIDTH).astype(F32)
    for j in range(channels // WIDTH):
        o_feat[WIDTH * j : WIDTH * j + WIDTH] = gsum[WIDTH * j : WIDTH * j + WIDTH].T
    for o_query, o_w, query, w, start in (
        (o_vq, o_vwq, vis_query, vis_wq, R_QV),
        (o_pq, o_pwq, prop_query, prop_wq, R_QP),
    ):
        grad = rows(start, 16).astype(BF)
        o_query[...] = nt(grad, w[...])
        o_w[...] = lax.dot_general(
            query[...], grad, (((0,), (0,)), ((), ())), preferred_element_type=F32
        )
    for o, start in ((o_vkv, R_VKV), (o_pkv, R_PKV)):
        o[:, :WIDTH] = rows(start, WIDTH)
        o[:, WIDTH:] = rows(start + WIDTH, WIDTH)
    o_vwo[...] = rows(R_SWO, WIDTH).T
    o_pwo[...] = rows(R_SWO + WIDTH, WIDTH).T
    o_w1[...] = rows(R_W1, 32)
    o_w2[...] = rows(R_W2, WIDTH)
    for j in range(3):
        o_qkv[:, WIDTH * j : WIDTH * j + WIDTH] = rows(R_Q + WIDTH * j, WIDTH)
    o_ao[...] = rows(R_AO, WIDTH)
    o_in[...] = rows(R_WIN, 512).T
    o_out[...] = rows(R_WOUT, 512)
    small = rows(R_LN, 16)
    for j, o in enumerate((o_g1, o_b1, o_g2, o_b2)):
        o[...] = small[j : j + 1]
    sums = [jnp.sum(small[R_STAT - R_LN + j : R_STAT - R_LN + j + 1], axis=1, keepdims=True) for j in range(4)]
    for j in range(3):
        o_rms[j] = jnp.sum(jnp.sqrt(sums[j] / (sums[3] * WIDTH)))
    for copy in copies:
        copy.wait()


def unpack_call(chunk, dother, proj, total, vis_query, vis_wq, prop_query, prop_wq, grad_vision):
    slots, channels = dother.shape[0], proj.shape[0]
    shapes = [
        (channels, WIDTH), (16, WIDTH), (WIDTH, WIDTH), (WIDTH, 256), (WIDTH, WIDTH), (32, WIDTH),
        (WIDTH, WIDTH), (16, WIDTH), (WIDTH, WIDTH), (WIDTH, 256), (WIDTH, WIDTH), (1, WIDTH), (1, WIDTH),
        (WIDTH, 384), (WIDTH, WIDTH), (1, WIDTH), (1, WIDTH), (WIDTH, 512), (512, WIDTH), (3,),
    ]
    vmem, hbm = pl.BlockSpec(memory_space=pltpu.VMEM), pl.BlockSpec(memory_space=pltpu.HBM)
    return pl.pallas_call(
        functools.partial(unpack_kernel, chunk),
        in_specs=[vmem] * 7 + [hbm],
        out_specs=[hbm] + [vmem] * (len(shapes) - 1) + [pl.BlockSpec(memory_space=pltpu.SMEM)],
        out_shape=[jax.ShapeDtypeStruct(grad_vision.shape, BF)] + [jax.ShapeDtypeStruct(s, F32) for s in shapes],
        scratch_shapes=[pltpu.VMEM((slots, channels), BF), pltpu.SemaphoreType.DMA((FEATURE_STEPS,))],
        input_output_aliases={7: 0},
        compiler_params=pltpu.CompilerParams(vmem_limit_bytes=20 * 2**20),
        name="unpack",
    )(dother, in_hbm(proj), total, *map(in_hbm, (vis_query, vis_wq, prop_query, prop_wq)), grad_vision)


def finish_kernel(
    n, chunk, gchunk, acc, gsum, dtok, feats, total, dother,
    fbuf, gbuf, own_a, recv_a, send_b, recv_b, send_g, recv_g, reduced,
    sem_t, sem_f, sem_a, sem_b, sem_c, sem_d, sem_g,
):
    me, core = lax.axis_index("dp"), lax.axis_index("mod")
    mesh = pl.DeviceIdType.MESH
    partner = (me, 1 - core)
    half = R_END // 2
    slots, channels = fbuf.shape
    piece = slots // FEATURE_STEPS

    def remote(src, dst, send_sem, recv_sem, device):
        return pltpu.make_async_remote_copy(
            src_ref=src, dst_ref=dst, send_sem=send_sem, recv_sem=recv_sem, device_id=device, device_id_type=mesh
        )

    def rows(index, count):
        return pl.ds(pl.multiple_of(index * count, 16), count)

    barrier = pltpu.get_barrier_semaphore()
    pl.semaphore_signal(barrier, inc=1, device_id=partner, device_id_type=mesh)

    def greet(k, carry):
        pl.semaphore_signal(barrier, inc=1, device_id=(lax.rem(me + k, n), core), device_id_type=mesh)
        return carry

    lax.fori_loop(1, n, greet, 0)
    load_a = pltpu.make_async_copy(acc.at[rows(core, half)], own_a, sem_a.at[2])
    load_a.start()
    load_g = pltpu.make_async_copy(gsum, gbuf, sem_a.at[3])
    load_g.start()
    tokens, features = [], []
    for j in range(FEATURE_STEPS):
        part = pl.ds(piece * j, piece)
        start_row = pl.multiple_of((1 - core) * slots + piece * j, 16)
        features.append(pltpu.make_async_copy(feats.at[pl.ds(start_row, piece)], fbuf.at[part], sem_f.at[j]))
        features[j].start()
    pl.semaphore_wait(barrier, n)

    copy_a = remote(acc.at[rows(1 - core, half)], recv_a, sem_a.at[0], sem_a.at[1], partner)
    copy_a.start()
    for j in range(FEATURE_STEPS):
        part = pl.ds(piece * j, piece)
        tokens.append(remote(dtok.at[part], dother.at[part], sem_t.at[0, j], sem_t.at[1, j], partner))
        tokens[j].start()
    if half < n * chunk:
        send_b[half:] = jnp.zeros((n * chunk - half, WIDTH), BF)
    load_a.wait()
    copy_a.wait()
    send_b[:half] = (own_a[...].astype(F32) + recv_a[...].astype(F32)).astype(BF)

    def scatter(k):
        peer = lax.rem(me + k, n)
        return remote(
            send_b.at[rows(peer, chunk)], recv_b.at[k - 1], sem_b.at[0, k - 1], sem_b.at[1, k - 1], (peer, core)
        )

    def scatter_g(k):
        peer = lax.rem(me + k, n)
        return remote(
            send_g.at[rows(peer, gchunk)], recv_g.at[k - 1], sem_g.at[0, k - 1], sem_g.at[1, k - 1], (peer, core)
        )

    def gather(k):
        peer = lax.rem(me + k, n)
        return remote(reduced, total.at[core, me], sem_c.at[0, k - 1], sem_c.at[1, k - 1], (peer, core))

    def forward(k):
        piece_k = total.at[core, lax.rem(me + n - k, n), pl.ds(0, chunk)]
        return remote(piece_k, piece_k, sem_d.at[0, k], sem_d.at[1, k], partner)

    def each(first, step):
        def body(k, carry):
            step(k)
            return carry

        lax.fori_loop(first, n, body, 0)

    each(1, lambda k: scatter(k).start())

    load_g.wait()
    grad = gbuf[...]
    for j in range(FEATURE_STEPS):
        tokens[j].wait()
        features[j].wait()
        part = slice(piece * j, piece * j + piece)
        grad = grad + nn(dother[part].T, fbuf[part])
    used = WIDTH * (channels // WIDTH)
    for j in range(channels // WIDTH):
        send_g[WIDTH * j : WIDTH * j + WIDTH] = grad[:, WIDTH * j : WIDTH * j + WIDTH].astype(BF)
    if used < n * gchunk:
        send_g[used:] = jnp.zeros((n * gchunk - used, WIDTH), BF)
    each(1, lambda k: scatter_g(k).start())

    def add(k, value):
        scatter(k).wait()
        return value + recv_b[k - 1].astype(F32)

    def add_g(k, value):
        scatter_g(k).wait()
        return value + recv_g[k - 1].astype(F32)

    reduced[:chunk] = lax.fori_loop(1, n, add, send_b[rows(me, chunk)].astype(F32)).astype(BF)
    reduced[chunk:] = lax.fori_loop(1, n, add_g, send_g[rows(me, gchunk)].astype(F32)).astype(BF)
    each(1, lambda k: gather(k).start())
    total[core, me] = reduced[...]
    forward(0).start()

    def pass_on(k):
        gather(k).wait()
        forward(k).start()

    each(1, pass_on)
    each(0, lambda k: forward(k).wait())


def in_hbm(value):
    return pltpu.with_memory_space_constraint(value, pltpu.HBM)


def finish_call(acc, gsum, dtok, feats, n):
    slots, channels = dtok.shape[0], feats.shape[1]
    half = R_END // 2
    chunk = 16 * -(-half // (16 * n))
    gchunk = 16 * -(-channels // (16 * n))
    vmem = pl.BlockSpec(memory_space=pltpu.VMEM)
    hbm = pl.BlockSpec(memory_space=pltpu.HBM)
    dma = pltpu.SemaphoreType.DMA
    total, dother = pl.pallas_call(
        functools.partial(finish_kernel, n, chunk, gchunk),
        out_shape=(
            jax.ShapeDtypeStruct((2, n, chunk + gchunk, WIDTH), BF),
            jax.ShapeDtypeStruct(dtok.shape, BF),
        ),
        in_specs=[hbm, hbm, hbm, hbm],
        out_specs=(vmem, vmem),
        scratch_shapes=[
            pltpu.VMEM((slots, channels), BF),
            pltpu.VMEM(gsum.shape, F32),
            pltpu.VMEM((half, WIDTH), BF),
            pltpu.VMEM((half, WIDTH), BF),
            pltpu.VMEM((n * chunk, WIDTH), BF),
            pltpu.VMEM((n - 1, chunk, WIDTH), BF),
            pltpu.VMEM((n * gchunk, WIDTH), BF),
            pltpu.VMEM((n - 1, gchunk, WIDTH), BF),
            pltpu.VMEM((chunk + gchunk, WIDTH), BF),
            dma((2, FEATURE_STEPS)),
            dma((FEATURE_STEPS,)),
            dma((4,)),
            dma((2, n - 1)),
            dma((2, n - 1)),
            dma((2, n)),
            dma((2, n - 1)),
        ],
        compiler_params=pltpu.CompilerParams(
            collective_id=0, has_side_effects=True, vmem_limit_bytes=24 * 2**20
        ),
        name="finish",
    )(in_hbm(acc), in_hbm(gsum), in_hbm(dtok), in_hbm(feats))
    return chunk, total, dother


def per_device(
    vision_feats, vision_grid, proprio, proprio_mask, token_valid, mix_weight, out_cot, feat_proj,
    vis_query, vis_wq, vis_kv, vis_wo, prop_w1, prop_w2, prop_query, prop_wq, prop_kv, prop_wo,
    ln1_gain, ln1_bias, qkv_weight, attn_out, ln2_gain, ln2_bias, mlp_in, mlp_out,
):
    me = lax.axis_index("mod").astype(jnp.int32)
    own, other = me.reshape(1), (1 - me).reshape(1)
    swap = [(0, 1), (1, 0)]
    feats = vision_feats.reshape(-1, vision_feats.shape[3])
    sent = project_call(other, feats, feat_proj)
    received = lax.ppermute(sent, "mod", swap)
    aux = make_aux(proprio_mask, token_valid, mix_weight)
    ln = jnp.stack([ln1_gain, ln1_bias, ln2_gain, ln2_bias]).astype(F32)
    weights = (
        vis_query, vis_wq, vis_kv, vis_wo, prop_w1, prop_w2, prop_query, prop_wq, prop_kv, prop_wo,
        ln, qkv_weight, attn_out, mlp_in, mlp_out,
    )
    frames = jnp.transpose(proprio, (1, 2, 3, 0)).reshape(-1, proprio.shape[0])
    grid_sizes = jnp.transpose(vision_grid, (1, 2, 0)).reshape(4, -1)
    output, grad_vision, dtok, dframes, acc, gfeat = block_call(
        own, grid_sizes, feats, received, frames, aux, out_cot.reshape(-1, WIDTH), feat_proj, weights
    )
    chunk, total, dother = finish_call(acc, gfeat, dtok, feats, lax.axis_size("dp"))
    grad_vision, *outs = unpack_call(
        chunk, dother, feat_proj, total, vis_query, vis_wq, prop_query, prop_wq, grad_vision
    )
    vectors = {11, 12, 15, 16}
    outs = [o.reshape(WIDTH) if j in vectors else o for j, o in enumerate(outs)]
    return (
        output.reshape(out_cot.shape),
        grad_vision.reshape(vision_feats.shape),
        jnp.transpose(dframes.reshape(proprio.shape[1:] + proprio.shape[:1]), (3, 0, 1, 2)),
        *outs,
    )


def solution(mesh):
    both = ("dp", "mod")
    return jax.shard_map(
        per_device,
        mesh=mesh,
        in_specs=(
            P("dp", None, None, "mod"),
            P(both, None, None),
            P(both, None, None, None),
            P(both, None, None),
            P(both, None),
            P(both),
            P(both, None, None),
            P("mod", None),
        ) + (P(),) * 18,
        out_specs=(
            P(both, None, None),
            P("dp", None, None, "mod"),
            P(both, None, None, None),
            P("mod", None),
        ) + (P(),) * 19,
        check_vma=False,
    )
```

```python
import functools
import math

import jax
import jax.numpy as jnp
from jax import lax
from jax.experimental import pallas as pl
from jax.experimental.pallas import tpu as pltpu
from jax.sharding import PartitionSpec as P

HEADS = 8
HEAD = 16
WIDTH = 128
PROP = 32
NEG = -1e30
BF = jnp.bfloat16
F32 = jnp.float32
VMEM_LIMIT = 60 * 2**20
CHAINS = 8
FF_PART = 256

R_WIN, R_WOUT, R_Q, R_KV, R_AO = 0, 512, 1024, 1152, 1408
R_SWO, R_VKV, R_PKV, R_W2, R_W1 = 1536, 1792, 2048, 2304, 2432
R_QV, R_QP, R_LN, R_STAT, R_END = 2464, 2480, 2496, 2500, 2560


def nn(a, b):
    return lax.dot_general(a, b, (((1,), (0,)), ((), ())), preferred_element_type=F32)


def nt(a, b):
    return lax.dot_general(a, b, (((1,), (1,)), ((), ())), preferred_element_type=F32)


def cat(items, axis):
    return jnp.concatenate(items, axis=axis)


def lane_iota(rows, lanes):
    return lax.broadcasted_iota(jnp.int32, (rows, lanes), 1)


def tile_to(mask, rows, lanes):
    return cat([cat([mask] * (rows // mask.shape[0]), 0)] * (lanes // mask.shape[1]), 1)


def head_expand(value, masks):
    return cat([value * tile_to(mask, *value.shape) for mask in masks], 0)


def head_select(full, heads, period):
    rows, lanes = full.shape[0] // heads, full.shape[1]
    head = (lane_iota(rows, lanes) & (period - 1)) >> 4
    out = full[:rows]
    for h in range(1, heads):
        out = jnp.where(head == h, full[h * rows : (h + 1) * rows], out)
    return out


def turn(value):
    out = []
    for j in range(0, value.shape[1], WIDTH):
        out += [value[:, j + 64 : j + 128], value[:, j : j + 64]]
    return cat(out, 1)


def diagonal(blocks):
    out = []
    for j, block in enumerate(blocks):
        row = [block if k == j else jnp.zeros((block.shape[0], other.shape[1]), BF) for k, other in enumerate(blocks)]
        out.append(cat(row, 1))
    return cat(out, 0)


def pair_up(parts):
    return cat([cat(parts[j : j + 2], 1) for j in range(0, 8, 2)], 0)


def unpair(value, rows):
    out = []
    for j in range(4):
        part = value[rows * j : rows * j + rows]
        out += [part[:, :WIDTH], part[:, WIDTH:]]
    return cat(out, 0)


def softmax_rows(scores):
    peak = jnp.max(scores, axis=1, keepdims=True)
    weights = jnp.exp(scores - peak)
    return weights * (1.0 / jnp.sum(weights, axis=1, keepdims=True))


def softmax_grad(weights, grad):
    return weights * (grad - jnp.sum(weights * grad, axis=1, keepdims=True))


def mean_rows(value):
    return jnp.sum(value, axis=0, keepdims=True) * (1.0 / value.shape[0])


def norm_rows(value):
    centered = value - mean_rows(value)
    scale = lax.rsqrt(mean_rows(centered * centered) + 1e-05)
    return centered * scale, scale


def norm_rows_grad(grad, hat, scale):
    return scale * (grad - mean_rows(grad) - hat * mean_rows(grad * hat))


def split_samples(value, low_half, high_half):
    out = []
    for s in range(4):
        half = tile_to(high_half if s % 2 else low_half, 64, WIDTH)
        block = value[:, WIDTH * (s // 2) : WIDTH * (s // 2) + WIDTH] * half
        zero = jnp.zeros((64, WIDTH), BF)
        out.append(cat([block, zero] if s < 2 else [zero, block], 1))
    return cat(out, 0)


def gather_heads(value, turned, group, low_half, high_half):
    low_tall, high_tall = tile_to(low_half, 64, WIDTH), tile_to(high_half, 64, WIDTH)
    out = []
    for s in (0, 2):
        even, odd = slice(64 * s, 64 * s + 64), slice(64 * s + 64, 64 * s + 128)
        left, right = (value[even], turned[odd]) if group == 0 else (turned[even], value[odd])
        out.append(left * low_tall + right * high_tall)
    return cat(out, 1)


def scatter_heads(parts, low_half, high_half):
    low_tall, high_tall = tile_to(low_half, 64, WIDTH), tile_to(high_half, 64, WIDTH)
    turned = [turn(part) for part in parts]
    out = []
    for s in range(4):
        lanes = slice(WIDTH * (s // 2), WIDTH * (s // 2) + WIDTH)
        left = (turned if s % 2 else parts)[0][:, lanes]
        right = (parts if s % 2 else turned)[1][:, lanes]
        out.append(left * low_tall + right * high_tall)
    return cat(out, 0)


def spread_keys(value, turned, group, low_half, high_half):
    zero = jnp.zeros((HEAD, WIDTH), BF)
    rows = []
    for s in range(4):
        lanes = slice(WIDTH * (s // 2), WIDTH * (s // 2) + WIDTH)
        for local in range(4):
            h = group * 4 + local
            source = value if s % 2 == local % 2 else turned
            block = source[h * HEAD : (h + 1) * HEAD, lanes] * (high_half if local % 2 else low_half)
            rows.append(cat([block, zero] if local < 2 else [zero, block], 1))
    return cat(rows, 0)


def mix_keys(value, weights, low_half, high_half, first):
    turned = turn(value)
    out = []
    for group in range(2):
        full = nn(spread_keys(value, turned, group, low_half, high_half), weights[group])
        left = jnp.where(first, full[:64, :WIDTH], full[64:128, :WIDTH])
        right = jnp.where(first, full[128:192, WIDTH:], full[192:, WIDTH:])
        out.append(cat([left, right], 1))
    return cat(out, 0)


def stem_queries(query, w_query, masks):
    value = nn(query, w_query).astype(BF)
    return head_expand(value * jnp.asarray(0.25, BF), masks)


def block_kernel(
    half, grid_ref, feats, pr, frames, frame_mask, token_valid, mix_weight, cot, proj,
    vis_query, vis_wq, vis_kv, vis_wo, prop_w1, prop_w2, prop_query, prop_wq, prop_kv, prop_wo,
    ln1_gain, ln1_bias, ln2_gain, ln2_bias, qkv_w, attn_out, mlp_in, mlp_out,
    out, grad_feats, dtok_ref, dframes, acc_out, gsum,
    masks_ref, qv_ref, qp_ref, wqkv_t, ao_t, win_t, wout_t, stem_t, ln_ref,
    gv_ref, gp_ref, lnacc, stat, acc, fr_ref, df_ref, aux_ref, turn_ref,
):
    blocks = token_valid.shape[0] // 4
    step = pl.program_id(0)

    @pl.when(step == 0)
    def _():
        lane = lane_iota(16, WIDTH) >> 4
        for h in range(HEADS):
            masks_ref[h] = jnp.where(lane == h, 1.0, 0.0).astype(BF)
        for h in range(4):
            masks_ref[HEADS + h] = jnp.where((lane & 3) == h, 1.0, 0.0).astype(BF)
        masks = [masks_ref[h] for h in range(HEADS)]
        qv_ref[...] = diagonal([stem_queries(vis_query[...], vis_wq[...], masks)] * 2)
        qp_ref[...] = diagonal([stem_queries(prop_query[...], prop_wq[...], masks)] * 2)
        wqkv_t[...] = qkv_w[...].T
        ao_t[...] = attn_out[...].T
        win_t[...] = mlp_in[...].T
        wout_t[...] = mlp_out[...].T
        stem_t[:, :WIDTH] = vis_wo[...].T
        stem_t[:, WIDTH:] = prop_wo[...].T
        for j, vector in enumerate((ln1_gain, ln1_bias, ln2_gain, ln2_bias)):
            ln_ref[j] = jnp.broadcast_to(vector[...].astype(F32), (WIDTH, WIDTH)).T

        def by_block(ref):
            return cat([ref[pl.ds(j, blocks, stride=4)].astype(F32) for j in range(4)], 1)

        valid = by_block(token_valid)
        turn_ref[...] = jnp.broadcast_to(mix_weight[...].astype(F32), turn_ref.shape).T
        mix = by_block(turn_ref)
        turn_ref[:, : frame_mask.shape[0]] = frame_mask[...].astype(F32).T
        frame_keep = cat([turn_ref[pl.ds(j, blocks, stride=4)][:, : frame_mask.shape[0]] for j in range(4)], 1)
        values = (valid, mix, jnp.where(valid > 0, 0.0, NEG), jnp.where(cat([frame_keep] * 2, 1) > 0, 0.0, NEG))
        for i in range(blocks):
            for j, value in enumerate(values):
                aux_ref[i, j : j + 1] = value[i : i + 1]

        for j in range(frames.shape[0] // PROP):
            block = frames[PROP * j : PROP * j + PROP].astype(F32).T
            fr_ref[pl.ds(j, block.shape[0], stride=frames.shape[0] // PROP)] = block
        acc[...] = jnp.zeros_like(acc)
        gsum[...] = jnp.zeros_like(gsum)
        gv_ref[...] = jnp.zeros_like(gv_ref)
        gp_ref[...] = jnp.zeros_like(gp_ref)
        lnacc[...] = jnp.zeros_like(lnacc)
        stat[...] = jnp.zeros_like(stat)

    masks = [masks_ref[h] for h in range(HEADS)]
    masks_group = [masks_ref[HEADS + h] for h in range(4)]
    qv, qp = qv_ref[...], qp_ref[...]
    lane = lane_iota(HEAD, WIDTH)
    low_half = jnp.where(lane < 64, 1.0, 0.0).astype(BF)
    high_half = jnp.where(lane < 64, 0.0, 1.0).astype(BF)
    first = lane_iota(64, WIDTH) < 64


    def chain(g):
        block = step * CHAINS + g
        slots = slice(512 * g, 512 * g + 512)
        kept = nn(feats[slots], proj[...]).astype(BF)
        tok = (kept.astype(F32) + pr[slots].astype(F32)).astype(BF)
        vkv = nn(tok, vis_kv[...]).astype(BF)
        vk, vv = vkv[:, :WIDTH], vkv[:, WIDTH:]
        slot = lax.broadcasted_iota(jnp.int32, (64, WIDTH), 0)
        slot_row, slot_col = slot >> 3, slot & 7
        bias = []
        for st in range(8):
            s, t = (step * CHAINS + g) * 4 + st // 2, st % 2
            keep = (slot_row < grid_ref[2 * t, s]) & (slot_col < grid_ref[2 * t + 1, s])
            bias.append(jnp.where(keep, 0.0, NEG))
        bias = pair_up(bias).reshape(4, 64, 256)
        vk2 = pair_up([vk[64 * st : 64 * st + 64] for st in range(8)])
        vv2 = pair_up([vv[64 * st : 64 * st + 64] for st in range(8)])
        yield
        vp = softmax_rows(nt(vk2, qv).reshape(4, 64, 256) + bias)
        vpb = vp.reshape(256, 256).astype(BF)
        yield
        vpt = vpb.T
        vmixed = [None] * 8
        for e in range(2):
            for m in range(2):
                one, two = 4 * m + e, 4 * m + 2 + e
                spread = diagonal([vv[64 * one : 64 * one + 64], vv[64 * two : 64 * two + 64]])
                lhs = vpt[WIDTH * e : WIDTH * e + WIDTH, WIDTH * m : WIDTH * m + WIDTH]
                both = head_select(nn(lhs, spread), HEADS, WIDTH).astype(BF)
                vmixed[one], vmixed[two] = both[:, :WIDTH], both[:, WIDTH:]

        yield
        fr_rows = pl.ds(pl.multiple_of((step * CHAINS + g) * 128, 128), 128)
        fr = fr_ref[fr_rows].astype(BF)
        pre = nn(fr, prop_w1[...])
        gate = jax.nn.sigmoid(pre)
        hidden = (pre * gate).astype(BF)
        ptok = nn(hidden, prop_w2[...]).astype(BF)
        pkv = nn(ptok, prop_kv[...]).astype(BF)
        pk, pv = pkv[:, :WIDTH], pkv[:, WIDTH:]
        column = jnp.broadcast_to(aux_ref[block, 3:4, :WIDTH], (WIDTH, WIDTH)).T
        parts = lambda v: [v[HEAD * st : HEAD * st + HEAD] for st in range(8)]
        pbias = pair_up(parts(column))
        pk2, pv2 = pair_up(parts(pk)), pair_up(parts(pv))
        yield
        pp = softmax_rows((nt(pk2, qp) + pbias).reshape(4, HEAD, 256))
        ppb = pp.reshape(64, 256).astype(BF)
        ppt = ppb.T
        pmixed = [None] * 8
        for e in range(2):
            spread = diagonal([pv[HEAD * st : HEAD * st + HEAD] for st in range(e, 8, 2)])
            both = head_select(nn(ppt[WIDTH * e : WIDTH * e + WIDTH], spread), HEADS, WIDTH).astype(BF)
            for j in range(4):
                pmixed[2 * j + e] = both[:, WIDTH * j : WIDTH * j + WIDTH]

        yield
        zero16 = jnp.zeros((HEAD, WIDTH), BF)
        rows = []
        for st in range(8):
            rows.append(cat([vmixed[st], zero16], 1))
            rows.append(cat([zero16, pmixed[st]], 1))
        mixed_ext = cat(rows, 0)
        x = nt(stem_t[...], mixed_ext)
        g1, b1, g2, b2 = [cat([ln_ref[j]] * 2, 1) for j in range(4)]
        hat1, scale1 = norm_rows(x)
        n1 = (hat1 * g1 + b1).astype(BF)
        yield
        qkv = nn(wqkv_t[...], n1).astype(BF)
        qt, kt, vt = qkv[:WIDTH] * jnp.asarray(0.25, BF), qkv[WIDTH : 2 * WIDTH], qkv[2 * WIDTH :]
        kn, vn = kt.T, vt.T
        kn_turned, vn_turned = turn(kn), turn(vn)
        yield
        weights, weights_b, query_bd = [], [], []
        tbias = []
        for p in range(2):
            column = jnp.broadcast_to(aux_ref[block, 2:3, 128 * p : 128 * p + 128], (WIDTH, WIDTH)).T
            tbias.append(jnp.where(first, column[:64], column[64:]))
        tbias = cat(tbias, 1)[None]
        for group in range(2):
            part = slice(64 * group, 64 * group + 64)
            qbd = split_samples(qt[part], low_half, high_half)
            keys = head_expand(gather_heads(kn, kn_turned, group, low_half, high_half), masks_group)
            scores = nn(keys, qbd).reshape(4, 64, 256) + tbias
            yield
            w = softmax_rows(scores)
            weights.append(w)
            weights_b.append(w.reshape(256, 256).astype(BF))
            query_bd.append(qbd)
            yield
        mixed = mix_keys(vt, weights_b, low_half, high_half, first).astype(BF)
        yield
        branch = nn(ao_t[...], mixed)
        middle = x + branch
        hat2, scale2 = norm_rows(middle)
        n2 = (hat2 * g2 + b2).astype(BF)
        yield
        c = math.sqrt(2.0 / math.pi)
        seed = cot[256 * g : 256 * g + 256].T.astype(F32) * aux_ref[block, 1:2, :]
        dmlp = seed.astype(BF)
        mlp, dn2, act_all, dup_all = 0.0, 0.0, [], []
        for j in range(512 // FF_PART):
            part = slice(FF_PART * j, FF_PART * j + FF_PART)
            up = nn(win_t[part], n2)
            yield
            square = up * up
            h = 0.5 + 0.5 * jnp.tanh(up * (c + (c * 0.044715) * square))
            act = up * h
            slope = h + act * (1.0 - h) * (2 * c + (6 * c * 0.044715) * square)
            act_b = act.astype(BF)
            mlp = mlp + nn(wout_t[:, part], act_b)
            dup = (nn(mlp_out[part], dmlp) * slope).astype(BF)
            yield
            dn2 = dn2 + nn(mlp_in[:, part], dup)
            acc[R_WOUT + FF_PART * j : R_WOUT + FF_PART * j + FF_PART] += nt(act_b, dmlp)
            acc[R_WIN + FF_PART * j : R_WIN + FF_PART * j + FF_PART] += nt(dup, n2)
            yield
        final = middle + mlp
        out[256 * g : 256 * g + 256] = final.astype(BF).T
        valid = aux_ref[block, 0:1, :]
        for j, value in enumerate((final, branch, mlp)):
            stat[j : j + 1, :] += jnp.sum(value * value, axis=0, keepdims=True) * valid
        stat[3:4, :] += valid

        yield
        fold = lambda v: v[:, :WIDTH] + v[:, WIDTH:]
        lnacc[2] += fold(dn2 * hat2)
        lnacc[3] += fold(dn2)
        dmid = seed + norm_rows_grad(dn2 * g2, hat2, scale2)
        dbranch = dmid.astype(BF)
        acc[R_AO : R_AO + WIDTH] += nt(mixed, dbranch)
        yield
        dmixed = nn(attn_out[...], dbranch).astype(BF)
        yield
        ds_all, dk, dv = [], [], []
        for group in range(2):
            part = slice(64 * group, 64 * group + 64)
            dbd = split_samples(dmixed[part], low_half, high_half)
            values = head_expand(gather_heads(vn, vn_turned, group, low_half, high_half), masks_group)
            dw = nn(values, dbd).reshape(4, 64, 256)
            yield
            ds = softmax_grad(weights[group], dw).reshape(256, 256).astype(BF)
            dv.append(head_select(nt(weights_b[group], dbd), 4, 64).astype(BF))
            dk.append(head_select(nt(ds, query_bd[group]), 4, 64).astype(BF))
            ds_all.append(ds)
        dq = (mix_keys(kt, ds_all, low_half, high_half, first) * 0.25).astype(BF)
        dkv = cat([scatter_heads(dk, low_half, high_half), scatter_heads(dv, low_half, high_half)], 1)
        yield
        acc[R_Q : R_Q + WIDTH] += nt(n1, dq)
        grad = nn(n1, dkv)
        acc[R_KV : R_KV + WIDTH] += grad[:, :WIDTH]
        acc[R_KV + WIDTH : R_KV + 2 * WIDTH] += grad[:, WIDTH:]
        dn1 = nn(qkv_w[:, :WIDTH], dq) + nt(qkv_w[:, WIDTH:], dkv)
        lnacc[0] += fold(dn1 * hat1)
        lnacc[1] += fold(dn1)
        dx = (dmid + norm_rows_grad(dn1 * g1, hat1, scale1)).astype(BF)

        yield
        grad = nn(dx, mixed_ext)
        acc[R_SWO : R_SWO + WIDTH] += grad[:, :WIDTH]
        acc[R_SWO + WIDTH : R_SWO + 2 * WIDTH] += grad[:, WIDTH:]
        dstem = nn(dx.T, stem_t[...]).astype(BF)
        dw, dv, pdw, pdv = [], [], [], []
        for st in range(8):
            j, e, r = st // 2, st % 2, 32 * st
            tall, short, lanes = slice(64 * j, 64 * j + 64), slice(HEAD * j, HEAD * j + HEAD), slice(WIDTH * e, WIDTH * e + WIDTH)
            spread = head_expand(cat([dstem[r : r + 16, :WIDTH], dstem[r + 16 : r + 32, WIDTH:]], 1), masks)
            full = nt(diagonal([vv2[tall, lanes], pv2[short, lanes]]), spread)
            dw.append(full[:64])
            pdw.append(full[64:])
            full = nn(
                diagonal([vpb[tall, lanes], ppb[short, lanes]]), cat([spread[:, :WIDTH], spread[:, WIDTH:]], 0)
            ).astype(BF)
            dv.append(full[:64])
            pdv.append(full[64:])
        yield
        ds = softmax_grad(vp, pair_up(dw).reshape(4, 64, 256)).reshape(256, 256).astype(BF)
        dkv = cat([unpair(nn(ds, qv).astype(BF), 64), cat(dv, 0)], 1)
        dtok = nt(dkv, vis_kv[...]).astype(BF)
        dtok_ref[slots] = dtok
        grad_feats[slots] = nt(dtok, proj[...]).astype(BF)
        gsum[...] += nn(dtok.T, feats[slots])
        grad = nn(tok.T, dkv)
        acc[R_VKV : R_VKV + WIDTH] += grad[:, :WIDTH]
        acc[R_VKV + WIDTH : R_VKV + 2 * WIDTH] += grad[:, WIDTH:]
        full = nn(ds.T, vk2)
        gv_ref[...] += full[:WIDTH, :WIDTH] + full[WIDTH:, WIDTH:]

        yield
        ds = softmax_grad(pp, pair_up(pdw).reshape(4, HEAD, 256)).reshape(64, 256).astype(BF)
        dkv = cat([unpair(nn(ds, qp).astype(BF), HEAD), cat(pdv, 0)], 1)
        dptok = nt(dkv, prop_kv[...]).astype(BF)
        grad = nn(ptok.T, dkv)
        acc[R_PKV : R_PKV + WIDTH] += grad[:, :WIDTH]
        acc[R_PKV + WIDTH : R_PKV + 2 * WIDTH] += grad[:, WIDTH:]
        full = nn(ds.T, pk2)
        gp_ref[...] += full[:WIDTH, :WIDTH] + full[WIDTH:, WIDTH:]
        yield
        acc[R_W2 : R_W2 + WIDTH] += nn(hidden.T, dptok)
        dhidden = nt(dptok, prop_w2[...])
        dpre = (dhidden * (gate * (1.0 + pre * (1.0 - gate)))).astype(BF)
        acc[R_W1 : R_W1 + 32] += nn(fr.T, dpre)
        df_ref[fr_rows] = nt(dpre, prop_w1[...])

        yield

    live = [(g // 2 * 6, chain(g)) for g in range(CHAINS)]
    tick = 0
    while live:
        for one in list(live):
            if tick >= one[0] and next(one[1], live) is live:
                live.remove(one)
        tick += 1

    @pl.when(step == pl.num_programs(0) - 1)
    def _():
        acc[R_QV : R_QV + 16] = head_select(gv_ref[...], HEADS, WIDTH) * 0.25
        acc[R_QP : R_QP + 16] = head_select(gp_ref[...], HEADS, WIDTH) * 0.25
        for j in range(4):
            acc[R_LN + j : R_LN + j + 1] = jnp.sum(lnacc[j].T, axis=0, keepdims=True)
            acc[R_STAT + j : R_STAT + j + 1] = stat[j : j + 1, :WIDTH] + stat[j : j + 1, WIDTH:]
        acc_out[...] = acc[...].astype(BF)
        for j in range(frames.shape[0] // PROP):
            block = df_ref[pl.ds(j, frames.shape[1], stride=frames.shape[0] // PROP)]
            dframes[PROP * j : PROP * j + PROP] = block.T.astype(BF)


def whole(shape):
    return pl.BlockSpec(shape, lambda i, *_: (0,) * len(shape))


def block_call(half, grid_sizes, feats, received, frames, frame_mask, token_valid, mix_weight, cot, proj, weights):
    samples, seq = token_valid.shape
    steps = samples // (4 * CHAINS)
    channels = feats.shape[1]
    row = lambda i, *_: (i, 0)
    own = lambda i, half, _: (half[0] * steps + i, 0)
    in_specs = [
        pl.BlockSpec((512 * CHAINS, channels), own),
        pl.BlockSpec((512 * CHAINS, WIDTH), row),
        whole(frames.shape),
        whole(frame_mask.shape),
        whole(token_valid.shape),
        whole(mix_weight.shape),
        pl.BlockSpec((256 * CHAINS, WIDTH), row),
        whole(proj.shape),
    ] + [whole(w.shape) for w in weights]
    out_shape = (
        jax.ShapeDtypeStruct((256 * CHAINS * steps, WIDTH), BF),
        jax.ShapeDtypeStruct(feats.shape, BF),
        jax.ShapeDtypeStruct((512 * CHAINS * steps, WIDTH), BF),
        jax.ShapeDtypeStruct(frames.shape, BF),
        jax.ShapeDtypeStruct((R_END, WIDTH), BF),
        jax.ShapeDtypeStruct((WIDTH, channels), F32),
    )
    out_specs = (
        pl.BlockSpec((256 * CHAINS, WIDTH), row),
        pl.BlockSpec((512 * CHAINS, channels), own),
        pl.BlockSpec((512 * CHAINS, WIDTH), row),
        whole(frames.shape),
        whole((R_END, WIDTH)),
        whole((WIDTH, channels)),
    )
    scratch = [
        pltpu.VMEM((12, 16, WIDTH), BF),
        pltpu.VMEM((256, 256), BF),
        pltpu.VMEM((256, 256), BF),
        pltpu.VMEM((384, WIDTH), BF),
        pltpu.VMEM((128, WIDTH), BF),
        pltpu.VMEM((512, WIDTH), BF),
        pltpu.VMEM((128, 512), BF),
        pltpu.VMEM((128, 256), BF),
        pltpu.VMEM((4, WIDTH, WIDTH), F32),
        pltpu.VMEM((WIDTH, WIDTH), F32),
        pltpu.VMEM((WIDTH, WIDTH), F32),
        pltpu.VMEM((4, WIDTH, WIDTH), F32),
        pltpu.VMEM((8, 256), F32),
        pltpu.VMEM((R_END, WIDTH), F32),
        pltpu.VMEM((frames.shape[0] // PROP * frames.shape[1], PROP), F32),
        pltpu.VMEM((frames.shape[0] // PROP * frames.shape[1], PROP), F32),
        pltpu.VMEM((samples // 4, 8, 4 * seq), F32),
        pltpu.VMEM((samples, seq), F32),
    ]
    return pl.pallas_call(
        block_kernel,
        grid_spec=pltpu.PrefetchScalarGridSpec(
            num_scalar_prefetch=2,
            grid=(steps,),
            in_specs=in_specs,
            out_specs=out_specs,
            scratch_shapes=scratch,
        ),
        out_shape=out_shape,
        compiler_params=pltpu.CompilerParams(vmem_limit_bytes=VMEM_LIMIT),
        name="stems_trunk",
    )(half, grid_sizes, feats, received, frames, frame_mask, token_valid, mix_weight, cot, proj, *weights)

PROJECT_STEPS = 8
FEATURE_STEPS = 4


def project_kernel(feats, proj, out, fbuf, stage, sem_f, sem_s):
    me, core = lax.axis_index("dp"), lax.axis_index("mod")
    mesh = pl.DeviceIdType.MESH
    partner = (me, 1 - core)
    slots = fbuf.shape[0]
    piece = slots // PROJECT_STEPS
    loads, sends = [], []
    for j in range(PROJECT_STEPS):
        start = pl.multiple_of((1 - core) * slots + piece * j, 16)
        loads.append(pltpu.make_async_copy(feats.at[pl.ds(start, piece)], fbuf.at[pl.ds(piece * j, piece)], sem_f.at[j]))
        loads[j].start()
    barrier = pltpu.get_barrier_semaphore()
    pl.semaphore_signal(barrier, inc=1, device_id=partner, device_id_type=mesh)
    pl.semaphore_wait(barrier, 1)
    for j in range(PROJECT_STEPS):
        part = pl.ds(piece * j, piece)
        loads[j].wait()
        stage[part] = nn(fbuf[part], proj[...]).astype(BF)
        sends.append(
            pltpu.make_async_remote_copy(
                src_ref=stage.at[part], dst_ref=out.at[part], send_sem=sem_s.at[0, j], recv_sem=sem_s.at[1, j],
                device_id=partner, device_id_type=mesh,
            )
        )
        sends[j].start()
    for j in range(PROJECT_STEPS):
        sends[j].wait()


def project_call(feats, proj):
    slots, channels = feats.shape[0] // 2, feats.shape[1]
    hbm = pl.BlockSpec(memory_space=pl.ANY)
    return pl.pallas_call(
        project_kernel,
        in_specs=[hbm, pl.BlockSpec(memory_space=pltpu.VMEM)],
        out_specs=hbm,
        out_shape=jax.ShapeDtypeStruct((slots, WIDTH), BF),
        scratch_shapes=[
            pltpu.VMEM((slots, channels), BF),
            pltpu.VMEM((slots, WIDTH), BF),
            pltpu.SemaphoreType.DMA((PROJECT_STEPS,)),
            pltpu.SemaphoreType.DMA((2, PROJECT_STEPS)),
        ],
        compiler_params=pltpu.CompilerParams(
            collective_id=1, has_side_effects=True, vmem_limit_bytes=VMEM_LIMIT
        ),
        name="project",
    )(feats, proj)


def unpack_kernel(
    chunk, vision, total, vis_query, vis_wq, prop_query, prop_wq, before,
    o_vision, o_feat, o_vq, o_vwq, o_vkv, o_vwo, o_w1, o_w2, o_pq, o_pwq, o_pkv, o_pwo,
    o_g1, o_b1, o_qkv, o_ao, o_g2, o_b2, o_in, o_out, o_rms, sem,
):
    core = lax.axis_index("mod")
    slots, channels = vision.shape
    start = pl.multiple_of((1 - core) * slots, 16)
    copy = pltpu.make_async_copy(vision, o_vision.at[pl.ds(start, slots)], sem)
    copy.start()

    n = total.shape[1]
    halves = [total[j, :, :chunk].reshape(n * chunk, WIDTH) for j in range(2)]
    half = R_END // 2

    def rows(start, count):
        source, at = halves[start // half], start % half
        return source[at : at + count].astype(F32)

    gsum = total[core, :, chunk:].reshape(n * (total.shape[2] - chunk), WIDTH).astype(F32)
    for j in range(channels // WIDTH):
        o_feat[WIDTH * j : WIDTH * j + WIDTH] = gsum[WIDTH * j : WIDTH * j + WIDTH].T
    for o_query, o_w, query, w, start in (
        (o_vq, o_vwq, vis_query, vis_wq, R_QV),
        (o_pq, o_pwq, prop_query, prop_wq, R_QP),
    ):
        grad = rows(start, 16).astype(BF)
        o_query[...] = nt(grad, w[...])
        o_w[...] = lax.dot_general(
            query[...], grad, (((0,), (0,)), ((), ())), preferred_element_type=F32
        )
    for o, start in ((o_vkv, R_VKV), (o_pkv, R_PKV)):
        o[:, :WIDTH] = rows(start, WIDTH)
        o[:, WIDTH:] = rows(start + WIDTH, WIDTH)
    o_vwo[...] = rows(R_SWO, WIDTH).T
    o_pwo[...] = rows(R_SWO + WIDTH, WIDTH).T
    o_w1[...] = rows(R_W1, 32)
    o_w2[...] = rows(R_W2, WIDTH)
    for j in range(3):
        o_qkv[:, WIDTH * j : WIDTH * j + WIDTH] = rows(R_Q + WIDTH * j, WIDTH)
    o_ao[...] = rows(R_AO, WIDTH)
    o_in[...] = rows(R_WIN, 512).T
    o_out[...] = rows(R_WOUT, 512)
    small = rows(R_LN, 16)
    for j, o in enumerate((o_g1, o_b1, o_g2, o_b2)):
        o[...] = small[j : j + 1]
    sums = [jnp.sum(small[R_STAT - R_LN + j : R_STAT - R_LN + j + 1], axis=1, keepdims=True) for j in range(4)]
    for j in range(3):
        o_rms[j] = jnp.sum(jnp.sqrt(sums[j] / (sums[3] * WIDTH)))
    copy.wait()


def unpack_call(chunk, vision, total, vis_query, vis_wq, prop_query, prop_wq, grad_vision):
    channels = vision.shape[1]
    shapes = [
        (channels, WIDTH), (16, WIDTH), (WIDTH, WIDTH), (WIDTH, 256), (WIDTH, WIDTH), (32, WIDTH),
        (WIDTH, WIDTH), (16, WIDTH), (WIDTH, WIDTH), (WIDTH, 256), (WIDTH, WIDTH), (1, WIDTH), (1, WIDTH),
        (WIDTH, 384), (WIDTH, WIDTH), (1, WIDTH), (1, WIDTH), (WIDTH, 512), (512, WIDTH), (3,),
    ]
    vmem, hbm = pl.BlockSpec(memory_space=pltpu.VMEM), pl.BlockSpec(memory_space=pltpu.HBM)
    return pl.pallas_call(
        functools.partial(unpack_kernel, chunk),
        in_specs=[vmem] * 6 + [hbm],
        out_specs=[hbm] + [vmem] * (len(shapes) - 1) + [pl.BlockSpec(memory_space=pltpu.SMEM)],
        out_shape=[jax.ShapeDtypeStruct(grad_vision.shape, BF)] + [jax.ShapeDtypeStruct(s, F32) for s in shapes],
        scratch_shapes=[pltpu.SemaphoreType.DMA],
        input_output_aliases={6: 0},
        compiler_params=pltpu.CompilerParams(vmem_limit_bytes=20 * 2**20),
        name="unpack",
    )(vision, total, *map(in_hbm, (vis_query, vis_wq, prop_query, prop_wq)), grad_vision)


def finish_kernel(
    n, chunk, gchunk, acc, gsum, dtok, feats, proj, total, vision,
    dother, pbuf, fbuf, gbuf, own_a, recv_a, send_b, recv_b, send_g, recv_g, reduced,
    sem_t, sem_f, sem_a, sem_b, sem_c, sem_d, sem_g,
):
    me, core = lax.axis_index("dp"), lax.axis_index("mod")
    mesh = pl.DeviceIdType.MESH
    partner = (me, 1 - core)
    half = R_END // 2
    slots, channels = fbuf.shape
    piece = slots // FEATURE_STEPS

    def remote(src, dst, send_sem, recv_sem, device):
        return pltpu.make_async_remote_copy(
            src_ref=src, dst_ref=dst, send_sem=send_sem, recv_sem=recv_sem, device_id=device, device_id_type=mesh
        )

    def rows(index, count):
        return pl.ds(pl.multiple_of(index * count, 16), count)

    barrier = pltpu.get_barrier_semaphore()
    pl.semaphore_signal(barrier, inc=1, device_id=partner, device_id_type=mesh)

    def greet(k, carry):
        pl.semaphore_signal(barrier, inc=1, device_id=(lax.rem(me + k, n), core), device_id_type=mesh)
        return carry

    lax.fori_loop(1, n, greet, 0)
    load_a = pltpu.make_async_copy(acc.at[rows(core, half)], own_a, sem_a.at[2])
    load_a.start()
    load_g = pltpu.make_async_copy(gsum, gbuf, sem_a.at[3])
    load_g.start()
    load_p = pltpu.make_async_copy(proj, pbuf, sem_a.at[4])
    load_p.start()
    tokens, features = [], []
    for j in range(FEATURE_STEPS):
        part = pl.ds(piece * j, piece)
        start_row = pl.multiple_of((1 - core) * slots + piece * j, 16)
        features.append(pltpu.make_async_copy(feats.at[pl.ds(start_row, piece)], fbuf.at[part], sem_f.at[j]))
        features[j].start()
    pl.semaphore_wait(barrier, n)

    copy_a = remote(acc.at[rows(1 - core, half)], recv_a, sem_a.at[0], sem_a.at[1], partner)
    copy_a.start()
    for j in range(FEATURE_STEPS):
        part = pl.ds(piece * j, piece)
        tokens.append(remote(dtok.at[part], dother.at[part], sem_t.at[0, j], sem_t.at[1, j], partner))
        tokens[j].start()
    if half < n * chunk:
        send_b[half:] = jnp.zeros((n * chunk - half, WIDTH), BF)
    load_a.wait()
    copy_a.wait()
    send_b[:half] = (own_a[...].astype(F32) + recv_a[...].astype(F32)).astype(BF)

    def scatter(k):
        peer = lax.rem(me + k, n)
        return remote(
            send_b.at[rows(peer, chunk)], recv_b.at[k - 1], sem_b.at[0, k - 1], sem_b.at[1, k - 1], (peer, core)
        )

    def scatter_g(k):
        peer = lax.rem(me + k, n)
        return remote(
            send_g.at[rows(peer, gchunk)], recv_g.at[k - 1], sem_g.at[0, k - 1], sem_g.at[1, k - 1], (peer, core)
        )

    def gather(k):
        peer = lax.rem(me + k, n)
        return remote(reduced, total.at[core, me], sem_c.at[0, k - 1], sem_c.at[1, k - 1], (peer, core))

    def forward(k):
        piece_k = total.at[core, lax.rem(me + n - k, n), pl.ds(0, chunk)]
        return remote(piece_k, piece_k, sem_d.at[0, k], sem_d.at[1, k], partner)

    def each(first, step):
        def body(k, carry):
            step(k)
            return carry

        lax.fori_loop(first, n, body, 0)

    each(1, lambda k: scatter(k).start())

    load_g.wait()
    grad = gbuf[...]
    for j in range(FEATURE_STEPS):
        tokens[j].wait()
        features[j].wait()
        part = slice(piece * j, piece * j + piece)
        grad = grad + nn(dother[part].T, fbuf[part])
    used = WIDTH * (channels // WIDTH)
    for j in range(channels // WIDTH):
        send_g[WIDTH * j : WIDTH * j + WIDTH] = grad[:, WIDTH * j : WIDTH * j + WIDTH].astype(BF)
    if used < n * gchunk:
        send_g[used:] = jnp.zeros((n * gchunk - used, WIDTH), BF)
    each(1, lambda k: scatter_g(k).start())
    load_p.wait()
    for j in range(FEATURE_STEPS):
        part = slice(piece * j, piece * j + piece)
        vision[part] = nt(dother[part], pbuf[...]).astype(BF)

    def add(k, value):
        scatter(k).wait()
        return value + recv_b[k - 1].astype(F32)

    def add_g(k, value):
        scatter_g(k).wait()
        return value + recv_g[k - 1].astype(F32)

    reduced[:chunk] = lax.fori_loop(1, n, add, send_b[rows(me, chunk)].astype(F32)).astype(BF)
    reduced[chunk:] = lax.fori_loop(1, n, add_g, send_g[rows(me, gchunk)].astype(F32)).astype(BF)
    each(1, lambda k: gather(k).start())
    total[core, me] = reduced[...]
    forward(0).start()

    def pass_on(k):
        gather(k).wait()
        forward(k).start()

    each(1, pass_on)
    each(0, lambda k: forward(k).wait())


def in_hbm(value):
    return pltpu.with_memory_space_constraint(value, pltpu.HBM)


def finish_call(acc, gsum, dtok, feats, proj, n):
    slots, channels = dtok.shape[0], feats.shape[1]
    half = R_END // 2
    chunk = 16 * -(-half // (16 * n))
    gchunk = 16 * -(-channels // (16 * n))
    vmem = pl.BlockSpec(memory_space=pltpu.VMEM)
    hbm = pl.BlockSpec(memory_space=pltpu.HBM)
    dma = pltpu.SemaphoreType.DMA
    total, vision = pl.pallas_call(
        functools.partial(finish_kernel, n, chunk, gchunk),
        out_shape=(
            jax.ShapeDtypeStruct((2, n, chunk + gchunk, WIDTH), BF),
            jax.ShapeDtypeStruct((slots, channels), BF),
        ),
        in_specs=[hbm] * 5,
        out_specs=(vmem, vmem),
        scratch_shapes=[
            pltpu.VMEM(dtok.shape, BF),
            pltpu.VMEM(proj.shape, BF),
            pltpu.VMEM((slots, channels), BF),
            pltpu.VMEM(gsum.shape, F32),
            pltpu.VMEM((half, WIDTH), BF),
            pltpu.VMEM((half, WIDTH), BF),
            pltpu.VMEM((n * chunk, WIDTH), BF),
            pltpu.VMEM((n - 1, chunk, WIDTH), BF),
            pltpu.VMEM((n * gchunk, WIDTH), BF),
            pltpu.VMEM((n - 1, gchunk, WIDTH), BF),
            pltpu.VMEM((chunk + gchunk, WIDTH), BF),
            dma((2, FEATURE_STEPS)),
            dma((FEATURE_STEPS,)),
            dma((5,)),
            dma((2, n - 1)),
            dma((2, n - 1)),
            dma((2, n)),
            dma((2, n - 1)),
        ],
        compiler_params=pltpu.CompilerParams(
            collective_id=0, has_side_effects=True, vmem_limit_bytes=28 * 2**20
        ),
        name="finish",
    )(*map(in_hbm, (acc, gsum, dtok, feats, proj)))
    return chunk, total, vision


def per_device(
    vision_feats, vision_grid, proprio, proprio_mask, token_valid, mix_weight, out_cot, feat_proj,
    vis_query, vis_wq, vis_kv, vis_wo, prop_w1, prop_w2, prop_query, prop_wq, prop_kv, prop_wo,
    ln1_gain, ln1_bias, qkv_weight, attn_out, ln2_gain, ln2_bias, mlp_in, mlp_out,
):
    me = lax.axis_index("mod").astype(jnp.int32)
    own = me.reshape(1)
    feats = vision_feats.reshape(-1, vision_feats.shape[3])
    received = project_call(feats, feat_proj)
    weights = (
        vis_query, vis_wq, vis_kv, vis_wo, prop_w1, prop_w2, prop_query, prop_wq, prop_kv, prop_wo,
        *(v.reshape(1, -1) for v in (ln1_gain, ln1_bias, ln2_gain, ln2_bias)), qkv_weight, attn_out, mlp_in, mlp_out,
    )
    frames = jnp.transpose(proprio, (1, 2, 3, 0)).reshape(-1, proprio.shape[0])
    frame_mask = jnp.transpose(proprio_mask, (1, 2, 0)).reshape(-1, proprio_mask.shape[0])
    grid_sizes = jnp.transpose(vision_grid, (1, 2, 0)).reshape(4, -1)
    output, grad_vision, dtok, dframes, acc, gfeat = block_call(
        own, grid_sizes, feats, received, frames, frame_mask, token_valid, mix_weight.reshape(1, -1),
        out_cot.reshape(-1, WIDTH), feat_proj, weights,
    )
    chunk, total, vision = finish_call(acc, gfeat, dtok, feats, feat_proj, lax.axis_size("dp"))
    grad_vision, *outs = unpack_call(
        chunk, vision, total, vis_query, vis_wq, prop_query, prop_wq, grad_vision
    )
    vectors = {11, 12, 15, 16}
    outs = [o.reshape(WIDTH) if j in vectors else o for j, o in enumerate(outs)]
    return (
        output.reshape(out_cot.shape),
        grad_vision.reshape(vision_feats.shape),
        jnp.transpose(dframes.reshape(proprio.shape[1:] + proprio.shape[:1]), (3, 0, 1, 2)),
        *outs,
    )


def solution(mesh):
    both = ("dp", "mod")
    return jax.shard_map(
        per_device,
        mesh=mesh,
        in_specs=(
            P("dp", None, None, "mod"),
            P(both, None, None),
            P(both, None, None, None),
            P(both, None, None),
            P(both, None),
            P(both),
            P(both, None, None),
            P("mod", None),
        ) + (P(),) * 18,
        out_specs=(
            P(both, None, None),
            P("dp", None, None, "mod"),
            P(both, None, None, None),
            P("mod", None),
        ) + (P(),) * 19,
        check_vma=False,
    )
```

```python
import functools
import math

import jax
import jax.numpy as jnp
from jax import lax
from jax.experimental import pallas as pl
from jax.experimental.pallas import tpu as pltpu
from jax.sharding import PartitionSpec as P

HEADS = 8
HEAD = 16
WIDTH = 128
PROP = 32
NEG = -1e30
BF = jnp.bfloat16
F32 = jnp.float32
VMEM_LIMIT = 60 * 2**20
CHAINS = 8
FF_PART = 256

R_WIN, R_WOUT, R_Q, R_KV, R_AO = 0, 512, 1024, 1152, 1408
R_SWO, R_VKV, R_PKV, R_W2, R_W1 = 1536, 1792, 2048, 2304, 2432
R_QV, R_QP, R_LN, R_STAT, R_END = 2464, 2480, 2496, 2500, 2560


def nn(a, b):
    return lax.dot_general(a, b, (((1,), (0,)), ((), ())), preferred_element_type=F32)


def nt(a, b):
    return lax.dot_general(a, b, (((1,), (1,)), ((), ())), preferred_element_type=F32)


def cat(items, axis):
    return jnp.concatenate(items, axis=axis)


def lane_iota(rows, lanes):
    return lax.broadcasted_iota(jnp.int32, (rows, lanes), 1)


def tile_to(mask, rows, lanes):
    return cat([cat([mask] * (rows // mask.shape[0]), 0)] * (lanes // mask.shape[1]), 1)


def head_expand(value, masks):
    return cat([value * tile_to(mask, *value.shape) for mask in masks], 0)


def head_select(full, heads, period):
    rows, lanes = full.shape[0] // heads, full.shape[1]
    head = (lane_iota(rows, lanes) & (period - 1)) >> 4
    out = full[:rows]
    for h in range(1, heads):
        out = jnp.where(head == h, full[h * rows : (h + 1) * rows], out)
    return out


def turn(value):
    out = []
    for j in range(0, value.shape[1], WIDTH):
        out += [value[:, j + 64 : j + 128], value[:, j : j + 64]]
    return cat(out, 1)


def diagonal(blocks):
    out = []
    for j, block in enumerate(blocks):
        row = [block if k == j else jnp.zeros((block.shape[0], other.shape[1]), BF) for k, other in enumerate(blocks)]
        out.append(cat(row, 1))
    return cat(out, 0)


def pair_up(parts):
    return cat([cat(parts[j : j + 2], 1) for j in range(0, 8, 2)], 0)


def unpair(value, rows):
    out = []
    for j in range(4):
        part = value[rows * j : rows * j + rows]
        out += [part[:, :WIDTH], part[:, WIDTH:]]
    return cat(out, 0)


def softmax_rows(scores):
    peak = jnp.max(scores, axis=1, keepdims=True)
    weights = jnp.exp(scores - peak)
    return weights * (1.0 / jnp.sum(weights, axis=1, keepdims=True))


def softmax_grad(weights, grad):
    return weights * (grad - jnp.sum(weights * grad, axis=1, keepdims=True))


def mean_rows(value):
    return jnp.sum(value, axis=0, keepdims=True) * (1.0 / value.shape[0])


def norm_rows(value):
    centered = value - mean_rows(value)
    scale = lax.rsqrt(mean_rows(centered * centered) + 1e-05)
    return centered * scale, scale


def norm_rows_grad(grad, hat, scale):
    return scale * (grad - mean_rows(grad) - hat * mean_rows(grad * hat))


def split_samples(value, low_half, high_half):
    out = []
    for s in range(4):
        half = tile_to(high_half if s % 2 else low_half, 64, WIDTH)
        block = value[:, WIDTH * (s // 2) : WIDTH * (s // 2) + WIDTH] * half
        zero = jnp.zeros((64, WIDTH), BF)
        out.append(cat([block, zero] if s < 2 else [zero, block], 1))
    return cat(out, 0)


def gather_heads(value, turned, group, low_half, high_half):
    low_tall, high_tall = tile_to(low_half, 64, WIDTH), tile_to(high_half, 64, WIDTH)
    out = []
    for s in (0, 2):
        even, odd = slice(64 * s, 64 * s + 64), slice(64 * s + 64, 64 * s + 128)
        left, right = (value[even], turned[odd]) if group == 0 else (turned[even], value[odd])
        out.append(left * low_tall + right * high_tall)
    return cat(out, 1)


def scatter_heads(parts, low_half, high_half):
    low_tall, high_tall = tile_to(low_half, 64, WIDTH), tile_to(high_half, 64, WIDTH)
    turned = [turn(part) for part in parts]
    out = []
    for s in range(4):
        lanes = slice(WIDTH * (s // 2), WIDTH * (s // 2) + WIDTH)
        left = (turned if s % 2 else parts)[0][:, lanes]
        right = (parts if s % 2 else turned)[1][:, lanes]
        out.append(left * low_tall + right * high_tall)
    return cat(out, 0)


def spread_keys(value, turned, group, low_half, high_half):
    zero = jnp.zeros((HEAD, WIDTH), BF)
    rows = []
    for s in range(4):
        lanes = slice(WIDTH * (s // 2), WIDTH * (s // 2) + WIDTH)
        for local in range(4):
            h = group * 4 + local
            source = value if s % 2 == local % 2 else turned
            block = source[h * HEAD : (h + 1) * HEAD, lanes] * (high_half if local % 2 else low_half)
            rows.append(cat([block, zero] if local < 2 else [zero, block], 1))
    return cat(rows, 0)


def mix_keys(value, weights, low_half, high_half, first):
    turned = turn(value)
    out = []
    for group in range(2):
        full = nn(spread_keys(value, turned, group, low_half, high_half), weights[group])
        left = jnp.where(first, full[:64, :WIDTH], full[64:128, :WIDTH])
        right = jnp.where(first, full[128:192, WIDTH:], full[192:, WIDTH:])
        out.append(cat([left, right], 1))
    return cat(out, 0)


def stem_queries(query, w_query, masks):
    value = nn(query, w_query).astype(BF)
    return head_expand(value * jnp.asarray(0.25, BF), masks)


def block_kernel(
    half, grid_ref, feats, pr, frames, frame_mask, token_valid, mix_weight, cot, proj,
    vis_query, vis_wq, vis_kv, vis_wo, prop_w1, prop_w2, prop_query, prop_wq, prop_kv, prop_wo,
    ln1_gain, ln1_bias, ln2_gain, ln2_bias, qkv_w, attn_out, mlp_in, mlp_out,
    out, grad_feats, dtok_ref, dframes, acc_out,
    masks_ref, qv_ref, qp_ref, wqkv_t, ao_t, win_t, wout_t, stem_t, ln_ref,
    gv_ref, gp_ref, lnacc, stat, acc, fr_ref, df_ref, aux_ref, turn_ref,
):
    blocks = token_valid.shape[0] // 4
    step = pl.program_id(0)

    @pl.when(step == 0)
    def _():
        lane = lane_iota(16, WIDTH) >> 4
        for h in range(HEADS):
            masks_ref[h] = jnp.where(lane == h, 1.0, 0.0).astype(BF)
        for h in range(4):
            masks_ref[HEADS + h] = jnp.where((lane & 3) == h, 1.0, 0.0).astype(BF)
        masks = [masks_ref[h] for h in range(HEADS)]
        qv_ref[...] = diagonal([stem_queries(vis_query[...], vis_wq[...], masks)] * 2)
        qp_ref[...] = diagonal([stem_queries(prop_query[...], prop_wq[...], masks)] * 2)
        wqkv_t[...] = qkv_w[...].T
        ao_t[...] = attn_out[...].T
        win_t[...] = mlp_in[...].T
        wout_t[...] = mlp_out[...].T
        stem_t[:, :WIDTH] = vis_wo[...].T
        stem_t[:, WIDTH:] = prop_wo[...].T
        for j, vector in enumerate((ln1_gain, ln1_bias, ln2_gain, ln2_bias)):
            ln_ref[j] = jnp.broadcast_to(vector[...].astype(F32), (WIDTH, WIDTH)).T

        def by_block(ref):
            return cat([ref[pl.ds(j, blocks, stride=4)].astype(F32) for j in range(4)], 1)

        valid = by_block(token_valid)
        turn_ref[...] = jnp.broadcast_to(mix_weight[...].astype(F32), turn_ref.shape).T
        mix = by_block(turn_ref)
        turn_ref[:, : frame_mask.shape[0]] = frame_mask[...].astype(F32).T
        frame_keep = cat([turn_ref[pl.ds(j, blocks, stride=4)][:, : frame_mask.shape[0]] for j in range(4)], 1)
        values = (valid, mix, jnp.where(valid > 0, 0.0, NEG), jnp.where(cat([frame_keep] * 2, 1) > 0, 0.0, NEG))
        for i in range(blocks):
            for j, value in enumerate(values):
                aux_ref[i, j : j + 1] = value[i : i + 1]

        for j in range(frames.shape[0] // PROP):
            block = frames[PROP * j : PROP * j + PROP].astype(F32).T
            fr_ref[pl.ds(j, block.shape[0], stride=frames.shape[0] // PROP)] = block
        acc[...] = jnp.zeros_like(acc)
        gv_ref[...] = jnp.zeros_like(gv_ref)
        gp_ref[...] = jnp.zeros_like(gp_ref)
        lnacc[...] = jnp.zeros_like(lnacc)
        stat[...] = jnp.zeros_like(stat)

    masks = [masks_ref[h] for h in range(HEADS)]
    masks_group = [masks_ref[HEADS + h] for h in range(4)]
    qv, qp = qv_ref[...], qp_ref[...]
    lane = lane_iota(HEAD, WIDTH)
    low_half = jnp.where(lane < 64, 1.0, 0.0).astype(BF)
    high_half = jnp.where(lane < 64, 0.0, 1.0).astype(BF)
    first = lane_iota(64, WIDTH) < 64


    def chain(g):
        block = step * CHAINS + g
        slots = slice(512 * g, 512 * g + 512)
        kept = nn(feats[slots], proj[...]).astype(BF)
        tok = (kept.astype(F32) + pr[slots].astype(F32)).astype(BF)
        vkv = nn(tok, vis_kv[...]).astype(BF)
        vk, vv = vkv[:, :WIDTH], vkv[:, WIDTH:]
        slot = lax.broadcasted_iota(jnp.int32, (64, WIDTH), 0)
        slot_row, slot_col = slot >> 3, slot & 7
        bias = []
        for st in range(8):
            s, t = (step * CHAINS + g) * 4 + st // 2, st % 2
            keep = (slot_row < grid_ref[2 * t, s]) & (slot_col < grid_ref[2 * t + 1, s])
            bias.append(jnp.where(keep, 0.0, NEG))
        bias = pair_up(bias).reshape(4, 64, 256)
        vk2 = pair_up([vk[64 * st : 64 * st + 64] for st in range(8)])
        vv2 = pair_up([vv[64 * st : 64 * st + 64] for st in range(8)])
        yield
        vp = softmax_rows(nt(vk2, qv).reshape(4, 64, 256) + bias)
        vpb = vp.reshape(256, 256).astype(BF)
        yield
        vpt = vpb.T
        vmixed = [None] * 8
        for e in range(2):
            for m in range(2):
                one, two = 4 * m + e, 4 * m + 2 + e
                spread = diagonal([vv[64 * one : 64 * one + 64], vv[64 * two : 64 * two + 64]])
                lhs = vpt[WIDTH * e : WIDTH * e + WIDTH, WIDTH * m : WIDTH * m + WIDTH]
                both = head_select(nn(lhs, spread), HEADS, WIDTH).astype(BF)
                vmixed[one], vmixed[two] = both[:, :WIDTH], both[:, WIDTH:]

        yield
        fr_rows = pl.ds(pl.multiple_of((step * CHAINS + g) * 128, 128), 128)
        fr = fr_ref[fr_rows].astype(BF)
        pre = nn(fr, prop_w1[...])
        gate = jax.nn.sigmoid(pre)
        hidden = (pre * gate).astype(BF)
        ptok = nn(hidden, prop_w2[...]).astype(BF)
        pkv = nn(ptok, prop_kv[...]).astype(BF)
        pk, pv = pkv[:, :WIDTH], pkv[:, WIDTH:]
        column = jnp.broadcast_to(aux_ref[block, 3:4, :WIDTH], (WIDTH, WIDTH)).T
        parts = lambda v: [v[HEAD * st : HEAD * st + HEAD] for st in range(8)]
        pbias = pair_up(parts(column))
        pk2, pv2 = pair_up(parts(pk)), pair_up(parts(pv))
        yield
        pp = softmax_rows((nt(pk2, qp) + pbias).reshape(4, HEAD, 256))
        ppb = pp.reshape(64, 256).astype(BF)
        ppt = ppb.T
        pmixed = [None] * 8
        for e in range(2):
            spread = diagonal([pv[HEAD * st : HEAD * st + HEAD] for st in range(e, 8, 2)])
            both = head_select(nn(ppt[WIDTH * e : WIDTH * e + WIDTH], spread), HEADS, WIDTH).astype(BF)
            for j in range(4):
                pmixed[2 * j + e] = both[:, WIDTH * j : WIDTH * j + WIDTH]

        yield
        zero16 = jnp.zeros((HEAD, WIDTH), BF)
        rows = []
        for st in range(8):
            rows.append(cat([vmixed[st], zero16], 1))
            rows.append(cat([zero16, pmixed[st]], 1))
        mixed_ext = cat(rows, 0)
        x = nt(stem_t[...], mixed_ext)
        g1, b1, g2, b2 = [cat([ln_ref[j]] * 2, 1) for j in range(4)]
        hat1, scale1 = norm_rows(x)
        n1 = (hat1 * g1 + b1).astype(BF)
        yield
        qkv = nn(wqkv_t[...], n1).astype(BF)
        qt, kt, vt = qkv[:WIDTH] * jnp.asarray(0.25, BF), qkv[WIDTH : 2 * WIDTH], qkv[2 * WIDTH :]
        kn, vn = kt.T, vt.T
        kn_turned, vn_turned = turn(kn), turn(vn)
        yield
        weights, weights_b, query_bd = [], [], []
        tbias = []
        for p in range(2):
            column = jnp.broadcast_to(aux_ref[block, 2:3, 128 * p : 128 * p + 128], (WIDTH, WIDTH)).T
            tbias.append(jnp.where(first, column[:64], column[64:]))
        tbias = cat(tbias, 1)[None]
        for group in range(2):
            part = slice(64 * group, 64 * group + 64)
            qbd = split_samples(qt[part], low_half, high_half)
            keys = head_expand(gather_heads(kn, kn_turned, group, low_half, high_half), masks_group)
            scores = nn(keys, qbd).reshape(4, 64, 256) + tbias
            yield
            w = softmax_rows(scores)
            weights.append(w)
            weights_b.append(w.reshape(256, 256).astype(BF))
            query_bd.append(qbd)
            yield
        mixed = mix_keys(vt, weights_b, low_half, high_half, first).astype(BF)
        yield
        branch = nn(ao_t[...], mixed)
        middle = x + branch
        hat2, scale2 = norm_rows(middle)
        n2 = (hat2 * g2 + b2).astype(BF)
        yield
        c = math.sqrt(2.0 / math.pi)
        seed = cot[256 * g : 256 * g + 256].T.astype(F32) * aux_ref[block, 1:2, :]
        dmlp = seed.astype(BF)
        mlp, dn2, act_all, dup_all = 0.0, 0.0, [], []
        for j in range(512 // FF_PART):
            part = slice(FF_PART * j, FF_PART * j + FF_PART)
            up = nn(win_t[part], n2)
            yield
            square = up * up
            h = 0.5 + 0.5 * jnp.tanh(up * (c + (c * 0.044715) * square))
            act = up * h
            slope = h + act * (1.0 - h) * (2 * c + (6 * c * 0.044715) * square)
            act_b = act.astype(BF)
            mlp = mlp + nn(wout_t[:, part], act_b)
            dup = (nn(mlp_out[part], dmlp) * slope).astype(BF)
            yield
            dn2 = dn2 + nn(mlp_in[:, part], dup)
            acc[R_WOUT + FF_PART * j : R_WOUT + FF_PART * j + FF_PART] += nt(act_b, dmlp)
            acc[R_WIN + FF_PART * j : R_WIN + FF_PART * j + FF_PART] += nt(dup, n2)
            yield
        final = middle + mlp
        out[256 * g : 256 * g + 256] = final.astype(BF).T
        valid = aux_ref[block, 0:1, :]
        for j, value in enumerate((final, branch, mlp)):
            stat[j : j + 1, :] += jnp.sum(value * value, axis=0, keepdims=True) * valid
        stat[3:4, :] += valid

        yield
        fold = lambda v: v[:, :WIDTH] + v[:, WIDTH:]
        lnacc[2] += fold(dn2 * hat2)
        lnacc[3] += fold(dn2)
        dmid = seed + norm_rows_grad(dn2 * g2, hat2, scale2)
        dbranch = dmid.astype(BF)
        acc[R_AO : R_AO + WIDTH] += nt(mixed, dbranch)
        yield
        dmixed = nn(attn_out[...], dbranch).astype(BF)
        yield
        ds_all, dk, dv = [], [], []
        for group in range(2):
            part = slice(64 * group, 64 * group + 64)
            dbd = split_samples(dmixed[part], low_half, high_half)
            values = head_expand(gather_heads(vn, vn_turned, group, low_half, high_half), masks_group)
            dw = nn(values, dbd).reshape(4, 64, 256)
            yield
            ds = softmax_grad(weights[group], dw).reshape(256, 256).astype(BF)
            dv.append(head_select(nt(weights_b[group], dbd), 4, 64).astype(BF))
            dk.append(head_select(nt(ds, query_bd[group]), 4, 64).astype(BF))
            ds_all.append(ds)
        dq = (mix_keys(kt, ds_all, low_half, high_half, first) * 0.25).astype(BF)
        dkv = cat([scatter_heads(dk, low_half, high_half), scatter_heads(dv, low_half, high_half)], 1)
        yield
        acc[R_Q : R_Q + WIDTH] += nt(n1, dq)
        grad = nn(n1, dkv)
        acc[R_KV : R_KV + WIDTH] += grad[:, :WIDTH]
        acc[R_KV + WIDTH : R_KV + 2 * WIDTH] += grad[:, WIDTH:]
        dn1 = nn(qkv_w[:, :WIDTH], dq) + nt(qkv_w[:, WIDTH:], dkv)
        lnacc[0] += fold(dn1 * hat1)
        lnacc[1] += fold(dn1)
        dx = (dmid + norm_rows_grad(dn1 * g1, hat1, scale1)).astype(BF)

        yield
        grad = nn(dx, mixed_ext)
        acc[R_SWO : R_SWO + WIDTH] += grad[:, :WIDTH]
        acc[R_SWO + WIDTH : R_SWO + 2 * WIDTH] += grad[:, WIDTH:]
        dstem = nn(dx.T, stem_t[...]).astype(BF)
        dw, dv, pdw, pdv = [], [], [], []
        for st in range(8):
            j, e, r = st // 2, st % 2, 32 * st
            tall, short, lanes = slice(64 * j, 64 * j + 64), slice(HEAD * j, HEAD * j + HEAD), slice(WIDTH * e, WIDTH * e + WIDTH)
            spread = head_expand(cat([dstem[r : r + 16, :WIDTH], dstem[r + 16 : r + 32, WIDTH:]], 1), masks)
            full = nt(diagonal([vv2[tall, lanes], pv2[short, lanes]]), spread)
            dw.append(full[:64])
            pdw.append(full[64:])
            full = nn(
                diagonal([vpb[tall, lanes], ppb[short, lanes]]), cat([spread[:, :WIDTH], spread[:, WIDTH:]], 0)
            ).astype(BF)
            dv.append(full[:64])
            pdv.append(full[64:])
        yield
        ds = softmax_grad(vp, pair_up(dw).reshape(4, 64, 256)).reshape(256, 256).astype(BF)
        dkv = cat([unpair(nn(ds, qv).astype(BF), 64), cat(dv, 0)], 1)
        dtok = nt(dkv, vis_kv[...]).astype(BF)
        dtok_ref[slots] = dtok
        grad_feats[slots] = nt(dtok, proj[...]).astype(BF)
        grad = nn(tok.T, dkv)
        acc[R_VKV : R_VKV + WIDTH] += grad[:, :WIDTH]
        acc[R_VKV + WIDTH : R_VKV + 2 * WIDTH] += grad[:, WIDTH:]
        full = nn(ds.T, vk2)
        gv_ref[...] += full[:WIDTH, :WIDTH] + full[WIDTH:, WIDTH:]

        yield
        ds = softmax_grad(pp, pair_up(pdw).reshape(4, HEAD, 256)).reshape(64, 256).astype(BF)
        dkv = cat([unpair(nn(ds, qp).astype(BF), HEAD), cat(pdv, 0)], 1)
        dptok = nt(dkv, prop_kv[...]).astype(BF)
        grad = nn(ptok.T, dkv)
        acc[R_PKV : R_PKV + WIDTH] += grad[:, :WIDTH]
        acc[R_PKV + WIDTH : R_PKV + 2 * WIDTH] += grad[:, WIDTH:]
        full = nn(ds.T, pk2)
        gp_ref[...] += full[:WIDTH, :WIDTH] + full[WIDTH:, WIDTH:]
        yield
        acc[R_W2 : R_W2 + WIDTH] += nn(hidden.T, dptok)
        dhidden = nt(dptok, prop_w2[...])
        dpre = (dhidden * (gate * (1.0 + pre * (1.0 - gate)))).astype(BF)
        acc[R_W1 : R_W1 + 32] += nn(fr.T, dpre)
        df_ref[fr_rows] = nt(dpre, prop_w1[...])

        yield

    live = [(g // 2 * 6, chain(g)) for g in range(CHAINS)]
    tick = 0
    while live:
        for one in list(live):
            if tick >= one[0] and next(one[1], live) is live:
                live.remove(one)
        tick += 1

    @pl.when(step == pl.num_programs(0) - 1)
    def _():
        acc[R_QV : R_QV + 16] = head_select(gv_ref[...], HEADS, WIDTH) * 0.25
        acc[R_QP : R_QP + 16] = head_select(gp_ref[...], HEADS, WIDTH) * 0.25
        for j in range(4):
            acc[R_LN + j : R_LN + j + 1] = jnp.sum(lnacc[j].T, axis=0, keepdims=True)
            acc[R_STAT + j : R_STAT + j + 1] = stat[j : j + 1, :WIDTH] + stat[j : j + 1, WIDTH:]
        acc_out[...] = acc[...].astype(BF)
        for j in range(frames.shape[0] // PROP):
            block = df_ref[pl.ds(j, frames.shape[1], stride=frames.shape[0] // PROP)]
            dframes[PROP * j : PROP * j + PROP] = block.T.astype(BF)


def whole(shape):
    return pl.BlockSpec(shape, lambda i, *_: (0,) * len(shape))


def block_call(half, grid_sizes, feats, received, frames, frame_mask, token_valid, mix_weight, cot, proj, weights):
    samples, seq = token_valid.shape
    steps = samples // (4 * CHAINS)
    channels = feats.shape[1]
    row = lambda i, *_: (i, 0)
    own = lambda i, half, _: (half[0] * steps + i, 0)
    in_specs = [
        pl.BlockSpec((512 * CHAINS, channels), own),
        pl.BlockSpec((512 * CHAINS, WIDTH), row),
        whole(frames.shape),
        whole(frame_mask.shape),
        whole(token_valid.shape),
        whole(mix_weight.shape),
        pl.BlockSpec((256 * CHAINS, WIDTH), row),
        whole(proj.shape),
    ] + [whole(w.shape) for w in weights]
    out_shape = (
        jax.ShapeDtypeStruct((256 * CHAINS * steps, WIDTH), BF),
        jax.ShapeDtypeStruct(feats.shape, BF),
        jax.ShapeDtypeStruct((512 * CHAINS * steps, WIDTH), BF),
        jax.ShapeDtypeStruct(frames.shape, BF),
        jax.ShapeDtypeStruct((R_END, WIDTH), BF),
    )
    out_specs = (
        pl.BlockSpec((256 * CHAINS, WIDTH), row),
        pl.BlockSpec((512 * CHAINS, channels), own),
        pl.BlockSpec((512 * CHAINS, WIDTH), row),
        whole(frames.shape),
        whole((R_END, WIDTH)),
    )
    scratch = [
        pltpu.VMEM((12, 16, WIDTH), BF),
        pltpu.VMEM((256, 256), BF),
        pltpu.VMEM((256, 256), BF),
        pltpu.VMEM((384, WIDTH), BF),
        pltpu.VMEM((128, WIDTH), BF),
        pltpu.VMEM((512, WIDTH), BF),
        pltpu.VMEM((128, 512), BF),
        pltpu.VMEM((128, 256), BF),
        pltpu.VMEM((4, WIDTH, WIDTH), F32),
        pltpu.VMEM((WIDTH, WIDTH), F32),
        pltpu.VMEM((WIDTH, WIDTH), F32),
        pltpu.VMEM((4, WIDTH, WIDTH), F32),
        pltpu.VMEM((8, 256), F32),
        pltpu.VMEM((R_END, WIDTH), F32),
        pltpu.VMEM((frames.shape[0] // PROP * frames.shape[1], PROP), F32),
        pltpu.VMEM((frames.shape[0] // PROP * frames.shape[1], PROP), F32),
        pltpu.VMEM((samples // 4, 8, 4 * seq), F32),
        pltpu.VMEM((samples, seq), F32),
    ]
    return pl.pallas_call(
        block_kernel,
        grid_spec=pltpu.PrefetchScalarGridSpec(
            num_scalar_prefetch=2,
            grid=(steps,),
            in_specs=in_specs,
            out_specs=out_specs,
            scratch_shapes=scratch,
        ),
        out_shape=out_shape,
        compiler_params=pltpu.CompilerParams(vmem_limit_bytes=VMEM_LIMIT),
        name="stems_trunk",
    )(half, grid_sizes, feats, received, frames, frame_mask, token_valid, mix_weight, cot, proj, *weights)

PROJECT_STEPS = 8
FEATURE_STEPS = 4


def project_kernel(feats, proj, out, fbuf, stage, sem_f, sem_s):
    me, core = lax.axis_index("dp"), lax.axis_index("mod")
    mesh = pl.DeviceIdType.MESH
    partner = (me, 1 - core)
    slots = fbuf.shape[0]
    piece = slots // PROJECT_STEPS
    loads, sends = [], []
    for j in range(PROJECT_STEPS):
        start = pl.multiple_of((1 - core) * slots + piece * j, 16)
        loads.append(pltpu.make_async_copy(feats.at[pl.ds(start, piece)], fbuf.at[pl.ds(piece * j, piece)], sem_f.at[j]))
        loads[j].start()
    barrier = pltpu.get_barrier_semaphore()
    pl.semaphore_signal(barrier, inc=1, device_id=partner, device_id_type=mesh)
    pl.semaphore_wait(barrier, 1)
    for j in range(PROJECT_STEPS):
        part = pl.ds(piece * j, piece)
        loads[j].wait()
        stage[part] = nn(fbuf[part], proj[...]).astype(BF)
        sends.append(
            pltpu.make_async_remote_copy(
                src_ref=stage.at[part], dst_ref=out.at[part], send_sem=sem_s.at[0, j], recv_sem=sem_s.at[1, j],
                device_id=partner, device_id_type=mesh,
            )
        )
        sends[j].start()
    for j in range(PROJECT_STEPS):
        sends[j].wait()


def project_call(feats, proj):
    slots, channels = feats.shape[0] // 2, feats.shape[1]
    hbm = pl.BlockSpec(memory_space=pl.ANY)
    return pl.pallas_call(
        project_kernel,
        in_specs=[hbm, pl.BlockSpec(memory_space=pltpu.VMEM)],
        out_specs=hbm,
        out_shape=jax.ShapeDtypeStruct((slots, WIDTH), BF),
        scratch_shapes=[
            pltpu.VMEM((slots, channels), BF),
            pltpu.VMEM((slots, WIDTH), BF),
            pltpu.SemaphoreType.DMA((PROJECT_STEPS,)),
            pltpu.SemaphoreType.DMA((2, PROJECT_STEPS)),
        ],
        compiler_params=pltpu.CompilerParams(
            collective_id=1, has_side_effects=True, vmem_limit_bytes=VMEM_LIMIT
        ),
        name="project",
    )(feats, proj)


def unpack_kernel(
    chunk, vision, total, vis_query, vis_wq, prop_query, prop_wq, before,
    o_vision, o_feat, o_vq, o_vwq, o_vkv, o_vwo, o_w1, o_w2, o_pq, o_pwq, o_pkv, o_pwo,
    o_g1, o_b1, o_qkv, o_ao, o_g2, o_b2, o_in, o_out, o_rms, sem,
):
    core = lax.axis_index("mod")
    slots, channels = vision.shape
    start = pl.multiple_of((1 - core) * slots, 16)
    copy = pltpu.make_async_copy(vision, o_vision.at[pl.ds(start, slots)], sem)
    copy.start()

    n = total.shape[1]
    halves = [total[j, :, :chunk].reshape(n * chunk, WIDTH) for j in range(2)]
    half = R_END // 2

    def rows(start, count):
        source, at = halves[start // half], start % half
        return source[at : at + count].astype(F32)

    gsum = total[core, :, chunk:].reshape(n * (total.shape[2] - chunk), WIDTH).astype(F32)
    for j in range(channels // WIDTH):
        o_feat[WIDTH * j : WIDTH * j + WIDTH] = gsum[WIDTH * j : WIDTH * j + WIDTH].T
    for o_query, o_w, query, w, start in (
        (o_vq, o_vwq, vis_query, vis_wq, R_QV),
        (o_pq, o_pwq, prop_query, prop_wq, R_QP),
    ):
        grad = rows(start, 16).astype(BF)
        o_query[...] = nt(grad, w[...])
        o_w[...] = lax.dot_general(
            query[...], grad, (((0,), (0,)), ((), ())), preferred_element_type=F32
        )
    for o, start in ((o_vkv, R_VKV), (o_pkv, R_PKV)):
        o[:, :WIDTH] = rows(start, WIDTH)
        o[:, WIDTH:] = rows(start + WIDTH, WIDTH)
    o_vwo[...] = rows(R_SWO, WIDTH).T
    o_pwo[...] = rows(R_SWO + WIDTH, WIDTH).T
    o_w1[...] = rows(R_W1, 32)
    o_w2[...] = rows(R_W2, WIDTH)
    for j in range(3):
        o_qkv[:, WIDTH * j : WIDTH * j + WIDTH] = rows(R_Q + WIDTH * j, WIDTH)
    o_ao[...] = rows(R_AO, WIDTH)
    o_in[...] = rows(R_WIN, 512).T
    o_out[...] = rows(R_WOUT, 512)
    small = rows(R_LN, 16)
    for j, o in enumerate((o_g1, o_b1, o_g2, o_b2)):
        o[...] = small[j : j + 1]
    sums = [jnp.sum(small[R_STAT - R_LN + j : R_STAT - R_LN + j + 1], axis=1, keepdims=True) for j in range(4)]
    for j in range(3):
        o_rms[j] = jnp.sum(jnp.sqrt(sums[j] / (sums[3] * WIDTH)))
    copy.wait()


def unpack_call(chunk, vision, total, vis_query, vis_wq, prop_query, prop_wq, grad_vision):
    channels = vision.shape[1]
    shapes = [
        (channels, WIDTH), (16, WIDTH), (WIDTH, WIDTH), (WIDTH, 256), (WIDTH, WIDTH), (32, WIDTH),
        (WIDTH, WIDTH), (16, WIDTH), (WIDTH, WIDTH), (WIDTH, 256), (WIDTH, WIDTH), (1, WIDTH), (1, WIDTH),
        (WIDTH, 384), (WIDTH, WIDTH), (1, WIDTH), (1, WIDTH), (WIDTH, 512), (512, WIDTH), (3,),
    ]
    vmem, hbm = pl.BlockSpec(memory_space=pltpu.VMEM), pl.BlockSpec(memory_space=pltpu.HBM)
    return pl.pallas_call(
        functools.partial(unpack_kernel, chunk),
        in_specs=[vmem] * 6 + [hbm],
        out_specs=[hbm] + [vmem] * (len(shapes) - 1) + [pl.BlockSpec(memory_space=pltpu.SMEM)],
        out_shape=[jax.ShapeDtypeStruct(grad_vision.shape, BF)] + [jax.ShapeDtypeStruct(s, F32) for s in shapes],
        scratch_shapes=[pltpu.SemaphoreType.DMA],
        input_output_aliases={6: 0},
        compiler_params=pltpu.CompilerParams(vmem_limit_bytes=20 * 2**20),
        name="unpack",
    )(vision, total, *map(in_hbm, (vis_query, vis_wq, prop_query, prop_wq)), grad_vision)


def finish_kernel(
    n, chunk, gchunk, acc, dtok, feats, proj, total, vision,
    dother, pbuf, fbuf, dbuf, obuf, own_a, recv_a, send_b, recv_b, send_g, recv_g, reduced,
    sem_t, sem_f, sem_a, sem_b, sem_c, sem_d, sem_g,
):
    me, core = lax.axis_index("dp"), lax.axis_index("mod")
    mesh = pl.DeviceIdType.MESH
    partner = (me, 1 - core)
    half = R_END // 2
    slots, channels = fbuf.shape
    piece = slots // FEATURE_STEPS

    def remote(src, dst, send_sem, recv_sem, device):
        return pltpu.make_async_remote_copy(
            src_ref=src, dst_ref=dst, send_sem=send_sem, recv_sem=recv_sem, device_id=device, device_id_type=mesh
        )

    def rows(index, count):
        return pl.ds(pl.multiple_of(index * count, 16), count)

    barrier = pltpu.get_barrier_semaphore()
    pl.semaphore_signal(barrier, inc=1, device_id=partner, device_id_type=mesh)

    def greet(k, carry):
        pl.semaphore_signal(barrier, inc=1, device_id=(lax.rem(me + k, n), core), device_id_type=mesh)
        return carry

    lax.fori_loop(1, n, greet, 0)
    load_a = pltpu.make_async_copy(acc.at[rows(core, half)], own_a, sem_a.at[2])
    load_a.start()
    load_d = pltpu.make_async_copy(dtok, dbuf, sem_a.at[3])
    load_d.start()
    load_o = pltpu.make_async_copy(feats.at[rows(core, slots)], obuf, sem_a.at[5])
    load_o.start()
    load_p = pltpu.make_async_copy(proj, pbuf, sem_a.at[4])
    load_p.start()
    tokens, features = [], []
    for j in range(FEATURE_STEPS):
        part = pl.ds(piece * j, piece)
        start_row = pl.multiple_of((1 - core) * slots + piece * j, 16)
        features.append(pltpu.make_async_copy(feats.at[pl.ds(start_row, piece)], fbuf.at[part], sem_f.at[j]))
        features[j].start()
    pl.semaphore_wait(barrier, n)

    copy_a = remote(acc.at[rows(1 - core, half)], recv_a, sem_a.at[0], sem_a.at[1], partner)
    copy_a.start()
    for j in range(FEATURE_STEPS):
        part = pl.ds(piece * j, piece)
        tokens.append(remote(dtok.at[part], dother.at[part], sem_t.at[0, j], sem_t.at[1, j], partner))
        tokens[j].start()
    if half < n * chunk:
        send_b[half:] = jnp.zeros((n * chunk - half, WIDTH), BF)
    load_a.wait()
    copy_a.wait()
    send_b[:half] = (own_a[...].astype(F32) + recv_a[...].astype(F32)).astype(BF)

    def scatter(k):
        peer = lax.rem(me + k, n)
        return remote(
            send_b.at[rows(peer, chunk)], recv_b.at[k - 1], sem_b.at[0, k - 1], sem_b.at[1, k - 1], (peer, core)
        )

    def scatter_g(k):
        peer = lax.rem(me + k, n)
        return remote(
            send_g.at[rows(peer, gchunk)], recv_g.at[k - 1], sem_g.at[0, k - 1], sem_g.at[1, k - 1], (peer, core)
        )

    def gather(k):
        peer = lax.rem(me + k, n)
        return remote(reduced, total.at[core, me], sem_c.at[0, k - 1], sem_c.at[1, k - 1], (peer, core))

    def forward(k):
        piece_k = total.at[core, lax.rem(me + n - k, n), pl.ds(0, chunk)]
        return remote(piece_k, piece_k, sem_d.at[0, k], sem_d.at[1, k], partner)

    def each(first, step):
        def body(k, carry):
            step(k)
            return carry

        lax.fori_loop(first, n, body, 0)

    each(1, lambda k: scatter(k).start())

    load_d.wait()
    load_o.wait()
    grad = jnp.zeros((WIDTH, channels), F32)
    for j in range(FEATURE_STEPS):
        part = slice(piece * j, piece * j + piece)
        grad = grad + nn(dbuf[part].T, obuf[part])
    for j in range(FEATURE_STEPS):
        tokens[j].wait()
        features[j].wait()
        part = slice(piece * j, piece * j + piece)
        grad = grad + nn(dother[part].T, fbuf[part])
    used = WIDTH * (channels // WIDTH)
    for j in range(channels // WIDTH):
        send_g[WIDTH * j : WIDTH * j + WIDTH] = grad[:, WIDTH * j : WIDTH * j + WIDTH].astype(BF)
    if used < n * gchunk:
        send_g[used:] = jnp.zeros((n * gchunk - used, WIDTH), BF)
    each(1, lambda k: scatter_g(k).start())
    load_p.wait()
    for j in range(FEATURE_STEPS):
        part = slice(piece * j, piece * j + piece)
        vision[part] = nt(dother[part], pbuf[...]).astype(BF)

    def add(k, value):
        scatter(k).wait()
        return value + recv_b[k - 1].astype(F32)

    def add_g(k, value):
        scatter_g(k).wait()
        return value + recv_g[k - 1].astype(F32)

    reduced[:chunk] = lax.fori_loop(1, n, add, send_b[rows(me, chunk)].astype(F32)).astype(BF)
    reduced[chunk:] = lax.fori_loop(1, n, add_g, send_g[rows(me, gchunk)].astype(F32)).astype(BF)
    each(1, lambda k: gather(k).start())
    total[core, me] = reduced[...]
    forward(0).start()

    def pass_on(k):
        gather(k).wait()
        forward(k).start()

    each(1, pass_on)
    each(0, lambda k: forward(k).wait())


def in_hbm(value):
    return pltpu.with_memory_space_constraint(value, pltpu.HBM)


def finish_call(acc, dtok, feats, proj, n):
    slots, channels = dtok.shape[0], feats.shape[1]
    half = R_END // 2
    chunk = 16 * -(-half // (16 * n))
    gchunk = 16 * -(-channels // (16 * n))
    vmem = pl.BlockSpec(memory_space=pltpu.VMEM)
    hbm = pl.BlockSpec(memory_space=pltpu.HBM)
    dma = pltpu.SemaphoreType.DMA
    total, vision = pl.pallas_call(
        functools.partial(finish_kernel, n, chunk, gchunk),
        out_shape=(
            jax.ShapeDtypeStruct((2, n, chunk + gchunk, WIDTH), BF),
            jax.ShapeDtypeStruct((slots, channels), BF),
        ),
        in_specs=[hbm] * 4,
        out_specs=(vmem, vmem),
        scratch_shapes=[
            pltpu.VMEM(dtok.shape, BF),
            pltpu.VMEM(proj.shape, BF),
            pltpu.VMEM((slots, channels), BF),
            pltpu.VMEM(dtok.shape, BF),
            pltpu.VMEM((slots, channels), BF),
            pltpu.VMEM((half, WIDTH), BF),
            pltpu.VMEM((half, WIDTH), BF),
            pltpu.VMEM((n * chunk, WIDTH), BF),
            pltpu.VMEM((n - 1, chunk, WIDTH), BF),
            pltpu.VMEM((n * gchunk, WIDTH), BF),
            pltpu.VMEM((n - 1, gchunk, WIDTH), BF),
            pltpu.VMEM((chunk + gchunk, WIDTH), BF),
            dma((2, FEATURE_STEPS)),
            dma((FEATURE_STEPS,)),
            dma((6,)),
            dma((2, n - 1)),
            dma((2, n - 1)),
            dma((2, n)),
            dma((2, n - 1)),
        ],
        compiler_params=pltpu.CompilerParams(
            collective_id=0, has_side_effects=True, vmem_limit_bytes=36 * 2**20
        ),
        name="finish",
    )(*map(in_hbm, (acc, dtok, feats, proj)))
    return chunk, total, vision


def per_device(
    vision_feats, vision_grid, proprio, proprio_mask, token_valid, mix_weight, out_cot, feat_proj,
    vis_query, vis_wq, vis_kv, vis_wo, prop_w1, prop_w2, prop_query, prop_wq, prop_kv, prop_wo,
    ln1_gain, ln1_bias, qkv_weight, attn_out, ln2_gain, ln2_bias, mlp_in, mlp_out,
):
    me = lax.axis_index("mod").astype(jnp.int32)
    own = me.reshape(1)
    feats = vision_feats.reshape(-1, vision_feats.shape[3])
    received = project_call(feats, feat_proj)
    weights = (
        vis_query, vis_wq, vis_kv, vis_wo, prop_w1, prop_w2, prop_query, prop_wq, prop_kv, prop_wo,
        *(v.reshape(1, -1) for v in (ln1_gain, ln1_bias, ln2_gain, ln2_bias)), qkv_weight, attn_out, mlp_in, mlp_out,
    )
    frames = jnp.transpose(proprio, (1, 2, 3, 0)).reshape(-1, proprio.shape[0])
    frame_mask = jnp.transpose(proprio_mask, (1, 2, 0)).reshape(-1, proprio_mask.shape[0])
    grid_sizes = jnp.transpose(vision_grid, (1, 2, 0)).reshape(4, -1)
    output, grad_vision, dtok, dframes, acc = block_call(
        own, grid_sizes, feats, received, frames, frame_mask, token_valid, mix_weight.reshape(1, -1),
        out_cot.reshape(-1, WIDTH), feat_proj, weights,
    )
    chunk, total, vision = finish_call(acc, dtok, feats, feat_proj, lax.axis_size("dp"))
    grad_vision, *outs = unpack_call(
        chunk, vision, total, vis_query, vis_wq, prop_query, prop_wq, grad_vision
    )
    vectors = {11, 12, 15, 16}
    outs = [o.reshape(WIDTH) if j in vectors else o for j, o in enumerate(outs)]
    return (
        output.reshape(out_cot.shape),
        grad_vision.reshape(vision_feats.shape),
        jnp.transpose(dframes.reshape(proprio.shape[1:] + proprio.shape[:1]), (3, 0, 1, 2)),
        *outs,
    )


def solution(mesh):
    both = ("dp", "mod")
    return jax.shard_map(
        per_device,
        mesh=mesh,
        in_specs=(
            P("dp", None, None, "mod"),
            P(both, None, None),
            P(both, None, None, None),
            P(both, None, None),
            P(both, None),
            P(both),
            P(both, None, None),
            P("mod", None),
        ) + (P(),) * 18,
        out_specs=(
            P(both, None, None),
            P("dp", None, None, "mod"),
            P(both, None, None, None),
            P("mod", None),
        ) + (P(),) * 19,
        check_vma=False,
    )
```

```python
import functools
import math

import jax
import jax.numpy as jnp
from jax import lax
from jax.experimental import pallas as pl
from jax.experimental.pallas import tpu as pltpu
from jax.sharding import PartitionSpec as P

HEADS = 8
HEAD = 16
WIDTH = 128
PROP = 32
NEG = -1e30
BF = jnp.bfloat16
F32 = jnp.float32
VMEM_LIMIT = 60 * 2**20
CHAINS = 8
FF_PART = 256

R_WIN, R_WOUT, R_Q, R_KV, R_AO = 0, 512, 1024, 1152, 1408
R_SWO, R_VKV, R_PKV, R_W2, R_W1 = 1536, 1792, 2048, 2304, 2432
R_QV, R_QP, R_LN, R_STAT, R_END = 2464, 2480, 2496, 2500, 2560


def nn(a, b):
    return lax.dot_general(a, b, (((1,), (0,)), ((), ())), preferred_element_type=F32)


def nt(a, b):
    return lax.dot_general(a, b, (((1,), (1,)), ((), ())), preferred_element_type=F32)


def cat(items, axis):
    return jnp.concatenate(items, axis=axis)


def lane_iota(rows, lanes):
    return lax.broadcasted_iota(jnp.int32, (rows, lanes), 1)


def tile_to(mask, rows, lanes):
    return cat([cat([mask] * (rows // mask.shape[0]), 0)] * (lanes // mask.shape[1]), 1)


def head_expand(value, masks):
    return cat([value * tile_to(mask, *value.shape) for mask in masks], 0)


def head_select(full, heads, period):
    rows, lanes = full.shape[0] // heads, full.shape[1]
    head = (lane_iota(rows, lanes) & (period - 1)) >> 4
    out = full[:rows]
    for h in range(1, heads):
        out = jnp.where(head == h, full[h * rows : (h + 1) * rows], out)
    return out


def turn(value):
    out = []
    for j in range(0, value.shape[1], WIDTH):
        out += [value[:, j + 64 : j + 128], value[:, j : j + 64]]
    return cat(out, 1)


def diagonal(blocks):
    out = []
    for j, block in enumerate(blocks):
        row = [block if k == j else jnp.zeros((block.shape[0], other.shape[1]), BF) for k, other in enumerate(blocks)]
        out.append(cat(row, 1))
    return cat(out, 0)


def pair_up(parts):
    return cat([cat(parts[j : j + 2], 1) for j in range(0, 8, 2)], 0)


def unpair(value, rows):
    out = []
    for j in range(4):
        part = value[rows * j : rows * j + rows]
        out += [part[:, :WIDTH], part[:, WIDTH:]]
    return cat(out, 0)


def softmax_rows(scores):
    peak = jnp.max(scores, axis=1, keepdims=True)
    weights = jnp.exp(scores - peak)
    return weights * (1.0 / jnp.sum(weights, axis=1, keepdims=True))


def softmax_grad(weights, grad):
    return weights * (grad - jnp.sum(weights * grad, axis=1, keepdims=True))


def mean_rows(value):
    return jnp.sum(value, axis=0, keepdims=True) * (1.0 / value.shape[0])


def norm_rows(value):
    centered = value - mean_rows(value)
    scale = lax.rsqrt(mean_rows(centered * centered) + 1e-05)
    return centered * scale, scale


def norm_rows_grad(grad, hat, scale):
    return scale * (grad - mean_rows(grad) - hat * mean_rows(grad * hat))


def split_samples(value, low_half, high_half):
    out = []
    for s in range(4):
        half = tile_to(high_half if s % 2 else low_half, 64, WIDTH)
        block = value[:, WIDTH * (s // 2) : WIDTH * (s // 2) + WIDTH] * half
        zero = jnp.zeros((64, WIDTH), BF)
        out.append(cat([block, zero] if s < 2 else [zero, block], 1))
    return cat(out, 0)


def gather_heads(value, turned, group, low_half, high_half):
    low_tall, high_tall = tile_to(low_half, 64, WIDTH), tile_to(high_half, 64, WIDTH)
    out = []
    for s in (0, 2):
        even, odd = slice(64 * s, 64 * s + 64), slice(64 * s + 64, 64 * s + 128)
        left, right = (value[even], turned[odd]) if group == 0 else (turned[even], value[odd])
        out.append(left * low_tall + right * high_tall)
    return cat(out, 1)


def scatter_heads(parts, low_half, high_half):
    low_tall, high_tall = tile_to(low_half, 64, WIDTH), tile_to(high_half, 64, WIDTH)
    turned = [turn(part) for part in parts]
    out = []
    for s in range(4):
        lanes = slice(WIDTH * (s // 2), WIDTH * (s // 2) + WIDTH)
        left = (turned if s % 2 else parts)[0][:, lanes]
        right = (parts if s % 2 else turned)[1][:, lanes]
        out.append(left * low_tall + right * high_tall)
    return cat(out, 0)


def spread_keys(value, turned, group, low_half, high_half):
    zero = jnp.zeros((HEAD, WIDTH), BF)
    rows = []
    for s in range(4):
        lanes = slice(WIDTH * (s // 2), WIDTH * (s // 2) + WIDTH)
        for local in range(4):
            h = group * 4 + local
            source = value if s % 2 == local % 2 else turned
            block = source[h * HEAD : (h + 1) * HEAD, lanes] * (high_half if local % 2 else low_half)
            rows.append(cat([block, zero] if local < 2 else [zero, block], 1))
    return cat(rows, 0)


def mix_keys(value, weights, low_half, high_half, first):
    turned = turn(value)
    out = []
    for group in range(2):
        full = nn(spread_keys(value, turned, group, low_half, high_half), weights[group])
        left = jnp.where(first, full[:64, :WIDTH], full[64:128, :WIDTH])
        right = jnp.where(first, full[128:192, WIDTH:], full[192:, WIDTH:])
        out.append(cat([left, right], 1))
    return cat(out, 0)


def stem_queries(query, w_query, masks):
    value = nn(query, w_query).astype(BF)
    return head_expand(value * jnp.asarray(0.25, BF), masks)


def block_kernel(
    half, grid_ref, feats, pr, frames, frame_mask, token_valid, mix_weight, cot, proj,
    vis_query, vis_wq, vis_kv, vis_wo, prop_w1, prop_w2, prop_query, prop_wq, prop_kv, prop_wo,
    ln1_gain, ln1_bias, ln2_gain, ln2_bias, qkv_w, attn_out, mlp_in, mlp_out,
    out, grad_feats, dtok_ref, dframes, acc_out,
    masks_ref, qv_ref, qp_ref, wqkv_t, ao_t, win_t, wout_t, stem_t, ln_ref,
    gv_ref, gp_ref, lnacc, stat, acc, fr_ref, df_ref, aux_ref, turn_ref,
):
    blocks = token_valid.shape[0] // 4
    step = pl.program_id(0)

    @pl.when(step == 0)
    def _():
        lane = lane_iota(16, WIDTH) >> 4
        for h in range(HEADS):
            masks_ref[h] = jnp.where(lane == h, 1.0, 0.0).astype(BF)
        for h in range(4):
            masks_ref[HEADS + h] = jnp.where((lane & 3) == h, 1.0, 0.0).astype(BF)
        masks = [masks_ref[h] for h in range(HEADS)]
        qv_ref[...] = diagonal([stem_queries(vis_query[...], vis_wq[...], masks)] * 2)
        qp_ref[...] = diagonal([stem_queries(prop_query[...], prop_wq[...], masks)] * 2)
        wqkv_t[...] = qkv_w[...].T
        ao_t[...] = attn_out[...].T
        win_t[...] = mlp_in[...].T
        wout_t[...] = mlp_out[...].T
        stem_t[:, :WIDTH] = vis_wo[...].T
        stem_t[:, WIDTH:] = prop_wo[...].T
        for j, vector in enumerate((ln1_gain, ln1_bias, ln2_gain, ln2_bias)):
            ln_ref[j] = jnp.broadcast_to(vector[...].astype(F32), (WIDTH, WIDTH)).T

        def by_block(ref):
            return cat([ref[pl.ds(j, blocks, stride=4)].astype(F32) for j in range(4)], 1)

        valid = by_block(token_valid)
        turn_ref[...] = jnp.broadcast_to(mix_weight[...].astype(F32), turn_ref.shape).T
        mix = by_block(turn_ref)
        turn_ref[:, : frame_mask.shape[0]] = frame_mask[...].astype(F32).T
        frame_keep = cat([turn_ref[pl.ds(j, blocks, stride=4)][:, : frame_mask.shape[0]] for j in range(4)], 1)
        values = (valid, mix, jnp.where(valid > 0, 0.0, NEG), jnp.where(cat([frame_keep] * 2, 1) > 0, 0.0, NEG))
        for i in range(blocks):
            for j, value in enumerate(values):
                aux_ref[i, j : j + 1] = value[i : i + 1]

        for j in range(frames.shape[0] // PROP):
            block = frames[PROP * j : PROP * j + PROP].astype(F32).T
            fr_ref[pl.ds(j, block.shape[0], stride=frames.shape[0] // PROP)] = block
        acc[...] = jnp.zeros_like(acc)
        gv_ref[...] = jnp.zeros_like(gv_ref)
        gp_ref[...] = jnp.zeros_like(gp_ref)
        lnacc[...] = jnp.zeros_like(lnacc)
        stat[...] = jnp.zeros_like(stat)

    masks = [masks_ref[h] for h in range(HEADS)]
    masks_group = [masks_ref[HEADS + h] for h in range(4)]
    qv, qp = qv_ref[...], qp_ref[...]
    lane = lane_iota(HEAD, WIDTH)
    low_half = jnp.where(lane < 64, 1.0, 0.0).astype(BF)
    high_half = jnp.where(lane < 64, 0.0, 1.0).astype(BF)
    first = lane_iota(64, WIDTH) < 64


    def chain(g):
        block = step * CHAINS + g
        slots = slice(512 * g, 512 * g + 512)
        kept = nn(feats[slots], proj[...]).astype(BF)
        tok = (kept.astype(F32) + pr[slots].astype(F32)).astype(BF)
        vkv = nn(tok, vis_kv[...]).astype(BF)
        vk, vv = vkv[:, :WIDTH], vkv[:, WIDTH:]
        slot = lax.broadcasted_iota(jnp.int32, (64, WIDTH), 0)
        slot_row, slot_col = slot >> 3, slot & 7
        bias = []
        for st in range(8):
            s, t = (step * CHAINS + g) * 4 + st // 2, st % 2
            keep = (slot_row < grid_ref[2 * t, s]) & (slot_col < grid_ref[2 * t + 1, s])
            bias.append(jnp.where(keep, 0.0, NEG))
        bias = pair_up(bias).reshape(4, 64, 256)
        vk2 = pair_up([vk[64 * st : 64 * st + 64] for st in range(8)])
        vv2 = pair_up([vv[64 * st : 64 * st + 64] for st in range(8)])
        yield
        vp = softmax_rows(nt(vk2, qv).reshape(4, 64, 256) + bias)
        vpb = vp.reshape(256, 256).astype(BF)
        yield
        vpt = vpb.T
        vmixed = [None] * 8
        for e in range(2):
            for m in range(2):
                one, two = 4 * m + e, 4 * m + 2 + e
                spread = diagonal([vv[64 * one : 64 * one + 64], vv[64 * two : 64 * two + 64]])
                lhs = vpt[WIDTH * e : WIDTH * e + WIDTH, WIDTH * m : WIDTH * m + WIDTH]
                both = head_select(nn(lhs, spread), HEADS, WIDTH).astype(BF)
                vmixed[one], vmixed[two] = both[:, :WIDTH], both[:, WIDTH:]

        yield
        fr_rows = pl.ds(pl.multiple_of((step * CHAINS + g) * 128, 128), 128)
        fr = fr_ref[fr_rows].astype(BF)
        pre = nn(fr, prop_w1[...])
        gate = jax.nn.sigmoid(pre)
        hidden = (pre * gate).astype(BF)
        ptok = nn(hidden, prop_w2[...]).astype(BF)
        pkv = nn(ptok, prop_kv[...]).astype(BF)
        pk, pv = pkv[:, :WIDTH], pkv[:, WIDTH:]
        column = jnp.broadcast_to(aux_ref[block, 3:4, :WIDTH], (WIDTH, WIDTH)).T
        parts = lambda v: [v[HEAD * st : HEAD * st + HEAD] for st in range(8)]
        pbias = pair_up(parts(column))
        pk2, pv2 = pair_up(parts(pk)), pair_up(parts(pv))
        yield
        pp = softmax_rows((nt(pk2, qp) + pbias).reshape(4, HEAD, 256))
        ppb = pp.reshape(64, 256).astype(BF)
        ppt = ppb.T
        pmixed = [None] * 8
        for e in range(2):
            spread = diagonal([pv[HEAD * st : HEAD * st + HEAD] for st in range(e, 8, 2)])
            both = head_select(nn(ppt[WIDTH * e : WIDTH * e + WIDTH], spread), HEADS, WIDTH).astype(BF)
            for j in range(4):
                pmixed[2 * j + e] = both[:, WIDTH * j : WIDTH * j + WIDTH]

        yield
        zero16 = jnp.zeros((HEAD, WIDTH), BF)
        rows = []
        for st in range(8):
            rows.append(cat([vmixed[st], zero16], 1))
            rows.append(cat([zero16, pmixed[st]], 1))
        mixed_ext = cat(rows, 0)
        x = nt(stem_t[...], mixed_ext)
        g1, b1, g2, b2 = [cat([ln_ref[j]] * 2, 1) for j in range(4)]
        hat1, scale1 = norm_rows(x)
        n1 = (hat1 * g1 + b1).astype(BF)
        yield
        qkv = nn(wqkv_t[...], n1).astype(BF)
        qt, kt, vt = qkv[:WIDTH] * jnp.asarray(0.25, BF), qkv[WIDTH : 2 * WIDTH], qkv[2 * WIDTH :]
        kn, vn = kt.T, vt.T
        kn_turned, vn_turned = turn(kn), turn(vn)
        yield
        weights, weights_b, query_bd = [], [], []
        tbias = []
        for p in range(2):
            column = jnp.broadcast_to(aux_ref[block, 2:3, 128 * p : 128 * p + 128], (WIDTH, WIDTH)).T
            tbias.append(jnp.where(first, column[:64], column[64:]))
        tbias = cat(tbias, 1)[None]
        for group in range(2):
            part = slice(64 * group, 64 * group + 64)
            qbd = split_samples(qt[part], low_half, high_half)
            keys = head_expand(gather_heads(kn, kn_turned, group, low_half, high_half), masks_group)
            scores = nn(keys, qbd).reshape(4, 64, 256) + tbias
            yield
            w = softmax_rows(scores)
            weights.append(w)
            weights_b.append(w.reshape(256, 256).astype(BF))
            query_bd.append(qbd)
            yield
        mixed = mix_keys(vt, weights_b, low_half, high_half, first).astype(BF)
        yield
        branch = nn(ao_t[...], mixed)
        middle = x + branch
        hat2, scale2 = norm_rows(middle)
        n2 = (hat2 * g2 + b2).astype(BF)
        yield
        c = math.sqrt(2.0 / math.pi)
        seed = cot[256 * g : 256 * g + 256].T.astype(F32) * aux_ref[block, 1:2, :]
        dmlp = seed.astype(BF)
        mlp, dn2, act_all, dup_all = 0.0, 0.0, [], []
        for j in range(512 // FF_PART):
            part = slice(FF_PART * j, FF_PART * j + FF_PART)
            up = nn(win_t[part], n2)
            yield
            square = up * up
            h = 0.5 + 0.5 * jnp.tanh(up * (c + (c * 0.044715) * square))
            act = up * h
            slope = h + act * (1.0 - h) * (2 * c + (6 * c * 0.044715) * square)
            act_b = act.astype(BF)
            mlp = mlp + nn(wout_t[:, part], act_b)
            dup = (nn(mlp_out[part], dmlp) * slope).astype(BF)
            yield
            dn2 = dn2 + nn(mlp_in[:, part], dup)
            acc[R_WOUT + FF_PART * j : R_WOUT + FF_PART * j + FF_PART] += nt(act_b, dmlp)
            acc[R_WIN + FF_PART * j : R_WIN + FF_PART * j + FF_PART] += nt(dup, n2)
            yield
        final = middle + mlp
        out[256 * g : 256 * g + 256] = final.astype(BF).T
        valid = aux_ref[block, 0:1, :]
        for j, value in enumerate((final, branch, mlp)):
            stat[j : j + 1, :] += jnp.sum(value * value, axis=0, keepdims=True) * valid
        stat[3:4, :] += valid

        yield
        fold = lambda v: v[:, :WIDTH] + v[:, WIDTH:]
        lnacc[2] += fold(dn2 * hat2)
        lnacc[3] += fold(dn2)
        dmid = seed + norm_rows_grad(dn2 * g2, hat2, scale2)
        dbranch = dmid.astype(BF)
        acc[R_AO : R_AO + WIDTH] += nt(mixed, dbranch)
        yield
        dmixed = nn(attn_out[...], dbranch).astype(BF)
        yield
        ds_all, dk, dv = [], [], []
        for group in range(2):
            part = slice(64 * group, 64 * group + 64)
            dbd = split_samples(dmixed[part], low_half, high_half)
            values = head_expand(gather_heads(vn, vn_turned, group, low_half, high_half), masks_group)
            dw = nn(values, dbd).reshape(4, 64, 256)
            yield
            ds = softmax_grad(weights[group], dw).reshape(256, 256).astype(BF)
            dv.append(head_select(nt(weights_b[group], dbd), 4, 64).astype(BF))
            dk.append(head_select(nt(ds, query_bd[group]), 4, 64).astype(BF))
            ds_all.append(ds)
        dq = (mix_keys(kt, ds_all, low_half, high_half, first) * 0.25).astype(BF)
        dkv = cat([scatter_heads(dk, low_half, high_half), scatter_heads(dv, low_half, high_half)], 1)
        yield
        acc[R_Q : R_Q + WIDTH] += nt(n1, dq)
        grad = nn(n1, dkv)
        acc[R_KV : R_KV + WIDTH] += grad[:, :WIDTH]
        acc[R_KV + WIDTH : R_KV + 2 * WIDTH] += grad[:, WIDTH:]
        dn1 = nn(qkv_w[:, :WIDTH], dq) + nt(qkv_w[:, WIDTH:], dkv)
        lnacc[0] += fold(dn1 * hat1)
        lnacc[1] += fold(dn1)
        dx = (dmid + norm_rows_grad(dn1 * g1, hat1, scale1)).astype(BF)

        yield
        grad = nn(dx, mixed_ext)
        acc[R_SWO : R_SWO + WIDTH] += grad[:, :WIDTH]
        acc[R_SWO + WIDTH : R_SWO + 2 * WIDTH] += grad[:, WIDTH:]
        dstem = nn(dx.T, stem_t[...]).astype(BF)
        dw, dv, pdw, pdv = [], [], [], []
        for st in range(8):
            j, e, r = st // 2, st % 2, 32 * st
            tall, short, lanes = slice(64 * j, 64 * j + 64), slice(HEAD * j, HEAD * j + HEAD), slice(WIDTH * e, WIDTH * e + WIDTH)
            spread = head_expand(cat([dstem[r : r + 16, :WIDTH], dstem[r + 16 : r + 32, WIDTH:]], 1), masks)
            full = nt(diagonal([vv2[tall, lanes], pv2[short, lanes]]), spread)
            dw.append(full[:64])
            pdw.append(full[64:])
            full = nn(
                diagonal([vpb[tall, lanes], ppb[short, lanes]]), cat([spread[:, :WIDTH], spread[:, WIDTH:]], 0)
            ).astype(BF)
            dv.append(full[:64])
            pdv.append(full[64:])
        yield
        ds = softmax_grad(vp, pair_up(dw).reshape(4, 64, 256)).reshape(256, 256).astype(BF)
        dkv = cat([unpair(nn(ds, qv).astype(BF), 64), cat(dv, 0)], 1)
        dtok = nt(dkv, vis_kv[...]).astype(BF)
        dtok_ref[slots] = dtok
        grad_feats[slots] = nt(dtok, proj[...]).astype(BF)
        grad = nn(tok.T, dkv)
        acc[R_VKV : R_VKV + WIDTH] += grad[:, :WIDTH]
        acc[R_VKV + WIDTH : R_VKV + 2 * WIDTH] += grad[:, WIDTH:]
        full = nn(ds.T, vk2)
        gv_ref[...] += full[:WIDTH, :WIDTH] + full[WIDTH:, WIDTH:]

        yield
        ds = softmax_grad(pp, pair_up(pdw).reshape(4, HEAD, 256)).reshape(64, 256).astype(BF)
        dkv = cat([unpair(nn(ds, qp).astype(BF), HEAD), cat(pdv, 0)], 1)
        dptok = nt(dkv, prop_kv[...]).astype(BF)
        grad = nn(ptok.T, dkv)
        acc[R_PKV : R_PKV + WIDTH] += grad[:, :WIDTH]
        acc[R_PKV + WIDTH : R_PKV + 2 * WIDTH] += grad[:, WIDTH:]
        full = nn(ds.T, pk2)
        gp_ref[...] += full[:WIDTH, :WIDTH] + full[WIDTH:, WIDTH:]
        yield
        acc[R_W2 : R_W2 + WIDTH] += nn(hidden.T, dptok)
        dhidden = nt(dptok, prop_w2[...])
        dpre = (dhidden * (gate * (1.0 + pre * (1.0 - gate)))).astype(BF)
        acc[R_W1 : R_W1 + 32] += nn(fr.T, dpre)
        df_ref[fr_rows] = nt(dpre, prop_w1[...])

        yield

    live = [(g // 2 * 5, chain(g)) for g in range(CHAINS)]
    tick = 0
    while live:
        for one in list(live):
            if tick >= one[0] and next(one[1], live) is live:
                live.remove(one)
        tick += 1

    @pl.when(step == pl.num_programs(0) - 1)
    def _():
        acc[R_QV : R_QV + 16] = head_select(gv_ref[...], HEADS, WIDTH) * 0.25
        acc[R_QP : R_QP + 16] = head_select(gp_ref[...], HEADS, WIDTH) * 0.25
        for j in range(4):
            acc[R_LN + j : R_LN + j + 1] = jnp.sum(lnacc[j].T, axis=0, keepdims=True)
            acc[R_STAT + j : R_STAT + j + 1] = stat[j : j + 1, :WIDTH] + stat[j : j + 1, WIDTH:]
        acc_out[...] = acc[...].astype(BF)
        for j in range(frames.shape[0] // PROP):
            block = df_ref[pl.ds(j, frames.shape[1], stride=frames.shape[0] // PROP)]
            dframes[PROP * j : PROP * j + PROP] = block.T.astype(BF)


def whole(shape):
    return pl.BlockSpec(shape, lambda i, *_: (0,) * len(shape))


def block_call(half, grid_sizes, feats, received, frames, frame_mask, token_valid, mix_weight, cot, proj, weights):
    samples, seq = token_valid.shape
    steps = samples // (4 * CHAINS)
    channels = feats.shape[1]
    row = lambda i, *_: (i, 0)
    own = lambda i, half, _: (half[0] * steps + i, 0)
    in_specs = [
        pl.BlockSpec((512 * CHAINS, channels), own),
        pl.BlockSpec((512 * CHAINS, WIDTH), row),
        whole(frames.shape),
        whole(frame_mask.shape),
        whole(token_valid.shape),
        whole(mix_weight.shape),
        pl.BlockSpec((256 * CHAINS, WIDTH), row),
        whole(proj.shape),
    ] + [whole(w.shape) for w in weights]
    out_shape = (
        jax.ShapeDtypeStruct((256 * CHAINS * steps, WIDTH), BF),
        jax.ShapeDtypeStruct(feats.shape, BF),
        jax.ShapeDtypeStruct((512 * CHAINS * steps, WIDTH), BF),
        jax.ShapeDtypeStruct(frames.shape, BF),
        jax.ShapeDtypeStruct((R_END, WIDTH), BF),
    )
    out_specs = (
        pl.BlockSpec((256 * CHAINS, WIDTH), row),
        pl.BlockSpec((512 * CHAINS, channels), own),
        pl.BlockSpec((512 * CHAINS, WIDTH), row),
        whole(frames.shape),
        whole((R_END, WIDTH)),
    )
    scratch = [
        pltpu.VMEM((12, 16, WIDTH), BF),
        pltpu.VMEM((256, 256), BF),
        pltpu.VMEM((256, 256), BF),
        pltpu.VMEM((384, WIDTH), BF),
        pltpu.VMEM((128, WIDTH), BF),
        pltpu.VMEM((512, WIDTH), BF),
        pltpu.VMEM((128, 512), BF),
        pltpu.VMEM((128, 256), BF),
        pltpu.VMEM((4, WIDTH, WIDTH), F32),
        pltpu.VMEM((WIDTH, WIDTH), F32),
        pltpu.VMEM((WIDTH, WIDTH), F32),
        pltpu.VMEM((4, WIDTH, WIDTH), F32),
        pltpu.VMEM((8, 256), F32),
        pltpu.VMEM((R_END, WIDTH), F32),
        pltpu.VMEM((frames.shape[0] // PROP * frames.shape[1], PROP), F32),
        pltpu.VMEM((frames.shape[0] // PROP * frames.shape[1], PROP), F32),
        pltpu.VMEM((samples // 4, 8, 4 * seq), F32),
        pltpu.VMEM((samples, seq), F32),
    ]
    return pl.pallas_call(
        block_kernel,
        grid_spec=pltpu.PrefetchScalarGridSpec(
            num_scalar_prefetch=2,
            grid=(steps,),
            in_specs=in_specs,
            out_specs=out_specs,
            scratch_shapes=scratch,
        ),
        out_shape=out_shape,
        compiler_params=pltpu.CompilerParams(vmem_limit_bytes=VMEM_LIMIT),
        name="stems_trunk",
    )(half, grid_sizes, feats, received, frames, frame_mask, token_valid, mix_weight, cot, proj, *weights)

PROJECT_STEPS = 8
FEATURE_STEPS = 4


def project_kernel(feats, proj, out, fbuf, stage, sem_f, sem_s):
    me, core = lax.axis_index("dp"), lax.axis_index("mod")
    mesh = pl.DeviceIdType.MESH
    partner = (me, 1 - core)
    slots = fbuf.shape[0]
    piece = slots // PROJECT_STEPS
    loads, sends = [], []
    for j in range(PROJECT_STEPS):
        start = pl.multiple_of((1 - core) * slots + piece * j, 16)
        loads.append(pltpu.make_async_copy(feats.at[pl.ds(start, piece)], fbuf.at[pl.ds(piece * j, piece)], sem_f.at[j]))
        loads[j].start()
    barrier = pltpu.get_barrier_semaphore()
    pl.semaphore_signal(barrier, inc=1, device_id=partner, device_id_type=mesh)
    pl.semaphore_wait(barrier, 1)
    for j in range(PROJECT_STEPS):
        part = pl.ds(piece * j, piece)
        loads[j].wait()
        stage[part] = nn(fbuf[part], proj[...]).astype(BF)
        sends.append(
            pltpu.make_async_remote_copy(
                src_ref=stage.at[part], dst_ref=out.at[part], send_sem=sem_s.at[0, j], recv_sem=sem_s.at[1, j],
                device_id=partner, device_id_type=mesh,
            )
        )
        sends[j].start()
    for j in range(PROJECT_STEPS):
        sends[j].wait()


def project_call(feats, proj):
    slots, channels = feats.shape[0] // 2, feats.shape[1]
    hbm = pl.BlockSpec(memory_space=pl.ANY)
    return pl.pallas_call(
        project_kernel,
        in_specs=[hbm, pl.BlockSpec(memory_space=pltpu.VMEM)],
        out_specs=hbm,
        out_shape=jax.ShapeDtypeStruct((slots, WIDTH), BF),
        scratch_shapes=[
            pltpu.VMEM((slots, channels), BF),
            pltpu.VMEM((slots, WIDTH), BF),
            pltpu.SemaphoreType.DMA((PROJECT_STEPS,)),
            pltpu.SemaphoreType.DMA((2, PROJECT_STEPS)),
        ],
        compiler_params=pltpu.CompilerParams(
            collective_id=1, has_side_effects=True, vmem_limit_bytes=VMEM_LIMIT
        ),
        name="project",
    )(feats, proj)


def unpack_kernel(
    chunk, vision, total, vis_query, vis_wq, prop_query, prop_wq, before,
    o_vision, o_feat, o_vq, o_vwq, o_vkv, o_vwo, o_w1, o_w2, o_pq, o_pwq, o_pkv, o_pwo,
    o_g1, o_b1, o_qkv, o_ao, o_g2, o_b2, o_in, o_out, o_rms, sem,
):
    core = lax.axis_index("mod")
    slots, channels = vision.shape
    start = pl.multiple_of((1 - core) * slots, 16)
    copy = pltpu.make_async_copy(vision, o_vision.at[pl.ds(start, slots)], sem)
    copy.start()

    n = total.shape[1]
    halves = [total[j, :, :chunk].reshape(n * chunk, WIDTH) for j in range(2)]
    half = R_END // 2

    def rows(start, count):
        source, at = halves[start // half], start % half
        return source[at : at + count].astype(F32)

    gsum = total[core, :, chunk:].reshape(n * (total.shape[2] - chunk), WIDTH).astype(F32)
    for j in range(channels // WIDTH):
        o_feat[WIDTH * j : WIDTH * j + WIDTH] = gsum[WIDTH * j : WIDTH * j + WIDTH].T
    for o_query, o_w, query, w, start in (
        (o_vq, o_vwq, vis_query, vis_wq, R_QV),
        (o_pq, o_pwq, prop_query, prop_wq, R_QP),
    ):
        grad = rows(start, 16).astype(BF)
        o_query[...] = nt(grad, w[...])
        o_w[...] = lax.dot_general(
            query[...], grad, (((0,), (0,)), ((), ())), preferred_element_type=F32
        )
    for o, start in ((o_vkv, R_VKV), (o_pkv, R_PKV)):
        o[:, :WIDTH] = rows(start, WIDTH)
        o[:, WIDTH:] = rows(start + WIDTH, WIDTH)
    o_vwo[...] = rows(R_SWO, WIDTH).T
    o_pwo[...] = rows(R_SWO + WIDTH, WIDTH).T
    o_w1[...] = rows(R_W1, 32)
    o_w2[...] = rows(R_W2, WIDTH)
    for j in range(3):
        o_qkv[:, WIDTH * j : WIDTH * j + WIDTH] = rows(R_Q + WIDTH * j, WIDTH)
    o_ao[...] = rows(R_AO, WIDTH)
    o_in[...] = rows(R_WIN, 512).T
    o_out[...] = rows(R_WOUT, 512)
    small = rows(R_LN, 16)
    for j, o in enumerate((o_g1, o_b1, o_g2, o_b2)):
        o[...] = small[j : j + 1]
    sums = [jnp.sum(small[R_STAT - R_LN + j : R_STAT - R_LN + j + 1], axis=1, keepdims=True) for j in range(4)]
    for j in range(3):
        o_rms[j] = jnp.sum(jnp.sqrt(sums[j] / (sums[3] * WIDTH)))
    copy.wait()


def unpack_call(chunk, vision, total, vis_query, vis_wq, prop_query, prop_wq, grad_vision):
    channels = vision.shape[1]
    shapes = [
        (channels, WIDTH), (16, WIDTH), (WIDTH, WIDTH), (WIDTH, 256), (WIDTH, WIDTH), (32, WIDTH),
        (WIDTH, WIDTH), (16, WIDTH), (WIDTH, WIDTH), (WIDTH, 256), (WIDTH, WIDTH), (1, WIDTH), (1, WIDTH),
        (WIDTH, 384), (WIDTH, WIDTH), (1, WIDTH), (1, WIDTH), (WIDTH, 512), (512, WIDTH), (3,),
    ]
    vmem, hbm = pl.BlockSpec(memory_space=pltpu.VMEM), pl.BlockSpec(memory_space=pltpu.HBM)
    return pl.pallas_call(
        functools.partial(unpack_kernel, chunk),
        in_specs=[vmem] * 6 + [hbm],
        out_specs=[hbm] + [vmem] * (len(shapes) - 1) + [pl.BlockSpec(memory_space=pltpu.SMEM)],
        out_shape=[jax.ShapeDtypeStruct(grad_vision.shape, BF)] + [jax.ShapeDtypeStruct(s, F32) for s in shapes],
        scratch_shapes=[pltpu.SemaphoreType.DMA],
        input_output_aliases={6: 0},
        compiler_params=pltpu.CompilerParams(vmem_limit_bytes=20 * 2**20),
        name="unpack",
    )(vision, total, *map(in_hbm, (vis_query, vis_wq, prop_query, prop_wq)), grad_vision)


def finish_kernel(
    n, chunk, gchunk, acc, dtok, feats, proj, total, vision,
    dother, pbuf, fbuf, dbuf, obuf, own_a, recv_a, send_b, recv_b, send_g, recv_g, reduced,
    sem_t, sem_f, sem_a, sem_b, sem_c, sem_d, sem_g,
):
    me, core = lax.axis_index("dp"), lax.axis_index("mod")
    mesh = pl.DeviceIdType.MESH
    partner = (me, 1 - core)
    half = R_END // 2
    slots, channels = fbuf.shape
    piece = slots // FEATURE_STEPS

    def remote(src, dst, send_sem, recv_sem, device):
        return pltpu.make_async_remote_copy(
            src_ref=src, dst_ref=dst, send_sem=send_sem, recv_sem=recv_sem, device_id=device, device_id_type=mesh
        )

    def rows(index, count):
        return pl.ds(pl.multiple_of(index * count, 16), count)

    barrier = pltpu.get_barrier_semaphore()
    pl.semaphore_signal(barrier, inc=1, device_id=partner, device_id_type=mesh)

    def greet(k, carry):
        pl.semaphore_signal(barrier, inc=1, device_id=(lax.rem(me + k, n), core), device_id_type=mesh)
        return carry

    lax.fori_loop(1, n, greet, 0)
    load_a = pltpu.make_async_copy(acc.at[rows(core, half)], own_a, sem_a.at[2])
    load_a.start()
    load_d = pltpu.make_async_copy(dtok, dbuf, sem_a.at[3])
    load_d.start()
    load_o = pltpu.make_async_copy(feats.at[rows(core, slots)], obuf, sem_a.at[5])
    load_o.start()
    load_p = pltpu.make_async_copy(proj, pbuf, sem_a.at[4])
    load_p.start()
    tokens, features = [], []
    for j in range(FEATURE_STEPS):
        part = pl.ds(piece * j, piece)
        start_row = pl.multiple_of((1 - core) * slots + piece * j, 16)
        features.append(pltpu.make_async_copy(feats.at[pl.ds(start_row, piece)], fbuf.at[part], sem_f.at[j]))
        features[j].start()
    pl.semaphore_wait(barrier, n)

    copy_a = remote(acc.at[rows(1 - core, half)], recv_a, sem_a.at[0], sem_a.at[1], partner)
    copy_a.start()
    for j in range(FEATURE_STEPS):
        part = pl.ds(piece * j, piece)
        tokens.append(remote(dtok.at[part], dother.at[part], sem_t.at[0, j], sem_t.at[1, j], partner))
        tokens[j].start()
    if half < n * chunk:
        send_b[half:] = jnp.zeros((n * chunk - half, WIDTH), BF)
    load_a.wait()
    copy_a.wait()
    send_b[:half] = (own_a[...].astype(F32) + recv_a[...].astype(F32)).astype(BF)

    def scatter(k):
        peer = lax.rem(me + k, n)
        return remote(
            send_b.at[rows(peer, chunk)], recv_b.at[k - 1], sem_b.at[0, k - 1], sem_b.at[1, k - 1], (peer, core)
        )

    def scatter_g(k):
        peer = lax.rem(me + k, n)
        return remote(
            send_g.at[rows(peer, gchunk)], recv_g.at[k - 1], sem_g.at[0, k - 1], sem_g.at[1, k - 1], (peer, core)
        )

    def gather(k):
        peer = lax.rem(me + k, n)
        return remote(reduced, total.at[core, me], sem_c.at[0, k - 1], sem_c.at[1, k - 1], (peer, core))

    def forward(k):
        piece_k = total.at[core, lax.rem(me + n - k, n), pl.ds(0, chunk)]
        return remote(piece_k, piece_k, sem_d.at[0, k], sem_d.at[1, k], partner)

    def each(first, step):
        def body(k, carry):
            step(k)
            return carry

        lax.fori_loop(first, n, body, 0)

    each(1, lambda k: scatter(k).start())

    load_d.wait()
    load_o.wait()
    grad = jnp.zeros((WIDTH, channels), F32)
    for j in range(FEATURE_STEPS):
        part = slice(piece * j, piece * j + piece)
        grad = grad + nn(dbuf[part].T, obuf[part])
    for j in range(FEATURE_STEPS):
        tokens[j].wait()
        features[j].wait()
        part = slice(piece * j, piece * j + piece)
        grad = grad + nn(dother[part].T, fbuf[part])
    used = WIDTH * (channels // WIDTH)
    for j in range(channels // WIDTH):
        send_g[WIDTH * j : WIDTH * j + WIDTH] = grad[:, WIDTH * j : WIDTH * j + WIDTH].astype(BF)
    if used < n * gchunk:
        send_g[used:] = jnp.zeros((n * gchunk - used, WIDTH), BF)
    each(1, lambda k: scatter_g(k).start())
    load_p.wait()
    for j in range(FEATURE_STEPS):
        part = slice(piece * j, piece * j + piece)
        vision[part] = nt(dother[part], pbuf[...]).astype(BF)

    def add(k, value):
        scatter(k).wait()
        return value + recv_b[k - 1].astype(F32)

    def add_g(k, value):
        scatter_g(k).wait()
        return value + recv_g[k - 1].astype(F32)

    reduced[:chunk] = lax.fori_loop(1, n, add, send_b[rows(me, chunk)].astype(F32)).astype(BF)
    reduced[chunk:] = lax.fori_loop(1, n, add_g, send_g[rows(me, gchunk)].astype(F32)).astype(BF)
    each(1, lambda k: gather(k).start())
    total[core, me] = reduced[...]
    forward(0).start()

    def pass_on(k):
        gather(k).wait()
        forward(k).start()

    each(1, pass_on)
    each(0, lambda k: forward(k).wait())


def in_hbm(value):
    return pltpu.with_memory_space_constraint(value, pltpu.HBM)


def finish_call(acc, dtok, feats, proj, n):
    slots, channels = dtok.shape[0], feats.shape[1]
    half = R_END // 2
    chunk = 16 * -(-half // (16 * n))
    gchunk = 16 * -(-channels // (16 * n))
    vmem = pl.BlockSpec(memory_space=pltpu.VMEM)
    hbm = pl.BlockSpec(memory_space=pltpu.HBM)
    dma = pltpu.SemaphoreType.DMA
    total, vision = pl.pallas_call(
        functools.partial(finish_kernel, n, chunk, gchunk),
        out_shape=(
            jax.ShapeDtypeStruct((2, n, chunk + gchunk, WIDTH), BF),
            jax.ShapeDtypeStruct((slots, channels), BF),
        ),
        in_specs=[hbm] * 4,
        out_specs=(vmem, vmem),
        scratch_shapes=[
            pltpu.VMEM(dtok.shape, BF),
            pltpu.VMEM(proj.shape, BF),
            pltpu.VMEM((slots, channels), BF),
            pltpu.VMEM(dtok.shape, BF),
            pltpu.VMEM((slots, channels), BF),
            pltpu.VMEM((half, WIDTH), BF),
            pltpu.VMEM((half, WIDTH), BF),
            pltpu.VMEM((n * chunk, WIDTH), BF),
            pltpu.VMEM((n - 1, chunk, WIDTH), BF),
            pltpu.VMEM((n * gchunk, WIDTH), BF),
            pltpu.VMEM((n - 1, gchunk, WIDTH), BF),
            pltpu.VMEM((chunk + gchunk, WIDTH), BF),
            dma((2, FEATURE_STEPS)),
            dma((FEATURE_STEPS,)),
            dma((6,)),
            dma((2, n - 1)),
            dma((2, n - 1)),
            dma((2, n)),
            dma((2, n - 1)),
        ],
        compiler_params=pltpu.CompilerParams(
            collective_id=0, has_side_effects=True, vmem_limit_bytes=36 * 2**20
        ),
        name="finish",
    )(*map(in_hbm, (acc, dtok, feats, proj)))
    return chunk, total, vision


def per_device(
    vision_feats, vision_grid, proprio, proprio_mask, token_valid, mix_weight, out_cot, feat_proj,
    vis_query, vis_wq, vis_kv, vis_wo, prop_w1, prop_w2, prop_query, prop_wq, prop_kv, prop_wo,
    ln1_gain, ln1_bias, qkv_weight, attn_out, ln2_gain, ln2_bias, mlp_in, mlp_out,
):
    me = lax.axis_index("mod").astype(jnp.int32)
    own = me.reshape(1)
    feats = vision_feats.reshape(-1, vision_feats.shape[3])
    received = project_call(feats, feat_proj)
    weights = (
        vis_query, vis_wq, vis_kv, vis_wo, prop_w1, prop_w2, prop_query, prop_wq, prop_kv, prop_wo,
        *(v.reshape(1, -1) for v in (ln1_gain, ln1_bias, ln2_gain, ln2_bias)), qkv_weight, attn_out, mlp_in, mlp_out,
    )
    frames = jnp.transpose(proprio, (1, 2, 3, 0)).reshape(-1, proprio.shape[0])
    frame_mask = jnp.transpose(proprio_mask, (1, 2, 0)).reshape(-1, proprio_mask.shape[0])
    grid_sizes = jnp.transpose(vision_grid, (1, 2, 0)).reshape(4, -1)
    output, grad_vision, dtok, dframes, acc = block_call(
        own, grid_sizes, feats, received, frames, frame_mask, token_valid, mix_weight.reshape(1, -1),
        out_cot.reshape(-1, WIDTH), feat_proj, weights,
    )
    chunk, total, vision = finish_call(acc, dtok, feats, feat_proj, lax.axis_size("dp"))
    grad_vision, *outs = unpack_call(
        chunk, vision, total, vis_query, vis_wq, prop_query, prop_wq, grad_vision
    )
    vectors = {11, 12, 15, 16}
    outs = [o.reshape(WIDTH) if j in vectors else o for j, o in enumerate(outs)]
    return (
        output.reshape(out_cot.shape),
        grad_vision.reshape(vision_feats.shape),
        jnp.transpose(dframes.reshape(proprio.shape[1:] + proprio.shape[:1]), (3, 0, 1, 2)),
        *outs,
    )


def solution(mesh):
    both = ("dp", "mod")
    return jax.shard_map(
        per_device,
        mesh=mesh,
        in_specs=(
            P("dp", None, None, "mod"),
            P(both, None, None),
            P(both, None, None, None),
            P(both, None, None),
            P(both, None),
            P(both),
            P(both, None, None),
            P("mod", None),
        ) + (P(),) * 18,
        out_specs=(
            P(both, None, None),
            P("dp", None, None, "mod"),
            P(both, None, None, None),
            P("mod", None),
        ) + (P(),) * 19,
        check_vma=False,
    )
```

```python
import functools
import math

import jax
import jax.numpy as jnp
from jax import lax
from jax.experimental import pallas as pl
from jax.experimental.pallas import tpu as pltpu
from jax.sharding import PartitionSpec as P

HEADS = 8
HEAD = 16
WIDTH = 128
PROP = 32
NEG = -1e30
BF = jnp.bfloat16
F32 = jnp.float32
VMEM_LIMIT = 60 * 2**20
CHAINS = 8
FF_PART = 256

R_WIN, R_WOUT, R_Q, R_KV, R_AO = 0, 512, 1024, 1152, 1408
R_SWO, R_VKV, R_PKV, R_W2, R_W1 = 1536, 1792, 2048, 2304, 2432
R_QV, R_QP, R_LN, R_STAT, R_END = 2464, 2480, 2496, 2500, 2560


def nn(a, b):
    return lax.dot_general(a, b, (((1,), (0,)), ((), ())), preferred_element_type=F32)


def nt(a, b):
    return lax.dot_general(a, b, (((1,), (1,)), ((), ())), preferred_element_type=F32)


def cat(items, axis):
    return jnp.concatenate(items, axis=axis)


def lane_iota(rows, lanes):
    return lax.broadcasted_iota(jnp.int32, (rows, lanes), 1)


def tile_to(mask, rows, lanes):
    return cat([cat([mask] * (rows // mask.shape[0]), 0)] * (lanes // mask.shape[1]), 1)


def head_expand(value, masks):
    return cat([value * tile_to(mask, *value.shape) for mask in masks], 0)


def head_select(full, heads, period):
    rows, lanes = full.shape[0] // heads, full.shape[1]
    head = (lane_iota(rows, lanes) & (period - 1)) >> 4
    out = full[:rows]
    for h in range(1, heads):
        out = jnp.where(head == h, full[h * rows : (h + 1) * rows], out)
    return out


def turn(value):
    out = []
    for j in range(0, value.shape[1], WIDTH):
        out += [value[:, j + 64 : j + 128], value[:, j : j + 64]]
    return cat(out, 1)


def diagonal(blocks):
    out = []
    for j, block in enumerate(blocks):
        row = [block if k == j else jnp.zeros((block.shape[0], other.shape[1]), BF) for k, other in enumerate(blocks)]
        out.append(cat(row, 1))
    return cat(out, 0)


def pair_up(parts):
    return cat([cat(parts[j : j + 2], 1) for j in range(0, 8, 2)], 0)


def unpair(value, rows):
    out = []
    for j in range(4):
        part = value[rows * j : rows * j + rows]
        out += [part[:, :WIDTH], part[:, WIDTH:]]
    return cat(out, 0)


def softmax_rows(scores):
    peak = jnp.max(scores, axis=1, keepdims=True)
    weights = jnp.exp(scores - peak)
    return weights * (1.0 / jnp.sum(weights, axis=1, keepdims=True))


def softmax_grad(weights, grad):
    return weights * (grad - jnp.sum(weights * grad, axis=1, keepdims=True))


def mean_rows(value):
    return jnp.sum(value, axis=0, keepdims=True) * (1.0 / value.shape[0])


def norm_rows(value):
    centered = value - mean_rows(value)
    scale = lax.rsqrt(mean_rows(centered * centered) + 1e-05)
    return centered * scale, scale


def norm_rows_grad(grad, hat, scale):
    return scale * (grad - mean_rows(grad) - hat * mean_rows(grad * hat))


def split_samples(value, low_half, high_half):
    out = []
    for s in range(4):
        half = tile_to(high_half if s % 2 else low_half, 64, WIDTH)
        block = value[:, WIDTH * (s // 2) : WIDTH * (s // 2) + WIDTH] * half
        zero = jnp.zeros((64, WIDTH), BF)
        out.append(cat([block, zero] if s < 2 else [zero, block], 1))
    return cat(out, 0)


def gather_heads(value, turned, group, low_half, high_half):
    low_tall, high_tall = tile_to(low_half, 64, WIDTH), tile_to(high_half, 64, WIDTH)
    out = []
    for s in (0, 2):
        even, odd = slice(64 * s, 64 * s + 64), slice(64 * s + 64, 64 * s + 128)
        left, right = (value[even], turned[odd]) if group == 0 else (turned[even], value[odd])
        out.append(left * low_tall + right * high_tall)
    return cat(out, 1)


def scatter_heads(parts, low_half, high_half):
    low_tall, high_tall = tile_to(low_half, 64, WIDTH), tile_to(high_half, 64, WIDTH)
    turned = [turn(part) for part in parts]
    out = []
    for s in range(4):
        lanes = slice(WIDTH * (s // 2), WIDTH * (s // 2) + WIDTH)
        left = (turned if s % 2 else parts)[0][:, lanes]
        right = (parts if s % 2 else turned)[1][:, lanes]
        out.append(left * low_tall + right * high_tall)
    return cat(out, 0)


def spread_keys(value, turned, group, low_half, high_half):
    zero = jnp.zeros((HEAD, WIDTH), BF)
    rows = []
    for s in range(4):
        lanes = slice(WIDTH * (s // 2), WIDTH * (s // 2) + WIDTH)
        for local in range(4):
            h = group * 4 + local
            source = value if s % 2 == local % 2 else turned
            block = source[h * HEAD : (h + 1) * HEAD, lanes] * (high_half if local % 2 else low_half)
            rows.append(cat([block, zero] if local < 2 else [zero, block], 1))
    return cat(rows, 0)


def mix_keys(value, weights, low_half, high_half, first):
    turned = turn(value)
    out = []
    for group in range(2):
        full = nn(spread_keys(value, turned, group, low_half, high_half), weights[group])
        left = jnp.where(first, full[:64, :WIDTH], full[64:128, :WIDTH])
        right = jnp.where(first, full[128:192, WIDTH:], full[192:, WIDTH:])
        out.append(cat([left, right], 1))
    return cat(out, 0)


def stem_queries(query, w_query, masks):
    value = nn(query, w_query).astype(BF)
    return head_expand(value * jnp.asarray(0.25, BF), masks)


def block_kernel(
    half, grid_ref, feats, pr, frames, frame_mask, token_valid, mix_weight, cot, proj,
    vis_query, vis_wq, vis_kv, vis_wo, prop_w1, prop_w2, prop_query, prop_wq, prop_kv, prop_wo,
    ln1_gain, ln1_bias, ln2_gain, ln2_bias, qkv_w, attn_out, mlp_in, mlp_out,
    out, grad_feats, dtok_ref, dframes, acc_out,
    masks_ref, qv_ref, qp_ref, wqkv_t, ao_t, win_t, wout_t, stem_t, ln_ref,
    gv_ref, gp_ref, lnacc, stat, acc, fr_ref, df_ref, aux_ref, turn_ref,
):
    blocks = token_valid.shape[0] // 4
    step = pl.program_id(0)

    @pl.when(step == 0)
    def _():
        lane = lane_iota(16, WIDTH) >> 4
        for h in range(HEADS):
            masks_ref[h] = jnp.where(lane == h, 1.0, 0.0).astype(BF)
        for h in range(4):
            masks_ref[HEADS + h] = jnp.where((lane & 3) == h, 1.0, 0.0).astype(BF)
        masks = [masks_ref[h] for h in range(HEADS)]
        qv_ref[...] = diagonal([stem_queries(vis_query[...], vis_wq[...], masks)] * 2)
        qp_ref[...] = diagonal([stem_queries(prop_query[...], prop_wq[...], masks)] * 2)
        wqkv_t[...] = qkv_w[...].T
        ao_t[...] = attn_out[...].T
        win_t[...] = mlp_in[...].T
        wout_t[...] = mlp_out[...].T
        stem_t[:, :WIDTH] = vis_wo[...].T
        stem_t[:, WIDTH:] = prop_wo[...].T
        for j, vector in enumerate((ln1_gain, ln1_bias, ln2_gain, ln2_bias)):
            ln_ref[j] = jnp.broadcast_to(vector[...].astype(F32), (WIDTH, WIDTH)).T

        def by_block(ref):
            return cat([ref[pl.ds(j, blocks, stride=4)].astype(F32) for j in range(4)], 1)

        valid = by_block(token_valid)
        turn_ref[...] = jnp.broadcast_to(mix_weight[...].astype(F32), turn_ref.shape).T
        mix = by_block(turn_ref)
        turn_ref[:, : frame_mask.shape[0]] = frame_mask[...].astype(F32).T
        frame_keep = cat([turn_ref[pl.ds(j, blocks, stride=4)][:, : frame_mask.shape[0]] for j in range(4)], 1)
        values = (valid, mix, jnp.where(valid > 0, 0.0, NEG), jnp.where(cat([frame_keep] * 2, 1) > 0, 0.0, NEG))
        for i in range(blocks):
            for j, value in enumerate(values):
                aux_ref[i, j : j + 1] = value[i : i + 1]

        for j in range(frames.shape[0] // PROP):
            block = frames[PROP * j : PROP * j + PROP].astype(F32).T
            fr_ref[pl.ds(j, block.shape[0], stride=frames.shape[0] // PROP)] = block
        acc[...] = jnp.zeros_like(acc)
        gv_ref[...] = jnp.zeros_like(gv_ref)
        gp_ref[...] = jnp.zeros_like(gp_ref)
        lnacc[...] = jnp.zeros_like(lnacc)
        stat[...] = jnp.zeros_like(stat)

    masks = [masks_ref[h] for h in range(HEADS)]
    masks_group = [masks_ref[HEADS + h] for h in range(4)]
    qv, qp = qv_ref[...], qp_ref[...]
    lane = lane_iota(HEAD, WIDTH)
    low_half = jnp.where(lane < 64, 1.0, 0.0).astype(BF)
    high_half = jnp.where(lane < 64, 0.0, 1.0).astype(BF)
    first = lane_iota(64, WIDTH) < 64


    def chain(g):
        block = step * CHAINS + g
        slots = slice(512 * g, 512 * g + 512)
        kept = nn(feats[slots], proj[...]).astype(BF)
        tok = (kept.astype(F32) + pr[slots].astype(F32)).astype(BF)
        vkv = nn(tok, vis_kv[...]).astype(BF)
        vk, vv = vkv[:, :WIDTH], vkv[:, WIDTH:]
        slot = lax.broadcasted_iota(jnp.int32, (64, WIDTH), 0)
        slot_row, slot_col = slot >> 3, slot & 7
        bias = []
        for st in range(8):
            s, t = (step * CHAINS + g) * 4 + st // 2, st % 2
            keep = (slot_row < grid_ref[2 * t, s]) & (slot_col < grid_ref[2 * t + 1, s])
            bias.append(jnp.where(keep, 0.0, NEG))
        bias = pair_up(bias).reshape(4, 64, 256)
        vk2 = pair_up([vk[64 * st : 64 * st + 64] for st in range(8)])
        vv2 = pair_up([vv[64 * st : 64 * st + 64] for st in range(8)])
        yield
        vp = softmax_rows(nt(vk2, qv).reshape(4, 64, 256) + bias)
        vpb = vp.reshape(256, 256).astype(BF)
        yield
        vpt = vpb.T
        vmixed = [None] * 8
        for e in range(2):
            for m in range(2):
                one, two = 4 * m + e, 4 * m + 2 + e
                spread = diagonal([vv[64 * one : 64 * one + 64], vv[64 * two : 64 * two + 64]])
                lhs = vpt[WIDTH * e : WIDTH * e + WIDTH, WIDTH * m : WIDTH * m + WIDTH]
                both = head_select(nn(lhs, spread), HEADS, WIDTH).astype(BF)
                vmixed[one], vmixed[two] = both[:, :WIDTH], both[:, WIDTH:]

        yield
        fr_rows = pl.ds(pl.multiple_of((step * CHAINS + g) * 128, 128), 128)
        fr = fr_ref[fr_rows].astype(BF)
        pre = nn(fr, prop_w1[...])
        gate = jax.nn.sigmoid(pre)
        hidden = (pre * gate).astype(BF)
        ptok = nn(hidden, prop_w2[...]).astype(BF)
        pkv = nn(ptok, prop_kv[...]).astype(BF)
        pk, pv = pkv[:, :WIDTH], pkv[:, WIDTH:]
        column = jnp.broadcast_to(aux_ref[block, 3:4, :WIDTH], (WIDTH, WIDTH)).T
        parts = lambda v: [v[HEAD * st : HEAD * st + HEAD] for st in range(8)]
        pbias = pair_up(parts(column))
        pk2, pv2 = pair_up(parts(pk)), pair_up(parts(pv))
        yield
        pp = softmax_rows((nt(pk2, qp) + pbias).reshape(4, HEAD, 256))
        ppb = pp.reshape(64, 256).astype(BF)
        ppt = ppb.T
        pmixed = [None] * 8
        for e in range(2):
            spread = diagonal([pv[HEAD * st : HEAD * st + HEAD] for st in range(e, 8, 2)])
            both = head_select(nn(ppt[WIDTH * e : WIDTH * e + WIDTH], spread), HEADS, WIDTH).astype(BF)
            for j in range(4):
                pmixed[2 * j + e] = both[:, WIDTH * j : WIDTH * j + WIDTH]

        yield
        zero16 = jnp.zeros((HEAD, WIDTH), BF)
        rows = []
        for st in range(8):
            rows.append(cat([vmixed[st], zero16], 1))
            rows.append(cat([zero16, pmixed[st]], 1))
        mixed_ext = cat(rows, 0)
        x = nt(stem_t[...], mixed_ext)
        g1, b1, g2, b2 = [cat([ln_ref[j]] * 2, 1) for j in range(4)]
        hat1, scale1 = norm_rows(x)
        n1 = (hat1 * g1 + b1).astype(BF)
        yield
        qkv = nn(wqkv_t[...], n1).astype(BF)
        qt, kt, vt = qkv[:WIDTH] * jnp.asarray(0.25, BF), qkv[WIDTH : 2 * WIDTH], qkv[2 * WIDTH :]
        kn, vn = kt.T, vt.T
        kn_turned, vn_turned = turn(kn), turn(vn)
        yield
        weights, weights_b, query_bd = [], [], []
        tbias = []
        for p in range(2):
            column = jnp.broadcast_to(aux_ref[block, 2:3, 128 * p : 128 * p + 128], (WIDTH, WIDTH)).T
            tbias.append(jnp.where(first, column[:64], column[64:]))
        tbias = cat(tbias, 1)[None]
        for group in range(2):
            part = slice(64 * group, 64 * group + 64)
            qbd = split_samples(qt[part], low_half, high_half)
            keys = head_expand(gather_heads(kn, kn_turned, group, low_half, high_half), masks_group)
            scores = nn(keys, qbd).reshape(4, 64, 256) + tbias
            yield
            w = softmax_rows(scores)
            weights.append(w)
            weights_b.append(w.reshape(256, 256).astype(BF))
            query_bd.append(qbd)
            yield
        mixed = mix_keys(vt, weights_b, low_half, high_half, first).astype(BF)
        yield
        branch = nn(ao_t[...], mixed)
        middle = x + branch
        hat2, scale2 = norm_rows(middle)
        n2 = (hat2 * g2 + b2).astype(BF)
        yield
        c = math.sqrt(2.0 / math.pi)
        seed = cot[256 * g : 256 * g + 256].T.astype(F32) * aux_ref[block, 1:2, :]
        dmlp = seed.astype(BF)
        mlp, dn2, act_all, dup_all = 0.0, 0.0, [], []
        for j in range(512 // FF_PART):
            part = slice(FF_PART * j, FF_PART * j + FF_PART)
            up = nn(win_t[part], n2)
            yield
            square = up * up
            h = 0.5 + 0.5 * jnp.tanh(up * (c + (c * 0.044715) * square))
            act = up * h
            slope = h + act * (1.0 - h) * (2 * c + (6 * c * 0.044715) * square)
            act_b = act.astype(BF)
            mlp = mlp + nn(wout_t[:, part], act_b)
            dup = (nn(mlp_out[part], dmlp) * slope).astype(BF)
            yield
            dn2 = dn2 + nn(mlp_in[:, part], dup)
            acc[R_WOUT + FF_PART * j : R_WOUT + FF_PART * j + FF_PART] += nt(act_b, dmlp)
            acc[R_WIN + FF_PART * j : R_WIN + FF_PART * j + FF_PART] += nt(dup, n2)
            yield
        final = middle + mlp
        out[256 * g : 256 * g + 256] = final.astype(BF).T
        valid = aux_ref[block, 0:1, :]
        for j, value in enumerate((final, branch, mlp)):
            stat[j : j + 1, :] += jnp.sum(value * value, axis=0, keepdims=True) * valid
        stat[3:4, :] += valid

        yield
        fold = lambda v: v[:, :WIDTH] + v[:, WIDTH:]
        lnacc[2] += fold(dn2 * hat2)
        lnacc[3] += fold(dn2)
        dmid = seed + norm_rows_grad(dn2 * g2, hat2, scale2)
        dbranch = dmid.astype(BF)
        acc[R_AO : R_AO + WIDTH] += nt(mixed, dbranch)
        yield
        dmixed = nn(attn_out[...], dbranch).astype(BF)
        yield
        ds_all, dk, dv = [], [], []
        for group in range(2):
            part = slice(64 * group, 64 * group + 64)
            dbd = split_samples(dmixed[part], low_half, high_half)
            values = head_expand(gather_heads(vn, vn_turned, group, low_half, high_half), masks_group)
            dw = nn(values, dbd).reshape(4, 64, 256)
            yield
            ds = softmax_grad(weights[group], dw).reshape(256, 256).astype(BF)
            dv.append(head_select(nt(weights_b[group], dbd), 4, 64).astype(BF))
            dk.append(head_select(nt(ds, query_bd[group]), 4, 64).astype(BF))
            ds_all.append(ds)
        dq = (mix_keys(kt, ds_all, low_half, high_half, first) * 0.25).astype(BF)
        dkv = cat([scatter_heads(dk, low_half, high_half), scatter_heads(dv, low_half, high_half)], 1)
        yield
        acc[R_Q : R_Q + WIDTH] += nt(n1, dq)
        grad = nn(n1, dkv)
        acc[R_KV : R_KV + WIDTH] += grad[:, :WIDTH]
        acc[R_KV + WIDTH : R_KV + 2 * WIDTH] += grad[:, WIDTH:]
        dn1 = nn(qkv_w[:, :WIDTH], dq) + nt(qkv_w[:, WIDTH:], dkv)
        lnacc[0] += fold(dn1 * hat1)
        lnacc[1] += fold(dn1)
        dx = (dmid + norm_rows_grad(dn1 * g1, hat1, scale1)).astype(BF)

        yield
        grad = nn(dx, mixed_ext)
        acc[R_SWO : R_SWO + WIDTH] += grad[:, :WIDTH]
        acc[R_SWO + WIDTH : R_SWO + 2 * WIDTH] += grad[:, WIDTH:]
        dstem = nn(dx.T, stem_t[...]).astype(BF)
        dw, dv, pdw, pdv = [], [], [], []
        for st in range(8):
            j, e, r = st // 2, st % 2, 32 * st
            tall, short, lanes = slice(64 * j, 64 * j + 64), slice(HEAD * j, HEAD * j + HEAD), slice(WIDTH * e, WIDTH * e + WIDTH)
            spread = head_expand(cat([dstem[r : r + 16, :WIDTH], dstem[r + 16 : r + 32, WIDTH:]], 1), masks)
            full = nt(diagonal([vv2[tall, lanes], pv2[short, lanes]]), spread)
            dw.append(full[:64])
            pdw.append(full[64:])
            full = nn(
                diagonal([vpb[tall, lanes], ppb[short, lanes]]), cat([spread[:, :WIDTH], spread[:, WIDTH:]], 0)
            ).astype(BF)
            dv.append(full[:64])
            pdv.append(full[64:])
        yield
        ds = softmax_grad(vp, pair_up(dw).reshape(4, 64, 256)).reshape(256, 256).astype(BF)
        dkv = cat([unpair(nn(ds, qv).astype(BF), 64), cat(dv, 0)], 1)
        dtok = nt(dkv, vis_kv[...]).astype(BF)
        dtok_ref[slots] = dtok
        grad_feats[slots] = nt(dtok, proj[...]).astype(BF)
        grad = nn(tok.T, dkv)
        acc[R_VKV : R_VKV + WIDTH] += grad[:, :WIDTH]
        acc[R_VKV + WIDTH : R_VKV + 2 * WIDTH] += grad[:, WIDTH:]
        full = nn(ds.T, vk2)
        gv_ref[...] += full[:WIDTH, :WIDTH] + full[WIDTH:, WIDTH:]

        yield
        ds = softmax_grad(pp, pair_up(pdw).reshape(4, HEAD, 256)).reshape(64, 256).astype(BF)
        dkv = cat([unpair(nn(ds, qp).astype(BF), HEAD), cat(pdv, 0)], 1)
        dptok = nt(dkv, prop_kv[...]).astype(BF)
        grad = nn(ptok.T, dkv)
        acc[R_PKV : R_PKV + WIDTH] += grad[:, :WIDTH]
        acc[R_PKV + WIDTH : R_PKV + 2 * WIDTH] += grad[:, WIDTH:]
        full = nn(ds.T, pk2)
        gp_ref[...] += full[:WIDTH, :WIDTH] + full[WIDTH:, WIDTH:]
        yield
        acc[R_W2 : R_W2 + WIDTH] += nn(hidden.T, dptok)
        dhidden = nt(dptok, prop_w2[...])
        dpre = (dhidden * (gate * (1.0 + pre * (1.0 - gate)))).astype(BF)
        acc[R_W1 : R_W1 + 32] += nn(fr.T, dpre)
        df_ref[fr_rows] = nt(dpre, prop_w1[...])

        yield

    live = [(g // 2 * 5, chain(g)) for g in range(CHAINS)]
    tick = 0
    while live:
        for one in list(live):
            if tick >= one[0] and next(one[1], live) is live:
                live.remove(one)
        tick += 1

    @pl.when(step == pl.num_programs(0) - 1)
    def _():
        acc[R_QV : R_QV + 16] = head_select(gv_ref[...], HEADS, WIDTH) * 0.25
        acc[R_QP : R_QP + 16] = head_select(gp_ref[...], HEADS, WIDTH) * 0.25
        for j in range(4):
            acc[R_LN + j : R_LN + j + 1] = jnp.sum(lnacc[j].T, axis=0, keepdims=True)
            acc[R_STAT + j : R_STAT + j + 1] = stat[j : j + 1, :WIDTH] + stat[j : j + 1, WIDTH:]
        acc_out[...] = acc[...].astype(BF)
        for j in range(frames.shape[0] // PROP):
            block = df_ref[pl.ds(j, frames.shape[1], stride=frames.shape[0] // PROP)]
            dframes[PROP * j : PROP * j + PROP] = block.T.astype(BF)


def whole(shape):
    return pl.BlockSpec(shape, lambda i, *_: (0,) * len(shape))


def block_call(half, grid_sizes, feats, received, frames, frame_mask, token_valid, mix_weight, cot, proj, weights):
    samples, seq = token_valid.shape
    steps = samples // (4 * CHAINS)
    channels = feats.shape[1]
    row = lambda i, *_: (i, 0)
    own = lambda i, half, _: (half[0] * steps + i, 0)
    in_specs = [
        pl.BlockSpec((512 * CHAINS, channels), own),
        pl.BlockSpec((512 * CHAINS, WIDTH), row),
        whole(frames.shape),
        whole(frame_mask.shape),
        whole(token_valid.shape),
        whole(mix_weight.shape),
        pl.BlockSpec((256 * CHAINS, WIDTH), row),
        whole(proj.shape),
    ] + [whole(w.shape) for w in weights]
    out_shape = (
        jax.ShapeDtypeStruct((256 * CHAINS * steps, WIDTH), BF),
        jax.ShapeDtypeStruct(feats.shape, BF),
        jax.ShapeDtypeStruct((512 * CHAINS * steps, WIDTH), BF),
        jax.ShapeDtypeStruct(frames.shape, BF),
        jax.ShapeDtypeStruct((R_END, WIDTH), BF),
    )
    out_specs = (
        pl.BlockSpec((256 * CHAINS, WIDTH), row),
        pl.BlockSpec((512 * CHAINS, channels), own),
        pl.BlockSpec((512 * CHAINS, WIDTH), row),
        whole(frames.shape),
        whole((R_END, WIDTH)),
    )
    scratch = [
        pltpu.VMEM((12, 16, WIDTH), BF),
        pltpu.VMEM((256, 256), BF),
        pltpu.VMEM((256, 256), BF),
        pltpu.VMEM((384, WIDTH), BF),
        pltpu.VMEM((128, WIDTH), BF),
        pltpu.VMEM((512, WIDTH), BF),
        pltpu.VMEM((128, 512), BF),
        pltpu.VMEM((128, 256), BF),
        pltpu.VMEM((4, WIDTH, WIDTH), F32),
        pltpu.VMEM((WIDTH, WIDTH), F32),
        pltpu.VMEM((WIDTH, WIDTH), F32),
        pltpu.VMEM((4, WIDTH, WIDTH), F32),
        pltpu.VMEM((8, 256), F32),
        pltpu.VMEM((R_END, WIDTH), F32),
        pltpu.VMEM((frames.shape[0] // PROP * frames.shape[1], PROP), F32),
        pltpu.VMEM((frames.shape[0] // PROP * frames.shape[1], PROP), F32),
        pltpu.VMEM((samples // 4, 8, 4 * seq), F32),
        pltpu.VMEM((samples, seq), F32),
    ]
    return pl.pallas_call(
        block_kernel,
        grid_spec=pltpu.PrefetchScalarGridSpec(
            num_scalar_prefetch=2,
            grid=(steps,),
            in_specs=in_specs,
            out_specs=out_specs,
            scratch_shapes=scratch,
        ),
        out_shape=out_shape,
        compiler_params=pltpu.CompilerParams(vmem_limit_bytes=VMEM_LIMIT),
        name="stems_trunk",
    )(half, grid_sizes, feats, received, frames, frame_mask, token_valid, mix_weight, cot, proj, *weights)

PROJECT_STEPS = 8
FEATURE_STEPS = 4


def project_kernel(feats, proj, out, fbuf, stage, sem_f, sem_s):
    me, core = lax.axis_index("dp"), lax.axis_index("mod")
    mesh = pl.DeviceIdType.MESH
    partner = (me, 1 - core)
    slots = fbuf.shape[0]
    piece = slots // PROJECT_STEPS
    loads, sends = [], []
    for j in range(PROJECT_STEPS):
        start = pl.multiple_of((1 - core) * slots + piece * j, 16)
        loads.append(pltpu.make_async_copy(feats.at[pl.ds(start, piece)], fbuf.at[pl.ds(piece * j, piece)], sem_f.at[j]))
        loads[j].start()
    barrier = pltpu.get_barrier_semaphore()
    pl.semaphore_signal(barrier, inc=1, device_id=partner, device_id_type=mesh)
    pl.semaphore_wait(barrier, 1)
    for j in range(PROJECT_STEPS):
        part = pl.ds(piece * j, piece)
        loads[j].wait()
        stage[part] = nn(fbuf[part], proj[...]).astype(BF)
        sends.append(
            pltpu.make_async_remote_copy(
                src_ref=stage.at[part], dst_ref=out.at[part], send_sem=sem_s.at[0, j], recv_sem=sem_s.at[1, j],
                device_id=partner, device_id_type=mesh,
            )
        )
        sends[j].start()
    for j in range(PROJECT_STEPS):
        sends[j].wait()


def project_call(feats, proj):
    slots, channels = feats.shape[0] // 2, feats.shape[1]
    hbm = pl.BlockSpec(memory_space=pl.ANY)
    return pl.pallas_call(
        project_kernel,
        in_specs=[hbm, pl.BlockSpec(memory_space=pltpu.VMEM)],
        out_specs=hbm,
        out_shape=jax.ShapeDtypeStruct((slots, WIDTH), BF),
        scratch_shapes=[
            pltpu.VMEM((slots, channels), BF),
            pltpu.VMEM((slots, WIDTH), BF),
            pltpu.SemaphoreType.DMA((PROJECT_STEPS,)),
            pltpu.SemaphoreType.DMA((2, PROJECT_STEPS)),
        ],
        compiler_params=pltpu.CompilerParams(
            collective_id=1, has_side_effects=True, vmem_limit_bytes=VMEM_LIMIT
        ),
        name="project",
    )(feats, proj)


def unpack_kernel(
    chunk, vision, total, vis_query, vis_wq, prop_query, prop_wq, before,
    o_vision, o_feat, o_vq, o_vwq, o_vkv, o_vwo, o_w1, o_w2, o_pq, o_pwq, o_pkv, o_pwo,
    o_g1, o_b1, o_qkv, o_ao, o_g2, o_b2, o_in, o_out, o_rms, sem,
):
    core = lax.axis_index("mod")
    slots, channels = vision.shape
    piece = slots // FEATURE_STEPS
    copies = []
    for j in range(FEATURE_STEPS):
        start = pl.multiple_of((1 - core) * slots + piece * j, 16)
        copies.append(
            pltpu.make_async_copy(vision.at[pl.ds(piece * j, piece)], o_vision.at[pl.ds(start, piece)], sem.at[j])
        )
        copies[j].start()

    n = total.shape[1]
    halves = [total[j, :, :chunk].reshape(n * chunk, WIDTH) for j in range(2)]
    half = R_END // 2

    def rows(start, count):
        source, at = halves[start // half], start % half
        return source[at : at + count].astype(F32)

    gsum = total[core, :, chunk:].reshape(n * (total.shape[2] - chunk), WIDTH).astype(F32)
    for j in range(channels // WIDTH):
        o_feat[WIDTH * j : WIDTH * j + WIDTH] = gsum[WIDTH * j : WIDTH * j + WIDTH].T
    for o_query, o_w, query, w, start in (
        (o_vq, o_vwq, vis_query, vis_wq, R_QV),
        (o_pq, o_pwq, prop_query, prop_wq, R_QP),
    ):
        grad = rows(start, 16).astype(BF)
        o_query[...] = nt(grad, w[...])
        o_w[...] = lax.dot_general(
            query[...], grad, (((0,), (0,)), ((), ())), preferred_element_type=F32
        )
    for o, start in ((o_vkv, R_VKV), (o_pkv, R_PKV)):
        o[:, :WIDTH] = rows(start, WIDTH)
        o[:, WIDTH:] = rows(start + WIDTH, WIDTH)
    o_vwo[...] = rows(R_SWO, WIDTH).T
    o_pwo[...] = rows(R_SWO + WIDTH, WIDTH).T
    o_w1[...] = rows(R_W1, 32)
    o_w2[...] = rows(R_W2, WIDTH)
    for j in range(3):
        o_qkv[:, WIDTH * j : WIDTH * j + WIDTH] = rows(R_Q + WIDTH * j, WIDTH)
    o_ao[...] = rows(R_AO, WIDTH)
    o_in[...] = rows(R_WIN, 512).T
    o_out[...] = rows(R_WOUT, 512)
    small = rows(R_LN, 16)
    for j, o in enumerate((o_g1, o_b1, o_g2, o_b2)):
        o[...] = small[j : j + 1]
    sums = [jnp.sum(small[R_STAT - R_LN + j : R_STAT - R_LN + j + 1], axis=1, keepdims=True) for j in range(4)]
    for j in range(3):
        o_rms[j] = jnp.sum(jnp.sqrt(sums[j] / (sums[3] * WIDTH)))
    for copy in copies:
        copy.wait()


def unpack_call(chunk, vision, total, vis_query, vis_wq, prop_query, prop_wq, grad_vision):
    channels = vision.shape[1]
    shapes = [
        (channels, WIDTH), (16, WIDTH), (WIDTH, WIDTH), (WIDTH, 256), (WIDTH, WIDTH), (32, WIDTH),
        (WIDTH, WIDTH), (16, WIDTH), (WIDTH, WIDTH), (WIDTH, 256), (WIDTH, WIDTH), (1, WIDTH), (1, WIDTH),
        (WIDTH, 384), (WIDTH, WIDTH), (1, WIDTH), (1, WIDTH), (WIDTH, 512), (512, WIDTH), (3,),
    ]
    vmem, hbm = pl.BlockSpec(memory_space=pltpu.VMEM), pl.BlockSpec(memory_space=pltpu.HBM)
    return pl.pallas_call(
        functools.partial(unpack_kernel, chunk),
        in_specs=[vmem] * 6 + [hbm],
        out_specs=[hbm] + [vmem] * (len(shapes) - 1) + [pl.BlockSpec(memory_space=pltpu.SMEM)],
        out_shape=[jax.ShapeDtypeStruct(grad_vision.shape, BF)] + [jax.ShapeDtypeStruct(s, F32) for s in shapes],
        scratch_shapes=[pltpu.SemaphoreType.DMA((FEATURE_STEPS,))],
        input_output_aliases={6: 0},
        compiler_params=pltpu.CompilerParams(vmem_limit_bytes=20 * 2**20),
        name="unpack",
    )(vision, total, *map(in_hbm, (vis_query, vis_wq, prop_query, prop_wq)), grad_vision)


def finish_kernel(
    n, chunk, gchunk, acc, dtok, feats, proj, total, vision,
    dother, pbuf, fbuf, dbuf, obuf, own_a, recv_a, send_b, recv_b, send_g, recv_g, reduced,
    sem_t, sem_f, sem_o, sem_a, sem_b, sem_c, sem_d, sem_g,
):
    me, core = lax.axis_index("dp"), lax.axis_index("mod")
    mesh = pl.DeviceIdType.MESH
    partner = (me, 1 - core)
    half = R_END // 2
    slots, channels = fbuf.shape
    piece = slots // FEATURE_STEPS

    def remote(src, dst, send_sem, recv_sem, device):
        return pltpu.make_async_remote_copy(
            src_ref=src, dst_ref=dst, send_sem=send_sem, recv_sem=recv_sem, device_id=device, device_id_type=mesh
        )

    def rows(index, count):
        return pl.ds(pl.multiple_of(index * count, 16), count)

    barrier = pltpu.get_barrier_semaphore()
    pl.semaphore_signal(barrier, inc=1, device_id=partner, device_id_type=mesh)

    def greet(k, carry):
        pl.semaphore_signal(barrier, inc=1, device_id=(lax.rem(me + k, n), core), device_id_type=mesh)
        return carry

    lax.fori_loop(1, n, greet, 0)
    load_a = pltpu.make_async_copy(acc.at[rows(core, half)], own_a, sem_a.at[2])
    load_a.start()
    load_d = pltpu.make_async_copy(dtok, dbuf, sem_a.at[3])
    load_d.start()
    own_loads = []
    for j in range(FEATURE_STEPS):
        start_row = pl.multiple_of(core * slots + piece * j, 16)
        part = pl.ds(piece * j, piece)
        own_loads.append(pltpu.make_async_copy(feats.at[pl.ds(start_row, piece)], obuf.at[part], sem_o.at[j]))
        own_loads[j].start()
    load_p = pltpu.make_async_copy(proj, pbuf, sem_a.at[4])
    load_p.start()
    tokens, features = [], []
    for j in range(FEATURE_STEPS):
        part = pl.ds(piece * j, piece)
        start_row = pl.multiple_of((1 - core) * slots + piece * j, 16)
        features.append(pltpu.make_async_copy(feats.at[pl.ds(start_row, piece)], fbuf.at[part], sem_f.at[j]))
        features[j].start()
    pl.semaphore_wait(barrier, n)

    copy_a = remote(acc.at[rows(1 - core, half)], recv_a, sem_a.at[0], sem_a.at[1], partner)
    copy_a.start()
    for j in range(FEATURE_STEPS):
        part = pl.ds(piece * j, piece)
        tokens.append(remote(dtok.at[part], dother.at[part], sem_t.at[0, j], sem_t.at[1, j], partner))
        tokens[j].start()
    if half < n * chunk:
        send_b[half:] = jnp.zeros((n * chunk - half, WIDTH), BF)
    load_a.wait()
    copy_a.wait()
    send_b[:half] = (own_a[...].astype(F32) + recv_a[...].astype(F32)).astype(BF)

    def scatter(k):
        peer = lax.rem(me + k, n)
        return remote(
            send_b.at[rows(peer, chunk)], recv_b.at[k - 1], sem_b.at[0, k - 1], sem_b.at[1, k - 1], (peer, core)
        )

    def scatter_g(k):
        peer = lax.rem(me + k, n)
        return remote(
            send_g.at[rows(peer, gchunk)], recv_g.at[k - 1], sem_g.at[0, k - 1], sem_g.at[1, k - 1], (peer, core)
        )

    def gather(k):
        peer = lax.rem(me + k, n)
        return remote(reduced, total.at[core, me], sem_c.at[0, k - 1], sem_c.at[1, k - 1], (peer, core))

    def forward(k):
        piece_k = total.at[core, lax.rem(me + n - k, n), pl.ds(0, chunk)]
        return remote(piece_k, piece_k, sem_d.at[0, k], sem_d.at[1, k], partner)

    def each(first, step):
        def body(k, carry):
            step(k)
            return carry

        lax.fori_loop(first, n, body, 0)

    each(1, lambda k: scatter(k).start())

    load_d.wait()
    grad = jnp.zeros((WIDTH, channels), F32)
    for j in range(FEATURE_STEPS):
        part = slice(piece * j, piece * j + piece)
        own_loads[j].wait()
        grad = grad + nn(dbuf[part].T, obuf[part])
    for j in range(FEATURE_STEPS):
        tokens[j].wait()
        features[j].wait()
        part = slice(piece * j, piece * j + piece)
        grad = grad + nn(dother[part].T, fbuf[part])
    used = WIDTH * (channels // WIDTH)
    for j in range(channels // WIDTH):
        send_g[WIDTH * j : WIDTH * j + WIDTH] = grad[:, WIDTH * j : WIDTH * j + WIDTH].astype(BF)
    if used < n * gchunk:
        send_g[used:] = jnp.zeros((n * gchunk - used, WIDTH), BF)
    each(1, lambda k: scatter_g(k).start())
    load_p.wait()
    for j in range(FEATURE_STEPS):
        part = slice(piece * j, piece * j + piece)
        vision[part] = nt(dother[part], pbuf[...]).astype(BF)

    def add(k, value):
        scatter(k).wait()
        return value + recv_b[k - 1].astype(F32)

    def add_g(k, value):
        scatter_g(k).wait()
        return value + recv_g[k - 1].astype(F32)

    reduced[:chunk] = lax.fori_loop(1, n, add, send_b[rows(me, chunk)].astype(F32)).astype(BF)
    reduced[chunk:] = lax.fori_loop(1, n, add_g, send_g[rows(me, gchunk)].astype(F32)).astype(BF)
    each(1, lambda k: gather(k).start())
    total[core, me] = reduced[...]
    forward(0).start()

    def pass_on(k):
        gather(k).wait()
        forward(k).start()

    each(1, pass_on)
    each(0, lambda k: forward(k).wait())


def in_hbm(value):
    return pltpu.with_memory_space_constraint(value, pltpu.HBM)


def finish_call(acc, dtok, feats, proj, n):
    slots, channels = dtok.shape[0], feats.shape[1]
    half = R_END // 2
    chunk = 16 * -(-half // (16 * n))
    gchunk = 16 * -(-channels // (16 * n))
    vmem = pl.BlockSpec(memory_space=pltpu.VMEM)
    hbm = pl.BlockSpec(memory_space=pltpu.HBM)
    dma = pltpu.SemaphoreType.DMA
    total, vision = pl.pallas_call(
        functools.partial(finish_kernel, n, chunk, gchunk),
        out_shape=(
            jax.ShapeDtypeStruct((2, n, chunk + gchunk, WIDTH), BF),
            jax.ShapeDtypeStruct((slots, channels), BF),
        ),
        in_specs=[hbm] * 4,
        out_specs=(vmem, vmem),
        scratch_shapes=[
            pltpu.VMEM(dtok.shape, BF),
            pltpu.VMEM(proj.shape, BF),
            pltpu.VMEM((slots, channels), BF),
            pltpu.VMEM(dtok.shape, BF),
            pltpu.VMEM((slots, channels), BF),
            pltpu.VMEM((half, WIDTH), BF),
            pltpu.VMEM((half, WIDTH), BF),
            pltpu.VMEM((n * chunk, WIDTH), BF),
            pltpu.VMEM((n - 1, chunk, WIDTH), BF),
            pltpu.VMEM((n * gchunk, WIDTH), BF),
            pltpu.VMEM((n - 1, gchunk, WIDTH), BF),
            pltpu.VMEM((chunk + gchunk, WIDTH), BF),
            dma((2, FEATURE_STEPS)),
            dma((FEATURE_STEPS,)),
            dma((FEATURE_STEPS,)),
            dma((5,)),
            dma((2, n - 1)),
            dma((2, n - 1)),
            dma((2, n)),
            dma((2, n - 1)),
        ],
        compiler_params=pltpu.CompilerParams(
            collective_id=0, has_side_effects=True, vmem_limit_bytes=36 * 2**20
        ),
        name="finish",
    )(*map(in_hbm, (acc, dtok, feats, proj)))
    return chunk, total, vision


def per_device(
    vision_feats, vision_grid, proprio, proprio_mask, token_valid, mix_weight, out_cot, feat_proj,
    vis_query, vis_wq, vis_kv, vis_wo, prop_w1, prop_w2, prop_query, prop_wq, prop_kv, prop_wo,
    ln1_gain, ln1_bias, qkv_weight, attn_out, ln2_gain, ln2_bias, mlp_in, mlp_out,
):
    me = lax.axis_index("mod").astype(jnp.int32)
    own = me.reshape(1)
    feats = vision_feats.reshape(-1, vision_feats.shape[3])
    received = project_call(feats, feat_proj)
    weights = (
        vis_query, vis_wq, vis_kv, vis_wo, prop_w1, prop_w2, prop_query, prop_wq, prop_kv, prop_wo,
        *(v.reshape(1, -1) for v in (ln1_gain, ln1_bias, ln2_gain, ln2_bias)), qkv_weight, attn_out, mlp_in, mlp_out,
    )
    frames = jnp.transpose(proprio, (1, 2, 3, 0)).reshape(-1, proprio.shape[0])
    frame_mask = jnp.transpose(proprio_mask, (1, 2, 0)).reshape(-1, proprio_mask.shape[0])
    grid_sizes = jnp.transpose(vision_grid, (1, 2, 0)).reshape(4, -1)
    output, grad_vision, dtok, dframes, acc = block_call(
        own, grid_sizes, feats, received, frames, frame_mask, token_valid, mix_weight.reshape(1, -1),
        out_cot.reshape(-1, WIDTH), feat_proj, weights,
    )
    chunk, total, vision = finish_call(acc, dtok, feats, feat_proj, lax.axis_size("dp"))
    grad_vision, *outs = unpack_call(
        chunk, vision, total, vis_query, vis_wq, prop_query, prop_wq, grad_vision
    )
    vectors = {11, 12, 15, 16}
    outs = [o.reshape(WIDTH) if j in vectors else o for j, o in enumerate(outs)]
    return (
        output.reshape(out_cot.shape),
        grad_vision.reshape(vision_feats.shape),
        jnp.transpose(dframes.reshape(proprio.shape[1:] + proprio.shape[:1]), (3, 0, 1, 2)),
        *outs,
    )


def solution(mesh):
    both = ("dp", "mod")
    return jax.shard_map(
        per_device,
        mesh=mesh,
        in_specs=(
            P("dp", None, None, "mod"),
            P(both, None, None),
            P(both, None, None, None),
            P(both, None, None),
            P(both, None),
            P(both),
            P(both, None, None),
            P("mod", None),
        ) + (P(),) * 18,
        out_specs=(
            P(both, None, None),
            P("dp", None, None, "mod"),
            P(both, None, None, None),
            P("mod", None),
        ) + (P(),) * 19,
        check_vma=False,
    )
```
